32 devices in a mesh: section: 2 (over y), dp: 16 (over z, x, core).
Axes of the slice: x: 2, y: 2, z: 4, core: 2. Of those that a mesh axis runs over, the one named last changes fastest.
Arguments:
- fresh_acts: bfloat16 [3, 128, 8192], P(None, None, 'dp'), may hold values from -36 to 36
- carried: bfloat16 [2, 128, 8192], P('section', None, 'dp'), may hold values from -36 to 36
- norm_gain: float32 [2, 8192], P('section'), may hold values from 0.1 to 1.9
- w_in: bfloat16 [2, 3, 4096, 8192], P('section', None, 'dp'), may hold values from -0.0625 to 0.0625
- short_filter: float32 [2, 3, 4096, 3], P('section', None, 'dp'), may hold values from -3 to 3
- filter_taps: float32 [2, 4096, 128], P('section', 'dp'), may hold values from -0.9 to 0.9
- decay_rate: float32 [2, 4096], P('section', 'dp'), may hold values from 0.01 to 0.12
- w_out: bfloat16 [2, 4096, 8192], P('section', None, 'dp'), may hold values from -0.09375 to 0.09375
Outputs:
- section_outputs: bfloat16 [2, 3, 128, 8192], P('section', None, None, 'dp')
The draws below stay inside these ranges and needn't reach their ends.
All inputs are finite; a program needn't handle non-finite values.
Results may differ from the reference program's by a relative error of at most 0.011.
Values may be sent and summed in bfloat16 or wider, within the bound.
No kernel may reach another device: no remote copies, remote signals or barrier semaphores. Data moves between devices by JAX's collectives and lax.ppermute only.
A program may use at most 128 MiB of HBM per device.

```python
import math
import jax
import jax.numpy as jnp
from jax import lax

D = 8192
CH = 4096
SHORT = 3
FLEN = 128
SEQ = 128
TICKS = 3
N_SECTION = 2


def scaled_acts(key, shape, base_vals):
    key_row = jax.random.fold_in(key, 11)
    key_col = jax.random.fold_in(key, 12)
    row_scale = jnp.exp(jax.random.uniform(key_row, shape[:-1] + (1,), jnp.float32, math.log(0.3), math.log(3.0)))
    col_scale = jnp.exp(jax.random.uniform(key_col, (shape[-1],), jnp.float32, math.log(0.3), math.log(3.0)))
    return base_vals * row_scale * col_scale


def draw_fresh_acts(key, part):
    shape = (TICKS, SEQ, D)
    key_val = jax.random.fold_in(key, 10)
    base_vals = jnp.clip(jax.random.normal(key_val, shape, jnp.float32), -4.0, 4.0)
    return scaled_acts(key, shape, base_vals).astype(jnp.bfloat16)


def draw_carried(key, part):
    shape = (N_SECTION, SEQ, D)
    key_val = jax.random.fold_in(key, 20)
    base_vals = jnp.clip(jax.random.normal(key_val, shape, jnp.float32), -4.0, 4.0)
    return scaled_acts(key, shape, base_vals).astype(jnp.bfloat16)


def block_levels(rng, dims, cuts, smallest, largest):
    loudness = 1.0
    for position, shards_of in cuts:
        heights = jax.random.uniform(jax.random.fold_in(jax.random.fold_in(rng, 6), position), (shards_of,), jnp.float32, smallest / len(cuts), largest / len(cuts))
        loudness = loudness * jnp.repeat(jnp.exp(heights), dims[position] // shards_of).reshape((-1,) + (1,) * (len(dims) - 1 - position))
    return loudness


def noise(own_key, shape, width, most, cuts=(), held_as=jnp.bfloat16):
    values = jax.random.normal(own_key, shape, jnp.float32) * width
    if len(cuts) > 0:
        values = block_levels(own_key, shape, cuts, -0.22, 0.18) * values
    return jnp.clip(values, min=-most, max=most).astype(held_as)


def setup_inputs(seed: int = 0) -> dict:
    splits = jax.random.split(jax.random.key(seed), 9)
    return {
        "fresh_acts": draw_fresh_acts(jax.random.fold_in(splits[8], 71), 0),
        "carried": draw_carried(jax.random.fold_in(splits[8], 71), 0),
        "norm_gain": jnp.clip(1.0 + 0.18 * jax.random.normal(splits[2], (N_SECTION, D), jnp.float32), 0.1, 1.9),
        "w_in": noise(splits[3], (N_SECTION, 3, CH, D), D ** -0.5, 0.0625, ((0, 2), (2, 16))),
        "short_filter": noise(splits[4], (N_SECTION, 3, CH, SHORT), 0.6, 3.0, ((0, 2), (2, 16)), jnp.float32),
        "filter_taps": noise(splits[5], (N_SECTION, CH, FLEN), 0.15, 0.9, ((0, 2), (1, 16)), jnp.float32),
        "decay_rate": jnp.clip(jnp.exp(math.log(0.12) - 2.4849066 * jax.random.uniform(splits[6], (N_SECTION, CH), jnp.float32) ** block_levels(splits[6], (N_SECTION, CH), ((0, 2), (1, 16)), -0.2, 0.2)), 0.01, 0.12),
        "w_out": noise(splits[7], (N_SECTION, CH, D), CH ** -0.5, 0.09375, ((0, 2), (2, 16))),
    }


EPS = 1e-06

def hyena_layer(acts, norm_gain, w_in, short_filter, filter_taps, decay_rate, w_out):
    widened = acts.astype(jnp.float32)
    factor = lax.rsqrt(lax.optimization_barrier(jnp.mean(widened * widened, axis=1)) + EPS)
    normed = (widened * norm_gain).astype(jnp.bfloat16)
    proj_acc = lax.dot_general(normed, w_in.reshape(3 * CH, D), (((1,), (1,)), ((), ())), preferred_element_type=jnp.float32)
    u_proj = (proj_acc * factor[:, None]).reshape(SEQ, 3, CH)
    padded = jnp.pad(u_proj, ((SHORT - 1, 0), (0, 0), (0, 0)))
    mixed_out = short_filter[:, :, 0] * u_proj
    for j in range(1, SHORT):
        mixed_out = mixed_out + short_filter[:, :, j] * padded[SHORT - 1 - j:SHORT - 1 - j + SEQ]
    query_part = mixed_out[:, 0]
    key_part = mixed_out[:, 1]
    value_part = mixed_out[:, 2]
    filter_vals = filter_taps * jnp.exp(-decay_rate[:, None] * jnp.arange(FLEN, dtype=jnp.float32)[None, :])
    product = key_part * value_part
    padded_prod = jnp.pad(product, ((FLEN - 1, 0), (0, 0)))
    long_conv = filter_vals[:, 0] * product
    for j in range(1, FLEN):
        long_conv = long_conv + filter_vals[:, j] * padded_prod[FLEN - 1 - j:FLEN - 1 - j + SEQ]
    y_local = (query_part * long_conv).astype(jnp.bfloat16)
    return (widened + jnp.dot(y_local, w_out, preferred_element_type=jnp.float32)).astype(jnp.bfloat16)

def reference(fresh_acts, carried, norm_gain, w_in, short_filter, filter_taps, decay_rate, w_out):
    results = []
    for s in range(N_SECTION):
        section_rows = []
        for k in range(TICKS):
            if s == 0:
                layer_in = fresh_acts[k]
            elif k == 0:
                layer_in = carried[s]
            else:
                layer_in = results[s - 1][k - 1]
            section_rows.append(hyena_layer(layer_in, norm_gain[s], w_in[s], short_filter[s], filter_taps[s], decay_rate[s], w_out[s]))
        results.append(section_rows)
    return jnp.stack([jnp.stack(section_rows) for section_rows in results])
```

```python
import functools

import jax
import jax.numpy as jnp
from jax import lax
from jax.experimental import pallas as pl
from jax.experimental.pallas import tpu as pltpu
from jax.sharding import PartitionSpec as P

EPS = 1e-06
VMEM_LIMIT = 48 * 1024 * 1024
PAD = 8


def plan(section_count, tick_count):
    wave_count = min(section_count, tick_count)
    waves = [[[] for _ in range(section_count)] for _ in range(wave_count)]
    where = {}
    for k in range(tick_count):
        for s in range(section_count):
            first = where[s - 1, k - 1][0] + 1 if s > 0 and k > 0 else 0
            last = wave_count - 1 - min(section_count - 1 - s, tick_count - 1 - k)
            best = min(range(first, last + 1), key=lambda w: (len(waves[w][s]), w))
            where[s, k] = (best, len(waves[best][s]))
            waves[best][s].append(k)
    return waves, where


def split_dp(dp_count):
    core = 2 if dp_count % 2 == 0 else 1
    chips = dp_count // core
    near = 1
    while near * near * 4 <= chips:
        near *= 2
    return chips // near, near, core


def pick(section_idx, options):
    distinct = []
    for s, value in enumerate(options):
        if value is None:
            continue
        for held, members in distinct:
            if held is value:
                members.append(s)
                break
        else:
            distinct.append((value, [s]))
    result = distinct[0][0]
    for value, members in distinct[1:]:
        mine = functools.reduce(jnp.logical_or, [section_idx == s for s in members])
        result = jnp.where(mine, value, result)
    return result


def mix_kernel(group, tok_len, model_width, rank_ref, *refs):
    pieces = refs[:group]
    w_ref, gain_ref, short_ref, long_ref, y_ref = refs[group : group + 5]
    norm_ref, acc_ref, sq_ref, pad_ref = refs[group + 5 :]
    step = pl.program_id(0)
    feat = pieces[0].shape[2]
    rows = pieces[0].shape[1]
    chan = w_ref.shape[1]
    low = lax.rem(rank_ref[0], group)

    @pl.when(step == 0)
    def _():
        acc_ref[...] = jnp.zeros_like(acc_ref)
        sq_ref[...] = jnp.zeros_like(sq_ref)

    for q in range(group):
        start = pl.multiple_of((low ^ q) * feat, feat)
        wide = pieces[q][0].astype(jnp.float32)
        norm_ref[:, pl.ds(start, feat)] = (wide * gain_ref[:, pl.ds(start, feat)]).astype(jnp.bfloat16)
        squares = wide * wide
        lanes = min(feat, 128)
        part = squares[:, :lanes]
        for j in range(1, feat // lanes):
            part = part + squares[:, j * lanes : (j + 1) * lanes]
        sq_ref[...] += part
    for i in range(3):
        acc_ref[i] += lax.dot_general(
            norm_ref[...], w_ref[i], (((1,), (1,)), ((), ())), preferred_element_type=jnp.float32
        )

    @pl.when(step == pl.num_programs(0) - 1)
    def _():
        pad_ref[0:PAD, :] = jnp.zeros((PAD, chan), jnp.float32)
        taps = short_ref.shape[0] // 3
        for slot in range(rows // tok_len):
            low_row = slot * tok_len
            here = slice(low_row, low_row + tok_len)
            total = jnp.sum(sq_ref[here, :], axis=1, keepdims=True)
            factor = lax.rsqrt(total / model_width + EPS)

            def branch(i):
                u = acc_ref[i, here, :] * factor
                pad_ref[PAD : PAD + tok_len, :] = u
                z = short_ref[i * taps : i * taps + 1, :] * u
                for j in range(1, taps):
                    z = z + short_ref[i * taps + j : i * taps + j + 1, :] * pad_ref[PAD - j : PAD - j + tok_len, :]
                return z

            key = branch(1)
            product = key * branch(2)
            query = branch(0)
            acc_ref[0, here, :] = query
            pad_ref[PAD : PAD + tok_len, :] = product
            width = min(chan, 128)
            for c in range(0, chan, width):
                cols = slice(c, c + width)
                conv = [None] * (tok_len // 8)
                for b in range(8):
                    moved = [pad_ref[PAD - b + 8 * i : PAD - b + 8 * i + 8, cols] for i in range(tok_len // 8)]
                    for a in range(long_ref.shape[0] // 8):
                        tap = long_ref[8 * a + b : 8 * a + b + 1, cols]
                        for i in range(a, tok_len // 8):
                            term = tap * moved[i - a]
                            conv[i] = term if conv[i] is None else conv[i] + term
                for i in range(tok_len // 8):
                    at = low_row + 8 * i
                    acc_ref[1, at : at + 8, cols] = conv[i]
            y_ref[here, :] = (acc_ref[0, here, :] * acc_ref[1, here, :]).astype(jnp.bfloat16)


def mix(pieces, w_in, gain, short_rows, long_rows, rank, tok_len):
    group = len(pieces)
    far, rows, feat = pieces[0].shape
    branches, chan, model_width = w_in.shape
    wide = group * feat
    kernel = functools.partial(mix_kernel, group, tok_len, model_width)
    return pl.pallas_call(
        kernel,
        grid_spec=pltpu.PrefetchScalarGridSpec(
            num_scalar_prefetch=1,
            grid=(far,),
            in_specs=[pl.BlockSpec((1, rows, feat), lambda d, r: (d, 0, 0))] * group
            + [
                pl.BlockSpec((branches, chan, wide), lambda d, r: (0, 0, (r[0] // group) ^ d)),
                pl.BlockSpec((1, wide), lambda d, r: (0, (r[0] // group) ^ d)),
                pl.BlockSpec(short_rows.shape, lambda d, r: (0, 0)),
                pl.BlockSpec(long_rows.shape, lambda d, r: (0, 0)),
            ],
            out_specs=pl.BlockSpec((rows, chan), lambda d, r: (0, 0)),
            scratch_shapes=[
                pltpu.VMEM((rows, wide), jnp.bfloat16),
                pltpu.VMEM((branches, rows, chan), jnp.float32),
                pltpu.VMEM((rows, min(feat, 128)), jnp.float32),
                pltpu.VMEM((PAD + tok_len, chan), jnp.float32),
            ],
        ),
        out_shape=jax.ShapeDtypeStruct((rows, chan), jnp.bfloat16),
        compiler_params=pltpu.CompilerParams(
            dimension_semantics=("arbitrary",), vmem_limit_bytes=VMEM_LIMIT
        ),
        cost_estimate=pl.CostEstimate(
            flops=2 * rows * branches * chan * model_width,
            bytes_accessed=2 * branches * chan * model_width + 2 * rows * model_width,
            transcendentals=0,
        ),
        name="norm_project_mix",
    )(rank, *pieces, w_in, gain, short_rows, long_rows)


def out_kernel(group, rank_ref, *refs):
    pieces = refs[:group]
    w_ref, own_ref, result_ref, cat_ref, acc_ref = refs[group:]
    step = pl.program_id(0)
    chan = pieces[0].shape[2]
    low = lax.rem(rank_ref[0], group)

    @pl.when(step == 0)
    def _():
        acc_ref[...] = own_ref[...].astype(jnp.float32)

    if chan % 128 == 0:
        for q in range(group):
            start = pl.multiple_of((low ^ q) * chan, chan)
            cat_ref[:, pl.ds(start, chan)] = pieces[q][0]
        acc_ref[...] += jnp.dot(cat_ref[...], w_ref[...], preferred_element_type=jnp.float32)
    else:
        for q in range(group):
            start = pl.multiple_of((low ^ q) * chan, chan)
            acc_ref[...] += jnp.dot(
                pieces[q][0], w_ref[pl.ds(start, chan), :], preferred_element_type=jnp.float32
            )

    @pl.when(step == pl.num_programs(0) - 1)
    def _():
        result_ref[...] = acc_ref[...].astype(jnp.bfloat16)


def project_out(pieces, w_out, own, rank):
    group = len(pieces)
    far, rows, chan = pieces[0].shape
    feat = w_out.shape[1]
    wide = group * chan
    return pl.pallas_call(
        functools.partial(out_kernel, group),
        grid_spec=pltpu.PrefetchScalarGridSpec(
            num_scalar_prefetch=1,
            grid=(far,),
            in_specs=[pl.BlockSpec((1, rows, chan), lambda d, r: (d, 0, 0))] * group
            + [
                pl.BlockSpec((wide, feat), lambda d, r: ((r[0] // group) ^ d, 0)),
                pl.BlockSpec((rows, feat), lambda d, r: (0, 0)),
            ],
            out_specs=pl.BlockSpec((rows, feat), lambda d, r: (0, 0)),
            scratch_shapes=[
                pltpu.VMEM((rows, wide), jnp.bfloat16),
                pltpu.VMEM((rows, feat), jnp.float32),
            ],
        ),
        out_shape=jax.ShapeDtypeStruct((rows, feat), jnp.bfloat16),
        compiler_params=pltpu.CompilerParams(
            dimension_semantics=("arbitrary",), vmem_limit_bytes=VMEM_LIMIT
        ),
        cost_estimate=pl.CostEstimate(
            flops=2 * rows * w_out.shape[0] * feat,
            bytes_accessed=2 * w_out.shape[0] * feat + 2 * rows * w_out.shape[0],
            transcendentals=0,
        ),
        name="project_out",
    )(rank, *pieces, w_out, own)


def body(section_count, dp_count, fresh_acts, carried, norm_gain, w_in, short_filter, filter_taps, decay_rate, w_out):
    tick_count, tok_len, _ = fresh_acts.shape
    far, near, core = split_dp(dp_count)
    group = near * core
    waves, where = plan(section_count, tick_count)
    section_idx = lax.axis_index("section")
    rank_idx = lax.axis_index("dp")
    rank = rank_idx.astype(jnp.int32).reshape(1)

    def swap(value, offset):
        return lax.ppermute(value, "dp", [(r, r ^ offset) for r in range(dp_count)])

    def onward(value, offset):
        pairs = [
            (s * dp_count + r, (s + 1) % section_count * dp_count + (r ^ offset))
            for s in range(section_count)
            for r in range(dp_count)
        ]
        return lax.ppermute(value, ("section", "dp"), pairs)

    def spread(line):
        pieces = []
        for x in range(near):
            piece = line if x == 0 else swap(line, x * core)
            pieces.append(piece)
            for c in range(1, core):
                pieces.append(swap(piece, c))
        return pieces

    lags = jnp.arange(filter_taps.shape[2], dtype=jnp.float32)
    long_rows = (filter_taps[0] * jnp.exp(-decay_rate[0][:, None] * lags[None, :])).T
    short_rows = short_filter[0].transpose(0, 2, 1).reshape(-1, short_filter.shape[2])

    waiting = carried[0]
    results = {}
    for w, slots in enumerate(waves):
        slot_count = max(len(ticks) for ticks in slots)
        sources = []
        for i in range(slot_count):
            options = []
            for s in range(section_count):
                if w == 0:
                    ticks = slots[s]
                    if i >= len(ticks):
                        options.append(None)
                    elif s == 0:
                        options.append(fresh_acts[ticks[i]])
                    else:
                        options.append(waiting)
                else:
                    ticks = slots[(s + 1) % section_count]
                    if i >= len(ticks):
                        options.append(None)
                    elif s + 1 == section_count:
                        options.append(fresh_acts[ticks[i]])
                    else:
                        options.append(results[s, ticks[i] - 1])
            sources.append(pick(section_idx, options))
        source = jnp.concatenate(sources, axis=0)
        if w == 0:
            blocks = [source] + [swap(source, d * group) for d in range(1, far)]
        else:
            blocks = [onward(source, d * group) for d in range(far)]
        y = mix(spread(jnp.stack(blocks)), w_in[0], norm_gain, short_rows, long_rows, rank, tok_len)
        y_blocks = [y] + [swap(y, d * group) for d in range(1, far)]
        produced = project_out(spread(jnp.stack(y_blocks)), w_out[0], blocks[0], rank)
        made = [produced[i * tok_len : (i + 1) * tok_len] for i in range(slot_count)]
        for s in range(section_count):
            for i, k in enumerate(slots[s]):
                results[s, k] = made[i]
    outputs = []
    for k in range(tick_count):
        outputs.append(pick(section_idx, [results[s, k] for s in range(section_count)]))
    return jnp.stack(outputs)[None]


def solution(mesh):
    run = functools.partial(body, mesh.shape["section"], mesh.shape["dp"])
    return jax.shard_map(
        run,
        mesh=mesh,
        in_specs=(
            P(None, None, "dp"),
            P("section", None, "dp"),
            P("section", None),
            P("section", None, "dp", None),
            P("section", None, "dp", None),
            P("section", "dp", None),
            P("section", "dp"),
            P("section", None, "dp"),
        ),
        out_specs=P("section", None, None, "dp"),
        check_vma=False,
    )
```

```python
import functools
import itertools
import math

import jax
import jax.numpy as jnp
from jax import lax
from jax.experimental import pallas as pl
from jax.experimental.pallas import tpu as pltpu
from jax.sharding import PartitionSpec as P

EPS = 1e-06
VMEM_LIMIT = 48 * 1024 * 1024
PAD = 8


def plan(section_count, tick_count):
    wave_count = min(section_count, tick_count)
    waves = [[[] for _ in range(section_count)] for _ in range(wave_count)]
    where = {}
    for k in range(tick_count):
        for s in range(section_count):
            first = where[s - 1, k - 1][0] + 1 if s > 0 and k > 0 else 0
            last = wave_count - 1 - min(section_count - 1 - s, tick_count - 1 - k)
            best = min(range(first, last + 1), key=lambda w: (len(waves[w][s]), w))
            where[s, k] = (best, len(waves[best][s]))
            waves[best][s].append(k)
    return waves


def core_count(dp_count):
    return 2 if dp_count % 2 == 0 else 1


def step_count(chips):
    return math.gcd(chips, 4)


def pick(section_idx, options):
    distinct = []
    for s, value in enumerate(options):
        if value is None:
            continue
        for held, members in distinct:
            if held is value:
                members.append(s)
                break
        else:
            distinct.append((value, [s]))
    result = distinct[0][0]
    for value, members in distinct[1:]:
        mine = functools.reduce(jnp.logical_or, [section_idx == s for s in members])
        result = jnp.where(mine, value, result)
    return result


def mix_kernel(group, tok_len, model_width, rank_ref, *refs):
    pieces = refs[:group]
    w_ref, gain_ref, short_ref, long_ref, y_ref = refs[group : group + 5]
    norm_ref, acc_ref, sq_ref, pad_ref = refs[group + 5 :]
    step = pl.program_id(0)
    chips, rows, feat = pieces[0].shape
    chan = w_ref.shape[1]
    low = lax.rem(rank_ref[0], group)

    @pl.when(step == 0)
    def _():
        acc_ref[...] = jnp.zeros_like(acc_ref)
        sq_ref[...] = jnp.zeros_like(sq_ref)

    for j, q in itertools.product(range(chips), range(group)):
        start = pl.multiple_of((j * group + (low ^ q)) * feat, feat)
        wide = pieces[q][j].astype(jnp.float32)
        norm_ref[:, pl.ds(start, feat)] = (wide * gain_ref[:, pl.ds(start, feat)]).astype(jnp.bfloat16)
        squares = wide * wide
        lanes = min(feat, 128)
        part = squares[:, :lanes]
        for n in range(1, feat // lanes):
            part = part + squares[:, n * lanes : (n + 1) * lanes]
        sq_ref[...] += part
    for i in range(3):
        acc_ref[i] += lax.dot_general(
            norm_ref[...], w_ref[i], (((1,), (1,)), ((), ())), preferred_element_type=jnp.float32
        )

    @pl.when(step == pl.num_programs(0) - 1)
    def _():
        pad_ref[0:PAD, :] = jnp.zeros((PAD, chan), jnp.float32)
        taps = short_ref.shape[0] // 3
        for slot in range(rows // tok_len):
            low_row = slot * tok_len
            here = slice(low_row, low_row + tok_len)
            total = jnp.sum(sq_ref[here, :], axis=1, keepdims=True)
            factor = lax.rsqrt(total / model_width + EPS)

            def branch(i):
                u = acc_ref[i, here, :] * factor
                pad_ref[PAD : PAD + tok_len, :] = u
                z = short_ref[i * taps : i * taps + 1, :] * u
                for j in range(1, taps):
                    z = z + short_ref[i * taps + j : i * taps + j + 1, :] * pad_ref[PAD - j : PAD - j + tok_len, :]
                return z

            key = branch(1)
            product = key * branch(2)
            query = branch(0)
            acc_ref[0, here, :] = query
            pad_ref[PAD : PAD + tok_len, :] = product
            width = min(chan, 128)
            for c in range(0, chan, width):
                cols = slice(c, c + width)
                conv = [None] * (tok_len // 8)
                for b in range(8):
                    moved = [pad_ref[PAD - b + 8 * i : PAD - b + 8 * i + 8, cols] for i in range(tok_len // 8)]
                    for a in range(long_ref.shape[0] // 8):
                        tap = long_ref[8 * a + b : 8 * a + b + 1, cols]
                        for i in range(a, tok_len // 8):
                            term = tap * moved[i - a]
                            conv[i] = term if conv[i] is None else conv[i] + term
                for i in range(tok_len // 8):
                    at = low_row + 8 * i
                    acc_ref[1, at : at + 8, cols] = conv[i]
            y_ref[here, :] = (acc_ref[0, here, :] * acc_ref[1, here, :]).astype(jnp.bfloat16)


def mix(pieces, w_in, gain, short_rows, long_rows, rank, tok_len):
    group = len(pieces)
    chips, rows, feat = pieces[0].shape
    branches, chan, model_width = w_in.shape
    steps = step_count(chips)
    wide = model_width // steps
    kernel = functools.partial(mix_kernel, group, tok_len, model_width)
    return pl.pallas_call(
        kernel,
        grid_spec=pltpu.PrefetchScalarGridSpec(
            num_scalar_prefetch=1,
            grid=(steps,),
            in_specs=[pl.BlockSpec((chips // steps, rows, feat), lambda d, r: (d, 0, 0))] * group
            + [
                pl.BlockSpec((branches, chan, wide), lambda d, r: (0, 0, d)),
                pl.BlockSpec((1, wide), lambda d, r: (0, d)),
                pl.BlockSpec(short_rows.shape, lambda d, r: (0, 0)),
                pl.BlockSpec(long_rows.shape, lambda d, r: (0, 0)),
            ],
            out_specs=pl.BlockSpec((rows, chan), lambda d, r: (0, 0)),
            scratch_shapes=[
                pltpu.VMEM((rows, wide), jnp.bfloat16),
                pltpu.VMEM((branches, rows, chan), jnp.float32),
                pltpu.VMEM((rows, min(feat, 128)), jnp.float32),
                pltpu.VMEM((PAD + tok_len, chan), jnp.float32),
            ],
        ),
        out_shape=jax.ShapeDtypeStruct((rows, chan), jnp.bfloat16),
        compiler_params=pltpu.CompilerParams(
            dimension_semantics=("arbitrary",), vmem_limit_bytes=VMEM_LIMIT
        ),
        cost_estimate=pl.CostEstimate(
            flops=2 * rows * branches * chan * model_width,
            bytes_accessed=2 * branches * chan * model_width + 2 * rows * model_width,
            transcendentals=0,
        ),
        name="norm_project_mix",
    )(rank, *pieces, w_in, gain, short_rows, long_rows)


def out_kernel(group, rank_ref, *refs):
    pieces = refs[:group]
    w_ref, own_ref, result_ref, cat_ref, acc_ref = refs[group:]
    step = pl.program_id(0)
    chips, _, chan = pieces[0].shape
    low = lax.rem(rank_ref[0], group)

    @pl.when(step == 0)
    def _():
        acc_ref[...] = own_ref[...].astype(jnp.float32)

    if chan % 128 == 0:
        for j, q in itertools.product(range(chips), range(group)):
            start = pl.multiple_of((j * group + (low ^ q)) * chan, chan)
            cat_ref[:, pl.ds(start, chan)] = pieces[q][j]
        acc_ref[...] += jnp.dot(cat_ref[...], w_ref[...], preferred_element_type=jnp.float32)
    else:
        for j, q in itertools.product(range(chips), range(group)):
            start = pl.multiple_of((j * group + (low ^ q)) * chan, chan)
            acc_ref[...] += jnp.dot(
                pieces[q][j], w_ref[pl.ds(start, chan), :], preferred_element_type=jnp.float32
            )

    @pl.when(step == pl.num_programs(0) - 1)
    def _():
        result_ref[...] = acc_ref[...].astype(jnp.bfloat16)


def project_out(pieces, w_out, own, rank):
    group = len(pieces)
    chips, rows, chan = pieces[0].shape
    feat = w_out.shape[1]
    steps = step_count(chips)
    wide = w_out.shape[0] // steps
    return pl.pallas_call(
        functools.partial(out_kernel, group),
        grid_spec=pltpu.PrefetchScalarGridSpec(
            num_scalar_prefetch=1,
            grid=(steps,),
            in_specs=[pl.BlockSpec((chips // steps, rows, chan), lambda d, r: (d, 0, 0))] * group
            + [
                pl.BlockSpec((wide, feat), lambda d, r: (d, 0)),
                pl.BlockSpec((rows, feat), lambda d, r: (0, 0)),
            ],
            out_specs=pl.BlockSpec((rows, feat), lambda d, r: (0, 0)),
            scratch_shapes=[
                pltpu.VMEM((rows, wide), jnp.bfloat16),
                pltpu.VMEM((rows, feat), jnp.float32),
            ],
        ),
        out_shape=jax.ShapeDtypeStruct((rows, feat), jnp.bfloat16),
        compiler_params=pltpu.CompilerParams(
            dimension_semantics=("arbitrary",), vmem_limit_bytes=VMEM_LIMIT
        ),
        cost_estimate=pl.CostEstimate(
            flops=2 * rows * w_out.shape[0] * feat,
            bytes_accessed=2 * w_out.shape[0] * feat + 2 * rows * w_out.shape[0],
            transcendentals=0,
        ),
        name="project_out",
    )(rank, *pieces, w_out, own)


def body(section_count, dp_count, fresh_acts, carried, norm_gain, w_in, short_filter, filter_taps, decay_rate, w_out):
    tick_count, tok_len, _ = fresh_acts.shape
    core = core_count(dp_count)
    same_core = [list(range(c, dp_count, core)) for c in range(core)]
    waves = plan(section_count, tick_count)
    section_idx = lax.axis_index("section")
    rank = lax.axis_index("dp").astype(jnp.int32).reshape(1)

    def spread(own):
        line = lax.all_gather(own, "dp", axis=0, axis_index_groups=same_core)
        pieces = [line]
        for c in range(1, core):
            pieces.append(lax.ppermute(line, "dp", [(r, r ^ c) for r in range(dp_count)]))
        return pieces

    lags = jnp.arange(filter_taps.shape[2], dtype=jnp.float32)
    long_rows = (filter_taps[0] * jnp.exp(-decay_rate[0][:, None] * lags[None, :])).T
    short_rows = short_filter[0].transpose(0, 2, 1).reshape(-1, short_filter.shape[2])

    waiting = carried[0]
    results = {}
    for w, slots in enumerate(waves):
        slot_count = max(len(ticks) for ticks in slots)
        sources = []
        for i in range(slot_count):
            options = []
            for s in range(section_count):
                if w == 0:
                    ticks = slots[s]
                    if i >= len(ticks):
                        options.append(None)
                    elif s == 0:
                        options.append(fresh_acts[ticks[i]])
                    else:
                        options.append(waiting)
                else:
                    ticks = slots[(s + 1) % section_count]
                    if i >= len(ticks):
                        options.append(None)
                    elif s + 1 == section_count:
                        options.append(fresh_acts[ticks[i]])
                    else:
                        options.append(results[s, ticks[i] - 1])
            sources.append(pick(section_idx, options))
        if w > 0:
            shift = [(s, (s + 1) % section_count) for s in range(section_count)]
            sources = [lax.ppermute(source, "section", shift) for source in sources]
        made = []
        for own in sources:
            y = mix(spread(own), w_in[0], norm_gain, short_rows, long_rows, rank, tok_len)
            made.append(project_out(spread(y), w_out[0], own, rank))
        for s in range(section_count):
            for i, k in enumerate(slots[s]):
                results[s, k] = made[i]
    outputs = []
    for k in range(tick_count):
        outputs.append(pick(section_idx, [results[s, k] for s in range(section_count)]))
    return jnp.stack(outputs)[None]


def solution(mesh):
    run = functools.partial(body, mesh.shape["section"], mesh.shape["dp"])
    return jax.shard_map(
        run,
        mesh=mesh,
        in_specs=(
            P(None, None, "dp"),
            P("section", None, "dp"),
            P("section", None),
            P("section", None, "dp", None),
            P("section", None, "dp", None),
            P("section", "dp", None),
            P("section", "dp"),
            P("section", None, "dp"),
        ),
        out_specs=P("section", None, None, "dp"),
        check_vma=False,
    )
```

```python
import functools

import jax
import jax.numpy as jnp
from jax import lax
from jax.experimental import pallas as pl
from jax.experimental.pallas import tpu as pltpu
from jax.sharding import PartitionSpec as P

EPS = 1e-06
VMEM_LIMIT = 12 * 1024 * 1024
PAD = 8


def plan(section_count, tick_count):
    wave_count = min(section_count, tick_count)
    waves = [[[] for _ in range(section_count)] for _ in range(wave_count)]
    where = {}
    for k in range(tick_count):
        for s in range(section_count):
            first = where[s - 1, k - 1][0] + 1 if s > 0 and k > 0 else 0
            last = wave_count - 1 - min(section_count - 1 - s, tick_count - 1 - k)
            best = min(range(first, last + 1), key=lambda w: (len(waves[w][s]), w))
            where[s, k] = (best, len(waves[best][s]))
            waves[best][s].append(k)
    return waves


def split_dp(dp_count):
    core = 2 if dp_count % 2 == 0 else 1
    chips = dp_count // core
    near = 1
    while near * near * 4 <= chips:
        near *= 2
    return chips // near, near, core


def pick(section_idx, options):
    distinct = []
    for s, value in enumerate(options):
        if value is None:
            continue
        for held, members in distinct:
            if held is value:
                members.append(s)
                break
        else:
            distinct.append((value, [s]))
    result = distinct[0][0]
    for value, members in distinct[1:]:
        mine = functools.reduce(jnp.logical_or, [section_idx == s for s in members])
        result = jnp.where(mine, value, result)
    return result


def project_cells(cells, sides, rank_ref, w_ref, gain_ref, acc_ref, sq_ref, ready=None):
    feat = sides[0].shape[2]
    core = len(sides)
    lanes = sq_ref.shape[1]
    chip, side = lax.div(rank_ref[0], core), lax.rem(rank_ref[0], core)
    for n, cell in enumerate(cells):
        normed, columns = [], []
        for c in range(core):
            values = sides[c][n].astype(jnp.float32)
            columns.append(pl.ds(pl.multiple_of(((chip ^ cell) * core + (side ^ c)) * feat, feat), feat))
            normed.append((values * gain_ref[:, columns[c]]).astype(jnp.bfloat16))
            squares = values * values
            part = squares[:, :lanes]
            for m in range(1, feat // lanes):
                part = part + squares[:, m * lanes : (m + 1) * lanes]
            sq_ref[...] = part if n == 0 and c == 0 else sq_ref[...] + part
        if ready is not None:
            ready(n)
        for i in range(w_ref.shape[0]):
            terms = [
                lax.dot_general(
                    normed[c],
                    w_ref[i, :, columns[c]],
                    (((1,), (1,)), ((), ())),
                    preferred_element_type=jnp.float32,
                )
                for c in range(core)
            ]
            term = functools.reduce(jnp.add, terms)
            acc_ref[i] = term if n == 0 else acc_ref[i] + term


def early_kernel(cells, core, rank_ref, *refs):
    sides = refs[:core]
    w_ref, gain_ref, acc_ref, sq_ref = refs[core : core + 4]
    project_cells(cells, sides, rank_ref, w_ref, gain_ref, acc_ref, sq_ref)


def first_kernel(cells, later, core, rank_ref, *refs):
    sides = refs[:core]
    w_far, gain_ref, taps_ref, decay_ref, acc_ref, sq_ref, w_ref, gain_here, long_ref = refs[core : core + 9]
    sems = refs[-1]
    wide = core * sides[0].shape[2]
    chip = lax.div(rank_ref[0], core)
    copies = []
    for n, cell in enumerate(cells + later):
        columns = pl.ds(pl.multiple_of((chip ^ cell) * wide, wide), wide)
        copies.append(
            [
                pltpu.make_async_copy(w_far.at[i, :, columns], w_ref.at[i, :, columns], sems.at[n, i])
                for i in range(w_far.shape[0])
            ]
        )
    for group in copies:
        for copy in group:
            copy.start()

    gain_here[...] = gain_ref[...]
    lags = lax.broadcasted_iota(jnp.int32, long_ref.shape, 0).astype(jnp.float32)
    long_ref[...] = taps_ref[...].T * jnp.exp(-decay_ref[...] * lags)

    def ready(n):
        for copy in copies[n]:
            copy.wait()

    project_cells(cells, sides, rank_ref, w_ref, gain_ref, acc_ref, sq_ref, ready)
    for n in range(len(cells), len(copies)):
        ready(n)


def mix_kernel(cells, core, rank_ref, *refs):
    sides = refs[:core]
    w_ref, gain_ref, acc_in, sq_in, short_ref, long_ref, y_ref = refs[core : core + 7]
    acc_ref, sq_ref, pad_ref, query_ref = refs[core + 7 :]
    branches, chan, model_width = w_ref.shape
    tok_len = y_ref.shape[0]
    project_cells(cells, sides, rank_ref, w_ref, gain_ref, acc_ref, sq_ref)

    total = jnp.sum(sq_in[...] + sq_ref[...], axis=1, keepdims=True)
    factor = lax.rsqrt(total / model_width + EPS)
    taps = short_ref.shape[0] // branches
    pad_ref[0:PAD, :] = jnp.zeros((PAD, chan), jnp.float32)

    def branch(i):
        u = (acc_in[i] + acc_ref[i]) * factor
        pad_ref[PAD : PAD + tok_len, :] = u
        z = short_ref[i * taps : i * taps + 1, :] * u
        for j in range(1, taps):
            z = z + short_ref[i * taps + j : i * taps + j + 1, :] * pad_ref[PAD - j : PAD - j + tok_len, :]
        return z

    query_ref[...] = branch(1)
    product = query_ref[...] * branch(2)
    query_ref[...] = branch(0)
    pad_ref[PAD : PAD + tok_len, :] = product
    width = min(chan, 128)
    tiles = tok_len // 8
    for c in range(0, chan, width):
        cols = slice(c, c + width)
        conv = [None] * tiles
        for b in range(8):
            moved = [pad_ref[PAD - b + 8 * i : PAD - b + 8 * i + 8, cols] for i in range(tiles)]
            for a in range(long_ref.shape[0] // 8):
                tap = long_ref[8 * a + b : 8 * a + b + 1, cols]
                for i in range(a, tiles):
                    term = tap * moved[i - a]
                    conv[i] = term if conv[i] is None else conv[i] + term
        for i in range(0, tiles, 2):
            at = slice(8 * i, 8 * i + 16)
            both = jnp.concatenate(conv[i : i + 2], axis=0)
            y_ref[at, cols] = (query_ref[at, cols] * both).astype(jnp.bfloat16)


def out_kernel(parts, core, rank_ref, *refs):
    w_ref, own_ref, result_ref, acc_ref = refs[-4:]
    chan = refs[0].shape[2]
    chip, side = lax.div(rank_ref[0], core), lax.rem(rank_ref[0], core)
    acc_ref[...] = own_ref[...].astype(jnp.float32)
    for p, cells in enumerate(parts):
        sides = refs[p * core : (p + 1) * core]
        for n, cell in enumerate(cells):
            terms = []
            for c in range(core):
                at = pl.multiple_of(((chip ^ cell) * core + (side ^ c)) * chan, chan)
                terms.append(
                    jnp.dot(sides[c][n], w_ref[pl.ds(at, chan), :], preferred_element_type=jnp.float32)
                )
            acc_ref[...] += functools.reduce(jnp.add, terms)
    result_ref[...] = acc_ref[...].astype(jnp.bfloat16)


def in_vmem(count):
    return [pl.BlockSpec(memory_space=pltpu.VMEM)] * count


def call(kernel, operands, outs, scratch, flops, name, far_operands=(), moved=0):
    specs = [pl.BlockSpec(memory_space=pltpu.SMEM)] + in_vmem(len(operands) - 1)
    for n in far_operands:
        specs[n] = pl.BlockSpec(memory_space=pltpu.HBM)
    return pl.pallas_call(
        kernel,
        in_specs=specs,
        out_specs=in_vmem(len(outs)),
        out_shape=outs,
        scratch_shapes=scratch,
        compiler_params=pltpu.CompilerParams(vmem_limit_bytes=VMEM_LIMIT),
        cost_estimate=pl.CostEstimate(flops=flops, bytes_accessed=flops // 1024 + moved, transcendentals=0),
        name=name,
    )(*operands)


def project_early(part, later, w_in, gain, rank, taps=None, decay=None):
    cells, sides = part
    core = len(sides)
    rows, feat = sides[0].shape[1:]
    branches, chan, model_width = w_in.shape
    outs = [
        jax.ShapeDtypeStruct((branches, rows, chan), jnp.float32),
        jax.ShapeDtypeStruct((rows, min(feat, 128)), jnp.float32),
    ]
    scratch = []
    flops = 2 * rows * branches * chan * feat * core * len(cells)
    operands = [rank, *sides, w_in, gain]
    if taps is not None:
        operands += [taps, decay]
        operands[1 + core] = pltpu.with_memory_space_constraint(w_in, pltpu.HBM)
        outs.append(pltpu.VMEM(w_in.shape, w_in.dtype))
        outs.append(pltpu.VMEM(gain.shape, gain.dtype))
        outs.append(pltpu.VMEM(taps.shape[::-1], taps.dtype))
        scratch.append(pltpu.SemaphoreType.DMA((len(cells) + len(later), branches)))
        kernel = functools.partial(first_kernel, cells, later, core)
        return call(kernel, operands, outs, scratch, flops, "load_project", (1 + core,), 4 * w_in.size)
    return call(functools.partial(early_kernel, cells, core), operands, outs, scratch, flops, "project_early")


def mix(part, w_in, gain, acc, sq, short_rows, long_rows, rank):
    cells, sides = part
    core = len(sides)
    rows, feat = sides[0].shape[1:]
    branches, chan, _ = w_in.shape
    scratch = [
        pltpu.VMEM(acc.shape, jnp.float32),
        pltpu.VMEM(sq.shape, jnp.float32),
        pltpu.VMEM((PAD + rows, chan), jnp.float32),
        pltpu.VMEM((rows, chan), jnp.float32),
    ]
    return call(
        functools.partial(mix_kernel, cells, core),
        [rank, *sides, w_in, gain, acc, sq, short_rows, long_rows],
        [jax.ShapeDtypeStruct((rows, chan), jnp.bfloat16)],
        scratch,
        2 * rows * branches * chan * feat * core * len(cells),
        "project_mix",
    )[0]


def project_out(parts, w_out, own, rank):
    core = len(parts[0][1])
    rows, feat = own.shape
    arrays = [side for _, sides in parts for side in sides]
    return call(
        functools.partial(out_kernel, [cells for cells, _ in parts], core),
        [rank, *arrays, w_out, own],
        [jax.ShapeDtypeStruct((rows, feat), jnp.bfloat16)],
        [pltpu.VMEM((rows, feat), jnp.float32)],
        2 * rows * w_out.shape[0] * feat,
        "project_out",
    )[0]


def body(section_count, dp_count, fresh_acts, carried, norm_gain, w_in, short_filter, filter_taps, decay_rate, w_out):
    tick_count, tok_len, _ = fresh_acts.shape
    far, near, core = split_dp(dp_count)
    group = near * core
    waves = plan(section_count, tick_count)
    section_idx = lax.axis_index("section")
    rank_idx = lax.axis_index("dp")
    rank = rank_idx.astype(jnp.int32).reshape(1)

    def swap(value, offset):
        return lax.ppermute(value, "dp", [(r, r ^ offset) for r in range(dp_count)])

    def onward(value, offset):
        pairs = [
            (s * dp_count + r, (s + 1) % section_count * dp_count + (r ^ offset))
            for s in range(section_count)
            for r in range(dp_count)
        ]
        return lax.ppermute(value, ("section", "dp"), pairs)

    def after(value, earlier):
        return value if earlier is None else lax.optimization_barrier((value, earlier))[0]

    def gather(source, cross, order):
        source = after(source, order.get("near"))
        blocks = [onward(source, 0) if cross else source]
        blocks += [(onward if cross else swap)(source, d * group) for d in range(1, far)]
        blocks = after(blocks, order.get("early"))
        line = jnp.stack(blocks)
        cells = [d * near for d in range(far)]
        leaving = after(line, order.get("rest"))
        rest = [swap(leaving, d * core) for d in range(1, near)]
        rest = rest[0] if near == 2 else jnp.concatenate(rest)
        more = [cell ^ d for d in range(1, near) for cell in cells]
        early = both_cores(cells, line)
        order["near"], order["rest"] = early[1][-1], rest
        return early, (more, rest), blocks[0]

    def both_cores(cells, line):
        return cells, [line] + [swap(line, c) for c in range(1, core)]

    short_rows = short_filter[0].transpose(0, 2, 1).reshape(-1, short_filter.shape[2])
    w_in_here, gain, loaded = w_in[0], norm_gain, (filter_taps[0], decay_rate)
    waiting = carried[0]
    results = {}
    for w, slots in enumerate(waves):
        slot_count = max(len(ticks) for ticks in slots)
        sources = []
        for i in range(slot_count):
            options = []
            for s in range(section_count):
                if w == 0:
                    ticks = slots[s]
                    if i >= len(ticks):
                        options.append(None)
                    elif s == 0:
                        options.append(fresh_acts[ticks[i]])
                    else:
                        options.append(waiting)
                else:
                    ticks = slots[(s + 1) % section_count]
                    if i >= len(ticks):
                        options.append(None)
                    elif s + 1 == section_count:
                        options.append(fresh_acts[ticks[i]])
                    else:
                        options.append(results[s, ticks[i] - 1])
            sources.append(pick(section_idx, options))
        made = []
        order, y_order = {}, {}
        for source in sources:
            early, (cells, rest), own = gather(source, w > 0, order)
            acc, sq, *loads = project_early(early, cells, w_in_here, gain, rank, *loaded)
            if loads:
                w_in_here, gain, long_rows = [pltpu.with_memory_space_constraint(x, pltpu.VMEM) for x in loads]
                loaded = ()
            order["early"] = acc
            late = both_cores(cells, after(rest, acc))
            acc = after(acc, y_order.get("near"))
            y = mix(late, w_in_here, gain, acc, sq, short_rows, long_rows, rank)
            y_order["near"] = y_order.get("rest")
            early, late, _ = gather(y, False, y_order)
            made.append(project_out([early, both_cores(*late)], w_out[0], own, rank))
        for s in range(section_count):
            for i, k in enumerate(slots[s]):
                results[s, k] = made[i]
    outputs = []
    for k in range(tick_count):
        outputs.append(pick(section_idx, [results[s, k] for s in range(section_count)]))
    return jnp.stack(outputs)[None]


def solution(mesh):
    run = functools.partial(body, mesh.shape["section"], mesh.shape["dp"])
    return jax.shard_map(
        run,
        mesh=mesh,
        in_specs=(
            P(None, None, "dp"),
            P("section", None, "dp"),
            P("section", None),
            P("section", None, "dp", None),
            P("section", None, "dp", None),
            P("section", "dp", None),
            P("section", "dp"),
            P("section", None, "dp"),
        ),
        out_specs=P("section", None, None, "dp"),
        check_vma=False,
    )
```

```python
import functools

import jax
import jax.numpy as jnp
from jax import lax
from jax.experimental import pallas as pl
from jax.experimental.pallas import tpu as pltpu
from jax.sharding import PartitionSpec as P

EPS = 1e-06
SENT = object()
VMEM_LIMIT = 12 * 1024 * 1024
PAD = 8


def plan(section_count, tick_count):
    wave_count = min(section_count, tick_count)
    waves = [[[] for _ in range(section_count)] for _ in range(wave_count)]
    where = {}
    for k in range(tick_count):
        for s in range(section_count):
            first = where[s - 1, k - 1][0] + 1 if s > 0 and k > 0 else 0
            last = wave_count - 1 - min(section_count - 1 - s, tick_count - 1 - k)
            best = min(range(first, last + 1), key=lambda w: (len(waves[w][s]), w))
            where[s, k] = (best, len(waves[best][s]))
            waves[best][s].append(k)
    return waves


def split_dp(dp_count):
    core = 2 if dp_count % 2 == 0 else 1
    chips = dp_count // core
    near = 1
    while near * near * 4 <= chips:
        near *= 2
    return chips // near, near, core


def pick(section_idx, options):
    distinct = []
    for s, value in enumerate(options):
        if value is None:
            continue
        for held, members in distinct:
            if held is value:
                members.append(s)
                break
        else:
            distinct.append((value, [s]))
    result = distinct[0][0]
    for value, members in distinct[1:]:
        mine = functools.reduce(jnp.logical_or, [section_idx == s for s in members])
        result = jnp.where(mine, value, result)
    return result


def routes(far, near):
    if (far, near) == (4, 2):
        return [4, 2, 1], [(1, [4, 2]), (2, [4]), (3, [4])]
    line = [d * near for d in range(far)]
    return line[1:], [(d, line) for d in range(1, near)]


def project_cells(cells, sides, rank_ref, w_ref, gain_ref, acc_ref, sq_ref, ready=None):
    feat = sides[0].shape[2]
    core = len(sides)
    lanes = sq_ref.shape[1]
    chip, side = lax.div(rank_ref[0], core), lax.rem(rank_ref[0], core)
    for n, cell in enumerate(cells):
        normed, columns = [], []
        for c in range(core):
            values = sides[c][n].astype(jnp.float32)
            columns.append(pl.ds(pl.multiple_of(((chip ^ cell) * core + (side ^ c)) * feat, feat), feat))
            normed.append((values * gain_ref[:, columns[c]]).astype(jnp.bfloat16))
            squares = values * values
            part = squares[:, :lanes]
            for m in range(1, feat // lanes):
                part = part + squares[:, m * lanes : (m + 1) * lanes]
            sq_ref[...] = part if n == 0 and c == 0 else sq_ref[...] + part
        if ready is not None:
            ready(n)
        for i in range(w_ref.shape[0]):
            terms = [
                lax.dot_general(
                    normed[c],
                    w_ref[i, :, columns[c]],
                    (((1,), (1,)), ((), ())),
                    preferred_element_type=jnp.float32,
                )
                for c in range(core)
            ]
            term = functools.reduce(jnp.add, terms)
            acc_ref[i] = term if n == 0 else acc_ref[i] + term


def early_kernel(cells, core, rank_ref, *refs):
    sides = refs[:core]
    w_ref, gain_ref, acc_ref, sq_ref = refs[core : core + 4]
    project_cells(cells, sides, rank_ref, w_ref, gain_ref, acc_ref, sq_ref)


def first_kernel(cells, later, core, rank_ref, *refs):
    sides = refs[:core]
    w_far, gain_far, taps_far, decay_far, acc_ref, sq_ref, w_ref, gain_ref, long_ref = refs[core : core + 9]
    taps_ref, decay_ref, sems, small_sems = refs[core + 9 :]
    wide = core * sides[0].shape[2]
    chip = lax.div(rank_ref[0], core)
    small = [(gain_far, gain_ref), (taps_far, taps_ref), (decay_far, decay_ref)]
    small = [pltpu.make_async_copy(src, dst, small_sems.at[n]) for n, (src, dst) in enumerate(small)]
    copies = []
    for n, cell in enumerate(cells + later):
        columns = pl.ds(pl.multiple_of((chip ^ cell) * wide, wide), wide)
        copies.append(
            [
                pltpu.make_async_copy(w_far.at[i, :, columns], w_ref.at[i, :, columns], sems.at[n, i])
                for i in range(w_far.shape[0])
            ]
        )
    for group in [small] + copies:
        for copy in group:
            copy.start()
    for copy in small:
        copy.wait()
    lags = lax.broadcasted_iota(jnp.int32, long_ref.shape, 0).astype(jnp.float32)
    long_ref[...] = taps_ref[...].T * jnp.exp(-decay_ref[...] * lags)

    def ready(n):
        for copy in copies[n]:
            copy.wait()

    project_cells(cells, sides, rank_ref, w_ref, gain_ref, acc_ref, sq_ref, ready)
    for n in range(len(cells), len(copies)):
        ready(n)


def mix_kernel(cells, core, rank_ref, *refs):
    sides = refs[:core]
    w_ref, gain_ref, acc_in, sq_in, short_ref, long_ref, y_ref = refs[core : core + 7]
    acc_ref, sq_ref, pad_ref, query_ref = refs[core + 7 :]
    branches, chan, model_width = w_ref.shape
    tok_len = y_ref.shape[0]
    project_cells(cells, sides, rank_ref, w_ref, gain_ref, acc_ref, sq_ref)

    total = jnp.sum(sq_in[...] + sq_ref[...], axis=1, keepdims=True)
    factor = lax.rsqrt(total / model_width + EPS)
    taps = short_ref.shape[0] // branches
    pad_ref[0:PAD, :] = jnp.zeros((PAD, chan), jnp.float32)

    def branch(i):
        u = (acc_in[i] + acc_ref[i]) * factor
        pad_ref[PAD : PAD + tok_len, :] = u
        z = short_ref[i * taps : i * taps + 1, :] * u
        for j in range(1, taps):
            z = z + short_ref[i * taps + j : i * taps + j + 1, :] * pad_ref[PAD - j : PAD - j + tok_len, :]
        return z

    query_ref[...] = branch(1)
    product = query_ref[...] * branch(2)
    query_ref[...] = branch(0)
    pad_ref[PAD : PAD + tok_len, :] = product
    width = min(chan, 128)
    tiles = tok_len // 8
    for c in range(0, chan, width):
        cols = slice(c, c + width)
        conv = [None] * tiles
        for b in range(8):
            moved = [pad_ref[PAD - b + 8 * i : PAD - b + 8 * i + 8, cols] for i in range(tiles)]
            for a in range(long_ref.shape[0] // 8):
                tap = long_ref[8 * a + b : 8 * a + b + 1, cols]
                for i in range(a, tiles):
                    term = tap * moved[i - a]
                    conv[i] = term if conv[i] is None else conv[i] + term
        for i in range(0, tiles, 2):
            at = slice(8 * i, 8 * i + 16)
            both = jnp.concatenate(conv[i : i + 2], axis=0)
            y_ref[at, cols] = (query_ref[at, cols] * both).astype(jnp.bfloat16)


def out_kernel(parts, core, rank_ref, *refs):
    w_ref, own_ref, result_ref, acc_ref = refs[-4:]
    chan = refs[0].shape[2]
    chip, side = lax.div(rank_ref[0], core), lax.rem(rank_ref[0], core)
    acc_ref[...] = own_ref[...].astype(jnp.float32)
    for p, cells in enumerate(parts):
        sides = refs[p * core : (p + 1) * core]
        for n, cell in enumerate(cells):
            terms = []
            for c in range(core):
                at = pl.multiple_of(((chip ^ cell) * core + (side ^ c)) * chan, chan)
                terms.append(
                    jnp.dot(sides[c][n], w_ref[pl.ds(at, chan), :], preferred_element_type=jnp.float32)
                )
            acc_ref[...] += functools.reduce(jnp.add, terms)
    result_ref[...] = acc_ref[...].astype(jnp.bfloat16)


def in_vmem(count):
    return [pl.BlockSpec(memory_space=pltpu.VMEM)] * count


def call(kernel, operands, outs, scratch, flops, name, far_operands=(), moved=0):
    specs = [pl.BlockSpec(memory_space=pltpu.SMEM)] + in_vmem(len(operands) - 1)
    for n in far_operands:
        specs[n] = pl.BlockSpec(memory_space=pltpu.HBM)
    return pl.pallas_call(
        kernel,
        in_specs=specs,
        out_specs=in_vmem(len(outs)),
        out_shape=outs,
        scratch_shapes=scratch,
        compiler_params=pltpu.CompilerParams(vmem_limit_bytes=VMEM_LIMIT),
        cost_estimate=pl.CostEstimate(flops=flops, bytes_accessed=flops // 1024 + moved, transcendentals=0),
        name=name,
    )(*operands)


def project_early(part, later, w_in, gain, rank, taps=None, decay=None):
    cells, sides = part
    core = len(sides)
    rows, feat = sides[0].shape[1:]
    branches, chan, model_width = w_in.shape
    outs = [
        jax.ShapeDtypeStruct((branches, rows, chan), jnp.float32),
        jax.ShapeDtypeStruct((rows, min(feat, 128)), jnp.float32),
    ]
    scratch = []
    flops = 2 * rows * branches * chan * feat * core * len(cells)
    operands = [rank, *sides, w_in, gain]
    if taps is not None:
        operands += [taps, decay]
        operands[1 + core :] = [pltpu.with_memory_space_constraint(x, pltpu.HBM) for x in operands[1 + core :]]
        scratch.append(pltpu.VMEM(taps.shape, taps.dtype))
        scratch.append(pltpu.VMEM(decay.shape, decay.dtype))
        outs.append(pltpu.VMEM(w_in.shape, w_in.dtype))
        outs.append(pltpu.VMEM(gain.shape, gain.dtype))
        outs.append(pltpu.VMEM(taps.shape[::-1], taps.dtype))
        scratch.append(pltpu.SemaphoreType.DMA((len(cells) + len(later), branches)))
        scratch.append(pltpu.SemaphoreType.DMA((3,)))
        kernel = functools.partial(first_kernel, cells, later, core)
        return call(kernel, operands, outs, scratch, flops, "load_project", range(1 + core, 5 + core), 4 * w_in.size)
    return call(functools.partial(early_kernel, cells, core), operands, outs, scratch, flops, "project_early")


def mix(part, w_in, gain, acc, sq, short_rows, long_rows, rank):
    cells, sides = part
    core = len(sides)
    rows, feat = sides[0].shape[1:]
    branches, chan, _ = w_in.shape
    scratch = [
        pltpu.VMEM(acc.shape, jnp.float32),
        pltpu.VMEM(sq.shape, jnp.float32),
        pltpu.VMEM((PAD + rows, chan), jnp.float32),
        pltpu.VMEM((rows, chan), jnp.float32),
    ]
    return call(
        functools.partial(mix_kernel, cells, core),
        [rank, *sides, w_in, gain, acc, sq, short_rows, long_rows],
        [jax.ShapeDtypeStruct((rows, chan), jnp.bfloat16)],
        scratch,
        2 * rows * branches * chan * feat * core * len(cells),
        "project_mix",
    )[0]


def project_out(parts, w_out, own, rank):
    core = len(parts[0][1])
    rows, feat = own.shape
    arrays = [side for _, sides in parts for side in sides]
    return call(
        functools.partial(out_kernel, [cells for cells, _ in parts], core),
        [rank, *arrays, w_out, own],
        [jax.ShapeDtypeStruct((rows, feat), jnp.bfloat16)],
        [pltpu.VMEM((rows, feat), jnp.float32)],
        2 * rows * w_out.shape[0] * feat,
        "project_out",
    )[0]


def body(section_count, dp_count, fresh_acts, carried, norm_gain, w_in, short_filter, filter_taps, decay_rate, w_out):
    tick_count, tok_len, _ = fresh_acts.shape
    far, near, core = split_dp(dp_count)
    group = near * core
    waves = plan(section_count, tick_count)
    section_idx = lax.axis_index("section")
    rank_idx = lax.axis_index("dp")
    rank = rank_idx.astype(jnp.int32).reshape(1)

    def swap(value, offset):
        return lax.ppermute(value, "dp", [(r, r ^ offset) for r in range(dp_count)])

    first_round, second_round = routes(far, near)

    def after(value, *earlier):
        return lax.optimization_barrier((value, [x for x in earlier if x is not None]))[0]

    def to_core(blocks):
        return [blocks] + [swap(blocks, c) for c in range(1, core)]

    def round_one(source):
        return {0: source} | {d: swap(source, d * core) for d in first_round}

    def round_two(blocks):
        cells, rest = [], []
        for d, sent in second_round:
            rest.append(swap(jnp.stack([blocks[b] for b in sent]), d * core))
            cells += [d ^ b for b in sent]
        return cells, rest

    short_rows = short_filter[0].transpose(0, 2, 1).reshape(-1, short_filter.shape[2])
    weights, loaded = {"in": w_in[0], "gain": norm_gain}, [filter_taps[0], decay_rate]
    waiting = carried[0]
    results = {}

    def start(slot, before, behind):
        source = after(slot["own"], before["line"]) if before else slot["own"]
        slot["blocks"] = after(round_one(source), before.get("acc"), before.get("rest"))
        slot["line"] = jnp.stack(list(slot["blocks"].values()))

    def spread(slot, before, behind):
        blocks = after(slot["blocks"], before.get("rest"))
        slot["cells"], slot["rest"] = round_two(blocks)
        early = list(blocks), after(to_core(slot["line"]), before.get("y"))
        slot["acc"], slot["sq"], *loads = project_early(early, slot["cells"], weights["in"], weights["gain"], rank, *loaded)
        if loads:
            weights["in"], weights["gain"], weights["long"] = loads
            loaded.clear()

    def work(slot, before, behind):
        rest = jnp.concatenate(after(slot["rest"], slot["acc"], before.get("y_blocks")))
        late = slot["cells"], to_core(rest)
        slot["y"] = mix(late, weights["in"], weights["gain"], slot["acc"], slot["sq"], short_rows, weights["long"], rank)
        slot["y_blocks"] = after(round_one(slot["y"]), before.get("y_rest"))
        slot["y_line"] = jnp.stack(list(slot["y_blocks"].values()))

    def spread_y(slot, before, behind):
        blocks = after(slot["y_blocks"], before.get("y_rest"), behind.get("rest"))
        slot["y_cells"], slot["y_rest"] = round_two(blocks)
        slot["y_early"] = list(blocks), to_core(slot["y_line"])

    def finish(slot, before, behind):
        late = slot["y_cells"], to_core(jnp.concatenate(after(slot["y_rest"], behind.get("y"))))
        slot["out"] = project_out([slot["y_early"], late], w_out[0], slot["own"], rank)

    phases = [start, spread, work, spread_y, finish]
    for w, ticks in enumerate(waves):
        slots = []
        for i in range(max(len(mine) for mine in ticks)):
            options = []
            for s in range(section_count):
                if i >= len(ticks[s]):
                    options.append(None)
                elif s == 0:
                    options.append(fresh_acts[ticks[s][i]])
                elif w == 0:
                    options.append(waiting)
                else:
                    options.append(SENT)
            if any(option is SENT for option in options):
                leaving = pick(
                    section_idx,
                    [
                        results[s, ticks[s + 1][i] - 1] if s + 1 < section_count and i < len(ticks[s + 1]) else None
                        for s in range(section_count)
                    ],
                )
                sent = lax.ppermute(leaving, "section", [(s, s + 1) for s in range(section_count - 1)])
                options = [sent if option is SENT else option for option in options]
            slots.append({"own": pick(section_idx, options)})
        for t in range(len(phases) + len(slots) - 1):
            for i, slot in enumerate(slots):
                if 0 <= t - i < len(phases):
                    before = slots[i - 1] if i > 0 else {}
                    behind = slots[i + 1] if i + 1 < len(slots) else {}
                    phases[t - i](slot, before, behind)
        for s in range(section_count):
            for i, k in enumerate(ticks[s]):
                results[s, k] = slots[i]["out"]
    outputs = []
    for k in range(tick_count):
        outputs.append(pick(section_idx, [results[s, k] for s in range(section_count)]))
    return jnp.stack(outputs)[None]


def solution(mesh):
    run = functools.partial(body, mesh.shape["section"], mesh.shape["dp"])
    return jax.shard_map(
        run,
        mesh=mesh,
        in_specs=(
            P(None, None, "dp"),
            P("section", None, "dp"),
            P("section", None),
            P("section", None, "dp", None),
            P("section", None, "dp", None),
            P("section", "dp", None),
            P("section", "dp"),
            P("section", None, "dp"),
        ),
        out_specs=P("section", None, None, "dp"),
        check_vma=False,
    )
```

```python
import functools

import jax
import jax.numpy as jnp
from jax import lax
from jax.experimental import pallas as pl
from jax.experimental.pallas import tpu as pltpu
from jax.sharding import PartitionSpec as P

EPS = 1e-06
VMEM_LIMIT = 12 * 1024 * 1024
PAD = 8


def split_dp(dp_count):
    core = 2 if dp_count % 2 == 0 else 1
    chips = dp_count // core
    near = 1
    while near * near * 4 <= chips:
        near *= 2
    return chips // near, near, core


def routes(far, near):
    if (far, near) == (4, 2):
        return [4, 2, 1], [(1, [4, 2]), (2, [4]), (3, [4])]
    line = [d * near for d in range(far)]
    return line[1:], [(d, line) for d in range(1, near)]


def fetch(cells, core, feat, rank_ref, w_far, w_ref, sems):
    wide = core * feat
    chip = lax.div(rank_ref[0], core)
    copies = []
    for n, cell in enumerate(cells):
        columns = pl.ds(pl.multiple_of((chip ^ cell) * wide, wide), wide)
        copies.append(
            [
                pltpu.make_async_copy(w_far.at[i, :, columns], w_ref.at[n, i], sems.at[n, i])
                for i in range(w_far.shape[0])
            ]
        )
    for group in copies:
        for copy in group:
            copy.start()

    def ready(n):
        for copy in copies[n]:
            copy.wait()

    return ready


def project_cells(cells, sides, rank_ref, w_ref, gain_ref, acc_ref, sq_ref, ready):
    feat = sides[0].shape[2]
    core = len(sides)
    lanes = sq_ref.shape[1]
    chip, side = lax.div(rank_ref[0], core), lax.rem(rank_ref[0], core)
    for n, cell in enumerate(cells):
        normed, columns = [], []
        for c in range(core):
            values = sides[c][n].astype(jnp.float32)
            columns.append(pl.ds(pl.multiple_of((side ^ c) * feat, feat), feat))
            gains = gain_ref[:, pl.ds(pl.multiple_of(((chip ^ cell) * core + (side ^ c)) * feat, feat), feat)]
            normed.append((values * gains).astype(jnp.bfloat16))
            squares = values * values
            part = squares[:, :lanes]
            for m in range(1, feat // lanes):
                part = part + squares[:, m * lanes : (m + 1) * lanes]
            sq_ref[...] = part if n == 0 and c == 0 else sq_ref[...] + part
        ready(n)
        for i in range(w_ref.shape[1]):
            terms = [
                lax.dot_general(
                    normed[c],
                    w_ref[n, i, :, columns[c]],
                    (((1,), (1,)), ((), ())),
                    preferred_element_type=jnp.float32,
                )
                for c in range(core)
            ]
            term = functools.reduce(jnp.add, terms)
            acc_ref[i] = term if n == 0 else acc_ref[i] + term


def early_kernel(cells, core, rank_ref, *refs):
    sides = refs[:core]
    w_far, gain_ref, acc_ref, sq_ref, w_ref, sems = refs[core:]
    ready = fetch(cells, core, sides[0].shape[2], rank_ref, w_far, w_ref, sems)
    project_cells(cells, sides, rank_ref, w_ref, gain_ref, acc_ref, sq_ref, ready)


def first_kernel(cells, core, rank_ref, *refs):
    sides = refs[:core]
    w_far, gain_far, taps_far, decay_far, acc_ref, sq_ref, gain_ref, long_ref = refs[core : core + 8]
    w_ref, sems, taps_ref, decay_ref, small_sems = refs[core + 8 :]
    ready = fetch(cells, core, sides[0].shape[2], rank_ref, w_far, w_ref, sems)
    small = [(gain_far, gain_ref), (taps_far, taps_ref), (decay_far, decay_ref)]
    small = [pltpu.make_async_copy(src, dst, small_sems.at[n]) for n, (src, dst) in enumerate(small)]
    for copy in small:
        copy.start()
    for copy in small:
        copy.wait()
    lags = lax.broadcasted_iota(jnp.int32, long_ref.shape, 0).astype(jnp.float32)
    long_ref[...] = taps_ref[...].T * jnp.exp(-decay_ref[...] * lags)
    project_cells(cells, sides, rank_ref, w_ref, gain_ref, acc_ref, sq_ref, ready)


def mix_kernel(cells, core, rank_ref, *refs):
    sides = refs[:core]
    w_far, gain_ref, acc_in, sq_in, short_ref, long_ref, y_ref = refs[core : core + 7]
    acc_ref, sq_ref, pad_ref, query_ref, w_ref, sems = refs[core + 7 :]
    branches, chan, model_width = w_far.shape
    tok_len = y_ref.shape[0]
    ready = fetch(cells, core, sides[0].shape[2], rank_ref, w_far, w_ref, sems)
    project_cells(cells, sides, rank_ref, w_ref, gain_ref, acc_ref, sq_ref, ready)

    total = jnp.sum(sq_in[...] + sq_ref[...], axis=1, keepdims=True)
    factor = lax.rsqrt(total / model_width + EPS)
    taps = short_ref.shape[0] // branches
    pad_ref[0:PAD, :] = jnp.zeros((PAD, chan), jnp.float32)

    def branch(i):
        u = (acc_in[i] + acc_ref[i]) * factor
        pad_ref[PAD : PAD + tok_len, :] = u
        z = short_ref[i * taps : i * taps + 1, :] * u
        for j in range(1, taps):
            z = z + short_ref[i * taps + j : i * taps + j + 1, :] * pad_ref[PAD - j : PAD - j + tok_len, :]
        return z

    query_ref[...] = branch(1)
    product = query_ref[...] * branch(2)
    query_ref[...] = branch(0)
    pad_ref[PAD : PAD + tok_len, :] = product
    width = min(chan, 128)
    tiles = tok_len // 8
    for c in range(0, chan, width):
        cols = slice(c, c + width)
        conv = [None] * tiles
        for b in range(8):
            moved = [pad_ref[PAD - b + 8 * i : PAD - b + 8 * i + 8, cols] for i in range(tiles)]
            for a in range(long_ref.shape[0] // 8):
                tap = long_ref[8 * a + b : 8 * a + b + 1, cols]
                for i in range(a, tiles):
                    term = tap * moved[i - a]
                    conv[i] = term if conv[i] is None else conv[i] + term
        for i in range(0, tiles, 2):
            at = slice(8 * i, 8 * i + 16)
            both = jnp.concatenate(conv[i : i + 2], axis=0)
            y_ref[at, cols] = (query_ref[at, cols] * both).astype(jnp.bfloat16)


def out_kernel(parts, core, rank_ref, *refs):
    w_ref, own_ref, result_ref, acc_ref = refs[-4:]
    chan = refs[0].shape[2]
    chip, side = lax.div(rank_ref[0], core), lax.rem(rank_ref[0], core)
    acc_ref[...] = own_ref[...].astype(jnp.float32)
    for p, cells in enumerate(parts):
        sides = refs[p * core : (p + 1) * core]
        for n, cell in enumerate(cells):
            terms = []
            for c in range(core):
                at = pl.multiple_of(((chip ^ cell) * core + (side ^ c)) * chan, chan)
                terms.append(
                    jnp.dot(sides[c][n], w_ref[pl.ds(at, chan), :], preferred_element_type=jnp.float32)
                )
            acc_ref[...] += functools.reduce(jnp.add, terms)
    result_ref[...] = acc_ref[...].astype(jnp.bfloat16)


def in_vmem(count):
    return [pl.BlockSpec(memory_space=pltpu.VMEM)] * count


def call(kernel, operands, outs, scratch, flops, name, far_operands=()):
    specs = [pl.BlockSpec(memory_space=pltpu.SMEM)] + in_vmem(len(operands) - 1)
    operands = list(operands)
    for n in far_operands:
        specs[n] = pl.BlockSpec(memory_space=pltpu.HBM)
        operands[n] = pltpu.with_memory_space_constraint(operands[n], pltpu.HBM)
    return pl.pallas_call(
        kernel,
        in_specs=specs,
        out_specs=in_vmem(len(outs)),
        out_shape=outs,
        scratch_shapes=scratch,
        compiler_params=pltpu.CompilerParams(vmem_limit_bytes=VMEM_LIMIT),
        cost_estimate=pl.CostEstimate(flops=flops, bytes_accessed=flops // 1024, transcendentals=0),
        name=name,
    )(*operands)


def streamed(cells, w_in, wide):
    branches, chan, _ = w_in.shape
    return [
        pltpu.VMEM((len(cells), branches, chan, wide), w_in.dtype),
        pltpu.SemaphoreType.DMA((len(cells), branches)),
    ]


def project_early(part, w_in, gain, rank, taps=None, decay=None):
    cells, sides = part
    core = len(sides)
    rows, feat = sides[0].shape[1:]
    branches, chan, model_width = w_in.shape
    outs = [
        jax.ShapeDtypeStruct((branches, rows, chan), jnp.float32),
        jax.ShapeDtypeStruct((rows, min(feat, 128)), jnp.float32),
    ]
    scratch = streamed(cells, w_in, core * feat)
    flops = 2 * rows * branches * chan * feat * core * len(cells)
    operands, far = [rank, *sides, w_in, gain], [1 + core]
    kernel = functools.partial(early_kernel, cells, core)
    if taps is not None:
        operands += [taps, decay]
        far = range(1 + core, 5 + core)
        outs.append(jax.ShapeDtypeStruct(gain.shape, gain.dtype))
        outs.append(jax.ShapeDtypeStruct(taps.shape[::-1], taps.dtype))
        scratch.append(pltpu.VMEM(taps.shape, taps.dtype))
        scratch.append(pltpu.VMEM(decay.shape, decay.dtype))
        scratch.append(pltpu.SemaphoreType.DMA((3,)))
        kernel = functools.partial(first_kernel, cells, core)
    return call(kernel, operands, outs, scratch, flops, "project_early", far)


def mix(part, w_in, gain, acc, sq, short_rows, long_rows, rank):
    cells, sides = part
    core = len(sides)
    rows, feat = sides[0].shape[1:]
    branches, chan, _ = w_in.shape
    scratch = [
        pltpu.VMEM(acc.shape, jnp.float32),
        pltpu.VMEM(sq.shape, jnp.float32),
        pltpu.VMEM((PAD + rows, chan), jnp.float32),
        pltpu.VMEM((rows, chan), jnp.float32),
    ]
    return call(
        functools.partial(mix_kernel, cells, core),
        [rank, *sides, w_in, gain, acc, sq, short_rows, long_rows],
        [jax.ShapeDtypeStruct((rows, chan), jnp.bfloat16)],
        scratch + streamed(cells, w_in, core * feat),
        2 * rows * branches * chan * feat * core * len(cells),
        "project_mix",
        [1 + core],
    )[0]


def project_out(parts, w_out, own, rank):
    core = len(parts[0][1])
    rows, feat = own.shape
    arrays = [side for _, sides in parts for side in sides]
    return call(
        functools.partial(out_kernel, [cells for cells, _ in parts], core),
        [rank, *arrays, w_out, own],
        [jax.ShapeDtypeStruct((rows, feat), jnp.bfloat16)],
        [pltpu.VMEM((rows, feat), jnp.float32)],
        2 * rows * w_out.shape[0] * feat,
        "project_out",
    )[0]


def body(section_count, dp_count, fresh_acts, carried, norm_gain, w_in, short_filter, filter_taps, decay_rate, w_out):
    tick_count, tok_len, _ = fresh_acts.shape
    far, near, core = split_dp(dp_count)
    group = near * core
    section_idx = lax.axis_index("section")
    rank = lax.axis_index("dp").astype(jnp.int32).reshape(1)

    def swap(value, offset):
        return lax.ppermute(value, "dp", [(r, r ^ offset) for r in range(dp_count)])

    first_round, second_round = routes(far, near)

    def after(value, *earlier):
        return lax.optimization_barrier((value, earlier))[0]

    def to_core(blocks):
        return [blocks] + [swap(blocks, c) for c in range(1, core)]

    def round_one(source):
        return lax.optimization_barrier({0: source} | {d: swap(source, d * core) for d in first_round})

    def round_two(blocks):
        cells, rest = [], []
        for d, sent in second_round:
            rest.append(swap(jnp.stack([blocks[b] for b in sent]), d * core))
            cells += [d ^ b for b in sent]
        return cells, rest

    def early_part(blocks):
        return list(blocks), to_core(jnp.stack(list(blocks.values())))

    short_rows = short_filter[0].transpose(0, 2, 1).reshape(-1, short_filter.shape[2])
    gain, small = norm_gain, (filter_taps[0], decay_rate)
    is_first = section_idx == 0
    onward = [(s, s + 1) for s in range(section_count - 1)]
    made = []
    for k in range(tick_count):
        before = carried[0] if k == 0 else lax.ppermute(made[-1], "section", onward)
        own = jnp.where(is_first, fresh_acts[k], before)
        blocks = round_one(own)
        cells, rest = round_two(blocks)
        acc, sq, *loads = project_early(early_part(blocks), w_in[0], gain, rank, *small)
        if loads:
            (gain, long_rows), small = loads, ()
        late = cells, to_core(jnp.concatenate(after(rest, acc)))
        y = mix(late, w_in[0], gain, acc, sq, short_rows, long_rows, rank)
        blocks = round_one(y)
        cells, rest = round_two(blocks)
        parts = [early_part(blocks), (cells, to_core(jnp.concatenate(rest)))]
        made.append(project_out(parts, w_out[0], own, rank))
    return jnp.stack(made)[None]


def solution(mesh):
    run = functools.partial(body, mesh.shape["section"], mesh.shape["dp"])
    return jax.shard_map(
        run,
        mesh=mesh,
        in_specs=(
            P(None, None, "dp"),
            P("section", None, "dp"),
            P("section", None),
            P("section", None, "dp", None),
            P("section", None, "dp", None),
            P("section", "dp", None),
            P("section", "dp"),
            P("section", None, "dp"),
        ),
        out_specs=P("section", None, None, "dp"),
        check_vma=False,
    )
```

```python
import functools

import jax
import jax.numpy as jnp
from jax import lax
from jax.experimental import pallas as pl
from jax.experimental.pallas import tpu as pltpu
from jax.sharding import PartitionSpec as P

EPS = 1e-06
VMEM_LIMIT = 12 * 1024 * 1024
PAD = 8
SPLIT = 2


def split_dp(dp_count):
    core = 2 if dp_count % 2 == 0 else 1
    chips = dp_count // core
    near = 1
    while near * near * 4 <= chips:
        near *= 2
    return chips // near, near, core


def routes(far, near):
    if (far, near) == (4, 2):
        return [4, 2, 1], [(1, [4, 2]), (2, [4]), (3, [4])]
    line = [d * near for d in range(far)]
    return line[1:], [(d, line) for d in range(1, near)]


def columns_of(rank_ref, core, cell, c, size):
    chip, side = lax.div(rank_ref[0], core), lax.rem(rank_ref[0], core)
    return pl.ds(pl.multiple_of(((chip ^ cell) * core + (side ^ c)) * size, size), size)


def fetch(blocks, core, feat, rank_ref, w_far, w_ref, sems):
    branches, chan, _ = w_far.shape
    part = chan // sems.shape[2]
    copies = []
    for n, (cell, c) in enumerate(blocks):
        columns = columns_of(rank_ref, core, cell, c, feat)
        copies.append(
            [
                pltpu.make_async_copy(
                    w_far.at[i, pl.ds(m * part, part), columns], w_ref.at[n, i, pl.ds(m * part, part)], sems.at[n, i, m]
                )
                for i in range(branches)
                for m in range(sems.shape[2])
            ]
        )
    for group in copies:
        for copy in group:
            copy.start()

    def ready(n):
        for copy in copies[n]:
            copy.wait()

    return ready


def project(blocks, core, values_of, rank_ref, w_ref, gain_ref, acc_ref, sq_ref, ready):
    lanes = sq_ref.shape[1]
    for n, (cell, c) in enumerate(blocks):
        values = values_of(n).astype(jnp.float32)
        feat = values.shape[1]
        gains = gain_ref[:, columns_of(rank_ref, core, cell, c, feat)]
        normed = (values * gains).astype(jnp.bfloat16)
        squares = values * values
        part = squares[:, :lanes]
        for m in range(1, feat // lanes):
            part = part + squares[:, m * lanes : (m + 1) * lanes]
        sq_ref[...] += part
        ready(n)
        for i in range(w_ref.shape[1]):
            acc_ref[i] += lax.dot_general(
                normed, w_ref[n, i], (((1,), (1,)), ((), ())), preferred_element_type=jnp.float32
            )


def first_kernel(blocks, core, prepare, rank_ref, x_ref, w_far, gain_far, *refs):
    if prepare:
        taps_far, decay_far, acc_ref, sq_ref, gain_ref, long_ref, w_ref, sems, taps_ref, decay_ref, small_sems = refs
    else:
        acc_ref, sq_ref, w_ref, sems = refs
        gain_ref = gain_far
    ready = fetch(blocks, core, x_ref.shape[2], rank_ref, w_far, w_ref, sems)
    if prepare:
        small = [(gain_far, gain_ref), (taps_far, taps_ref), (decay_far, decay_ref)]
        small = [pltpu.make_async_copy(src, dst, small_sems.at[n]) for n, (src, dst) in enumerate(small)]
        for copy in small:
            copy.start()
        for copy in small:
            copy.wait()
        lags = lax.broadcasted_iota(jnp.int32, long_ref.shape, 0).astype(jnp.float32)
        long_ref[...] = taps_ref[...].T * jnp.exp(-decay_ref[...] * lags)
    acc_ref[...] = jnp.zeros_like(acc_ref)
    sq_ref[...] = jnp.zeros_like(sq_ref)
    project(blocks, core, lambda n: x_ref[n], rank_ref, w_ref, gain_ref, acc_ref, sq_ref, ready)


def more_kernel(blocks, core, rank_ref, x_ref, w_far, gain_ref, acc_in, sq_in, acc_ref, sq_ref, w_ref, sems):
    ready = fetch(blocks, core, x_ref.shape[2], rank_ref, w_far, w_ref, sems)
    acc_ref[...] = acc_in[...]
    sq_ref[...] = sq_in[...]
    project(blocks, core, lambda n: x_ref[n], rank_ref, w_ref, gain_ref, acc_ref, sq_ref, ready)


def mix_kernel(blocks, core, rank_ref, *refs):
    sides = refs[: core - 1]
    w_far, gain_ref, acc_in, sq_in, short_ref, long_ref, y_ref = refs[core - 1 : core + 6]
    acc_ref, sq_ref, pad_ref, query_ref, w_ref, sems = refs[core + 6 :]
    branches, chan, model_width = w_far.shape
    tok_len = y_ref.shape[0]
    acc_ref[...] = acc_in[...]
    sq_ref[...] = sq_in[...]
    if core > 1:
        count, _, feat = sides[0].shape
        ready = fetch(blocks, core, feat, rank_ref, w_far, w_ref, sems)
        project(
            blocks,
            core,
            lambda n: sides[n // count][n % count],
            rank_ref,
            w_ref,
            gain_ref,
            acc_ref,
            sq_ref,
            ready,
        )

    total = jnp.sum(sq_ref[...], axis=1, keepdims=True)
    factor = lax.rsqrt(total / model_width + EPS)
    taps = short_ref.shape[0] // branches
    pad_ref[0:PAD, :] = jnp.zeros((PAD, chan), jnp.float32)

    def branch(i):
        u = acc_ref[i] * factor
        pad_ref[PAD : PAD + tok_len, :] = u
        z = short_ref[i * taps : i * taps + 1, :] * u
        for j in range(1, taps):
            z = z + short_ref[i * taps + j : i * taps + j + 1, :] * pad_ref[PAD - j : PAD - j + tok_len, :]
        return z

    query_ref[...] = branch(1)
    product = query_ref[...] * branch(2)
    query_ref[...] = branch(0)
    pad_ref[PAD : PAD + tok_len, :] = product
    width = min(chan, 128)
    tiles = tok_len // 8
    for c in range(0, chan, width):
        cols = slice(c, c + width)
        conv = [None] * tiles
        for b in range(8):
            moved = [pad_ref[PAD - b + 8 * i : PAD - b + 8 * i + 8, cols] for i in range(tiles)]
            for a in range(long_ref.shape[0] // 8):
                tap = long_ref[8 * a + b : 8 * a + b + 1, cols]
                for i in range(a, tiles):
                    term = tap * moved[i - a]
                    conv[i] = term if conv[i] is None else conv[i] + term
        for i in range(0, tiles, 2):
            at = slice(8 * i, 8 * i + 16)
            both = jnp.concatenate(conv[i : i + 2], axis=0)
            y_ref[at, cols] = (query_ref[at, cols] * both).astype(jnp.bfloat16)


def out_kernel(blocks, core, rank_ref, *refs):
    sides = refs[:core]
    w_ref, own_ref, result_ref, acc_ref = refs[core:]
    count, _, chan = sides[0].shape
    acc_ref[...] = own_ref[...].astype(jnp.float32)
    for n, (cell, c) in enumerate(blocks):
        rows = columns_of(rank_ref, core, cell, c, chan)
        acc_ref[...] += jnp.dot(sides[n // count][n % count], w_ref[rows, :], preferred_element_type=jnp.float32)
    result_ref[...] = acc_ref[...].astype(jnp.bfloat16)


def in_vmem(count):
    return [pl.BlockSpec(memory_space=pltpu.VMEM)] * count


def call(kernel, operands, outs, scratch, flops, name, far_operands=()):
    specs = [pl.BlockSpec(memory_space=pltpu.SMEM)] + in_vmem(len(operands) - 1)
    operands = list(operands)
    for n in far_operands:
        specs[n] = pl.BlockSpec(memory_space=pltpu.HBM)
        operands[n] = pltpu.with_memory_space_constraint(operands[n], pltpu.HBM)
    return pl.pallas_call(
        kernel,
        in_specs=specs,
        out_specs=in_vmem(len(outs)),
        out_shape=outs,
        scratch_shapes=scratch,
        compiler_params=pltpu.CompilerParams(vmem_limit_bytes=VMEM_LIMIT),
        cost_estimate=pl.CostEstimate(flops=flops, bytes_accessed=flops // 1024, transcendentals=0),
        name=name,
    )(*operands)


def streamed(count, w_in, feat):
    branches, chan, _ = w_in.shape
    return [
        pltpu.VMEM((count, branches, chan, feat), w_in.dtype),
        pltpu.SemaphoreType.DMA((count, branches, max(1, min(SPLIT, chan // 16)))),
    ]


def sums_of(rows, feat, w_in):
    return [
        jax.ShapeDtypeStruct((w_in.shape[0], rows, w_in.shape[1]), jnp.float32),
        jax.ShapeDtypeStruct((rows, min(feat, 128)), jnp.float32),
    ]


def work_of(x, w_in):
    return 2 * x.size * w_in.shape[0] * w_in.shape[1]


def project_first(blocks, core, x, w_in, gain, rank, taps=None, decay=None):
    count, rows, feat = x.shape
    operands, far, outs = [rank, x, w_in, gain], [2], sums_of(rows, feat, w_in)
    scratch = streamed(count, w_in, feat)
    if taps is not None:
        operands += [taps, decay]
        far = [2, 3, 4, 5]
        outs.append(jax.ShapeDtypeStruct(gain.shape, gain.dtype))
        outs.append(jax.ShapeDtypeStruct(taps.shape[::-1], taps.dtype))
        scratch += [pltpu.VMEM(taps.shape, taps.dtype), pltpu.VMEM(decay.shape, decay.dtype), pltpu.SemaphoreType.DMA((3,))]
    kernel = functools.partial(first_kernel, blocks, core, taps is not None)
    return call(kernel, operands, outs, scratch, work_of(x, w_in), "project_first", far)


def project_more(blocks, core, x, w_in, gain, sums, rank):
    count, rows, feat = x.shape
    kernel = functools.partial(more_kernel, blocks, core)
    operands, scratch = [rank, x, w_in, gain, *sums], streamed(count, w_in, feat)
    return call(kernel, operands, sums_of(rows, feat, w_in), scratch, work_of(x, w_in), "project_more", [2])


def mix(blocks, core, sides, w_in, gain, sums, short_rows, long_rows, rank):
    rows, chan = sums[0].shape[1:]
    feat = w_in.shape[2] // (len(blocks) // max(core - 1, 1) * core) if blocks else 128
    scratch = [pltpu.VMEM(total.shape, total.dtype) for total in sums]
    scratch += [pltpu.VMEM((PAD + rows, chan), jnp.float32), pltpu.VMEM((rows, chan), jnp.float32)]
    return call(
        functools.partial(mix_kernel, blocks, core),
        [rank, *sides, w_in, gain, *sums, short_rows, long_rows],
        [jax.ShapeDtypeStruct((rows, chan), jnp.bfloat16)],
        scratch + streamed(max(len(blocks), 1), w_in, feat),
        sum(work_of(x, w_in) for x in sides),
        "project_mix",
        [core],
    )[0]


def project_out(blocks, core, sides, w_out, own, rank):
    rows, feat = own.shape
    return call(
        functools.partial(out_kernel, blocks, core),
        [rank, *sides, w_out, own],
        [jax.ShapeDtypeStruct((rows, feat), jnp.bfloat16)],
        [pltpu.VMEM((rows, feat), jnp.float32)],
        2 * rows * w_out.shape[0] * feat,
        "project_out",
    )[0]


def body(section_count, dp_count, fresh_acts, carried, norm_gain, w_in, short_filter, filter_taps, decay_rate, w_out):
    tick_count, tok_len, _ = fresh_acts.shape
    far, near, core = split_dp(dp_count)
    group = near * core
    section_idx = lax.axis_index("section")
    rank = lax.axis_index("dp").astype(jnp.int32).reshape(1)

    def swap(value, offset):
        return lax.ppermute(value, "dp", [(r, r ^ offset) for r in range(dp_count)])

    first_round, second_round = routes(far, near)

    def after(value, *earlier):
        return lax.optimization_barrier((value, earlier))[0]

    def round_one(source):
        return lax.optimization_barrier({0: source} | {d: swap(source, d * core) for d in first_round})

    def round_two(blocks):
        leaving = lax.optimization_barrier([jnp.stack([blocks[b] for b in sent]) for _, sent in second_round])
        rest = [swap(payload, d * core) for payload, (d, _) in zip(leaving, second_round)]
        return [d ^ b for d, sent in second_round for b in sent], rest

    def of_core(cells, c):
        return [(cell, c) for cell in cells]

    short_rows = short_filter[0].transpose(0, 2, 1).reshape(-1, short_filter.shape[2])
    gain, small = norm_gain, (filter_taps[0], decay_rate)
    is_first = section_idx == 0
    onward = [(s, s + 1) for s in range(section_count - 1)]
    made = []
    for k in range(tick_count):
        before = carried[0] if k == 0 else lax.ppermute(made[-1], "section", onward)
        own = jnp.where(is_first, fresh_acts[k], before)
        blocks = round_one(own)
        cells, rest = round_two(blocks)
        direct = jnp.stack(list(blocks.values()))
        *sums, = project_first(of_core(blocks, 0), core, direct, w_in[0], gain, rank, *small)
        if small:
            *sums, gain, long_rows = sums
            small = ()
        relayed = jnp.concatenate(after(rest, sums))
        everything = jnp.concatenate([direct, relayed])
        sides = [swap(everything, c) for c in range(1, core)]
        sums = project_more(of_core(cells, 0), core, relayed, w_in[0], gain, sums, rank)
        sides = after(sides, sums)
        order = [*blocks, *cells]
        far_blocks = [block for c in range(1, core) for block in of_core(order, c)]
        y = mix(far_blocks, core, sides, w_in[0], gain, sums, short_rows, long_rows, rank)
        blocks = round_one(y)
        cells, rest = round_two(blocks)
        everything = jnp.concatenate([jnp.stack(list(blocks.values())), *rest])
        sides = [everything] + [swap(everything, c) for c in range(1, core)]
        order = [*blocks, *cells]
        all_blocks = [block for c in range(core) for block in of_core(order, c)]
        made.append(project_out(all_blocks, core, sides, w_out[0], own, rank))
    return jnp.stack(made)[None]


def solution(mesh):
    run = functools.partial(body, mesh.shape["section"], mesh.shape["dp"])
    return jax.shard_map(
        run,
        mesh=mesh,
        in_specs=(
            P(None, None, "dp"),
            P("section", None, "dp"),
            P("section", None),
            P("section", None, "dp", None),
            P("section", None, "dp", None),
            P("section", "dp", None),
            P("section", "dp"),
            P("section", None, "dp"),
        ),
        out_specs=P("section", None, None, "dp"),
        check_vma=False,
    )
```

```python
import functools

import jax
import jax.numpy as jnp
from jax import lax
from jax.experimental import pallas as pl
from jax.experimental.pallas import tpu as pltpu
from jax.sharding import PartitionSpec as P

EPS = 1e-06
VMEM_LIMIT = 20 * 1024 * 1024
PAD = 8


def plan(section_count, tick_count):
    wave_count = min(section_count, tick_count)
    waves = [[[] for _ in range(section_count)] for _ in range(wave_count)]
    where = {}
    for k in range(tick_count):
        for s in range(section_count):
            first = where[s - 1, k - 1][0] + 1 if s > 0 and k > 0 else 0
            last = wave_count - 1 - min(section_count - 1 - s, tick_count - 1 - k)
            best = min(range(first, last + 1), key=lambda w: (len(waves[w][s]), w))
            where[s, k] = (best, len(waves[best][s]))
            waves[best][s].append(k)
    return waves


def split_dp(dp_count):
    core = 2 if dp_count % 2 == 0 else 1
    chips = dp_count // core
    near = 1
    while near * near * 4 <= chips:
        near *= 2
    return chips // near, near, core


def pick(section_idx, options):
    distinct = []
    for s, value in enumerate(options):
        if value is None:
            continue
        for held, members in distinct:
            if held is value:
                members.append(s)
                break
        else:
            distinct.append((value, [s]))
    result = distinct[0][0]
    for value, members in distinct[1:]:
        mine = functools.reduce(jnp.logical_or, [section_idx == s for s in members])
        result = jnp.where(mine, value, result)
    return result


def routes(far, near, cross):
    if (far, near) == (4, 2):
        if cross:
            return [0, 4, 2], [(1, [4, 2, 0]), (2, [4]), (3, [4])]
        return [0, 4, 2, 1], [(1, [4, 2]), (2, [4]), (3, [4])]
    line = [d * near for d in range(far)]
    return line, [(d, line) for d in range(1, near)]


def columns_of(rank_ref, core, cell, c, size):
    chip, side = lax.div(rank_ref[0], core), lax.rem(rank_ref[0], core)
    return pl.ds(pl.multiple_of(((chip ^ cell) * core + (side ^ c)) * size, size), size)


def project(blocks, core, values_of, weights_of, rank_ref, gain_ref, acc_ref, sq_ref, ready=None):
    lanes = sq_ref.shape[1]
    side = lax.rem(rank_ref[0], core)
    for n, (cell, c) in enumerate(blocks):
        values = values_of(n).astype(jnp.float32)
        feat = values.shape[1]
        gains = gain_ref[:, columns_of(rank_ref, core, cell, c, feat)]
        normed = (values * gains).astype(jnp.bfloat16)
        squares = values * values
        part = squares[:, :lanes]
        for m in range(1, feat // lanes):
            part = part + squares[:, m * lanes : (m + 1) * lanes]
        sq_ref[...] += part
        if ready is not None:
            ready(n)
        inner = pl.ds(pl.multiple_of((side ^ c) * feat, feat), feat)
        for i in range(acc_ref.shape[0]):
            acc_ref[i] += lax.dot_general(
                normed, weights_of(n)[i, :, inner], (((1,), (1,)), ((), ())), preferred_element_type=jnp.float32
            )


def load_kernel(blocks, order, core, rank_ref, x_ref, w_far, gain_far, taps_far, decay_far, *refs):
    w_refs, (acc_ref, sq_ref, gain_ref, long_ref) = refs[: len(order)], refs[len(order) : len(order) + 4]
    sems, taps_ref, decay_ref, small_sems = refs[len(order) + 4 :]
    small = [(gain_far, gain_ref), (taps_far, taps_ref), (decay_far, decay_ref)]
    small = [pltpu.make_async_copy(src, dst, small_sems.at[n]) for n, (src, dst) in enumerate(small)]
    wide = w_refs[0].shape[2]
    chip = lax.div(rank_ref[0], core)
    copies = []
    for n, cell in enumerate(order):
        columns = pl.ds(pl.multiple_of((chip ^ cell) * wide, wide), wide)
        copies.append(
            [
                pltpu.make_async_copy(w_far.at[i, :, columns], w_refs[n].at[i], sems.at[n, i])
                for i in range(w_far.shape[0])
            ]
        )
    for group in [small] + copies:
        for copy in group:
            copy.start()
    for copy in small:
        copy.wait()
    lags = lax.broadcasted_iota(jnp.int32, long_ref.shape, 0).astype(jnp.float32)
    long_ref[...] = taps_ref[...].T * jnp.exp(-decay_ref[...] * lags)
    acc_ref[...] = jnp.zeros_like(acc_ref)
    sq_ref[...] = jnp.zeros_like(sq_ref)

    def ready(n):
        for copy in copies[n]:
            copy.wait()

    project(blocks, core, lambda n: x_ref[n], lambda n: w_refs[n], rank_ref, gain_ref, acc_ref, sq_ref, ready)
    for n in range(len(blocks), len(order)):
        ready(n)


def first_kernel(blocks, core, rank_ref, x_ref, gain_ref, *refs):
    w_refs, (acc_ref, sq_ref) = refs[:-2], refs[-2:]
    acc_ref[...] = jnp.zeros_like(acc_ref)
    sq_ref[...] = jnp.zeros_like(sq_ref)
    project(blocks, core, lambda n: x_ref[n], lambda n: w_refs[n], rank_ref, gain_ref, acc_ref, sq_ref)


def more_kernel(blocks, core, rank_ref, x_ref, gain_ref, acc_in, sq_in, *refs):
    w_refs, (acc_ref, sq_ref) = refs[:-2], refs[-2:]
    acc_ref[...] = acc_in[...]
    sq_ref[...] = sq_in[...]
    project(blocks, core, lambda n: x_ref[n], lambda n: w_refs[n], rank_ref, gain_ref, acc_ref, sq_ref)


def mix_kernel(blocks, core, model_width, rank_ref, *refs):
    sides, refs = refs[: core - 1], refs[core - 1 :]
    count = len(blocks) // max(core - 1, 1)
    gain_ref, acc_in, sq_in, short_ref, long_ref = refs[:5]
    w_refs = refs[5 : 5 + count]
    y_ref, acc_ref, sq_ref, pad_ref, query_ref = refs[5 + count :]
    branches, tok_len, chan = acc_in.shape
    acc_ref[...] = acc_in[...]
    sq_ref[...] = sq_in[...]
    project(
        blocks,
        core,
        lambda n: sides[n // count][n % count],
        lambda n: w_refs[n % count],
        rank_ref,
        gain_ref,
        acc_ref,
        sq_ref,
    )

    total = jnp.sum(sq_ref[...], axis=1, keepdims=True)
    factor = lax.rsqrt(total / model_width + EPS)
    taps = short_ref.shape[0] // branches
    pad_ref[0:PAD, :] = jnp.zeros((PAD, chan), jnp.float32)

    def branch(i):
        u = acc_ref[i] * factor
        pad_ref[PAD : PAD + tok_len, :] = u
        z = short_ref[i * taps : i * taps + 1, :] * u
        for j in range(1, taps):
            z = z + short_ref[i * taps + j : i * taps + j + 1, :] * pad_ref[PAD - j : PAD - j + tok_len, :]
        return z

    query_ref[...] = branch(1)
    product = query_ref[...] * branch(2)
    query_ref[...] = branch(0)
    pad_ref[PAD : PAD + tok_len, :] = product
    width = min(chan, 128)
    tiles = tok_len // 8
    for c in range(0, chan, width):
        cols = slice(c, c + width)
        conv = [None] * tiles
        for b in range(8):
            moved = [pad_ref[PAD - b + 8 * i : PAD - b + 8 * i + 8, cols] for i in range(tiles)]
            for a in range(long_ref.shape[0] // 8):
                tap = long_ref[8 * a + b : 8 * a + b + 1, cols]
                for i in range(a, tiles):
                    term = tap * moved[i - a]
                    conv[i] = term if conv[i] is None else conv[i] + term
        for i in range(0, tiles, 2):
            at = slice(8 * i, 8 * i + 16)
            both = jnp.concatenate(conv[i : i + 2], axis=0)
            y_ref[at, cols] = (query_ref[at, cols] * both).astype(jnp.bfloat16)


def out_kernel(blocks, core, rank_ref, *refs):
    sides = refs[:core]
    w_ref, own_ref, result_ref, acc_ref = refs[core:]
    count, _, chan = sides[0].shape
    acc_ref[...] = own_ref[...].astype(jnp.float32)
    for n, (cell, c) in enumerate(blocks):
        rows = columns_of(rank_ref, core, cell, c, chan)
        acc_ref[...] += jnp.dot(sides[n // count][n % count], w_ref[rows, :], preferred_element_type=jnp.float32)
    result_ref[...] = acc_ref[...].astype(jnp.bfloat16)


def in_vmem(count):
    return [pl.BlockSpec(memory_space=pltpu.VMEM)] * count


def call(kernel, operands, outs, scratch, flops, name, far_operands=()):
    specs = [pl.BlockSpec(memory_space=pltpu.SMEM)] + in_vmem(len(operands) - 1)
    operands = list(operands)
    for n in far_operands:
        specs[n] = pl.BlockSpec(memory_space=pltpu.HBM)
        operands[n] = pltpu.with_memory_space_constraint(operands[n], pltpu.HBM)
    return pl.pallas_call(
        kernel,
        in_specs=specs,
        out_specs=in_vmem(len(outs)),
        out_shape=outs,
        scratch_shapes=scratch,
        compiler_params=pltpu.CompilerParams(vmem_limit_bytes=VMEM_LIMIT),
        cost_estimate=pl.CostEstimate(flops=flops, bytes_accessed=flops // 1024, transcendentals=0),
        name=name,
    )(*operands)


def sums_of(x, branches, chan):
    _, rows, feat = x.shape
    return [
        jax.ShapeDtypeStruct((branches, rows, chan), jnp.float32),
        jax.ShapeDtypeStruct((rows, min(feat, 128)), jnp.float32),
    ]


def project_load(blocks, order, core, x, w_in, gain, taps, decay, rank):
    branches, chan, model_width = w_in.shape
    piece = jax.ShapeDtypeStruct((branches, chan, model_width // len(order)), w_in.dtype)
    outs = [piece] * len(order) + sums_of(x, branches, chan)
    outs += [jax.ShapeDtypeStruct(gain.shape, gain.dtype), jax.ShapeDtypeStruct(taps.shape[::-1], taps.dtype)]
    scratch = [
        pltpu.SemaphoreType.DMA((len(order), branches)),
        pltpu.VMEM(taps.shape, taps.dtype),
        pltpu.VMEM(decay.shape, decay.dtype),
        pltpu.SemaphoreType.DMA((3,)),
    ]
    kernel = functools.partial(load_kernel, blocks, order, core)
    flops = 2 * x.size * branches * chan
    *pieces, acc, sq, gain, long_rows = call(
        kernel, [rank, x, w_in, gain, taps, decay], outs, scratch, flops, "project_load", [2, 3, 4, 5]
    )
    return [acc, sq], {"in": dict(zip(order, pieces)), "gain": gain, "long": long_rows}


def project_part(blocks, core, x, params, sums, rank):
    w_refs = [params["in"][cell] for cell, _ in blocks]
    branches, chan, _ = w_refs[0].shape
    kernel, name = (more_kernel, "project_more") if sums else (first_kernel, "project_first")
    operands = [rank, x, params["gain"], *sums, *w_refs]
    flops = 2 * x.size * branches * chan
    return call(functools.partial(kernel, blocks, core), operands, sums_of(x, branches, chan), [], flops, name)


def mix(blocks, core, model_width, sides, params, sums, short_rows, rank):
    rows, chan = sums[0].shape[1:]
    scratch = [pltpu.VMEM(total.shape, total.dtype) for total in sums]
    scratch += [pltpu.VMEM((PAD + rows, chan), jnp.float32), pltpu.VMEM((rows, chan), jnp.float32)]
    w_refs = [params["in"][cell] for cell, _ in blocks[: len(blocks) // max(core - 1, 1)]]
    return call(
        functools.partial(mix_kernel, blocks, core, model_width),
        [rank, *sides, params["gain"], *sums, short_rows, params["long"], *w_refs],
        [jax.ShapeDtypeStruct((rows, chan), jnp.bfloat16)],
        scratch,
        2 * rows * model_width * 3 * chan,
        "project_mix",
    )[0]


def project_out(blocks, core, sides, w_out, own, rank):
    rows, feat = own.shape
    return call(
        functools.partial(out_kernel, blocks, core),
        [rank, *sides, w_out, own],
        [jax.ShapeDtypeStruct((rows, feat), jnp.bfloat16)],
        [pltpu.VMEM((rows, feat), jnp.float32)],
        2 * rows * w_out.shape[0] * feat,
        "project_out",
    )[0]


def body(section_count, dp_count, fresh_acts, carried, norm_gain, w_in, short_filter, filter_taps, decay_rate, w_out):
    tick_count, tok_len, _ = fresh_acts.shape
    far, near, core = split_dp(dp_count)
    group = near * core
    section_idx = lax.axis_index("section")
    rank = lax.axis_index("dp").astype(jnp.int32).reshape(1)

    def swap(value, offset):
        return lax.ppermute(value, "dp", [(r, r ^ offset) for r in range(dp_count)])


    def onward(value, offset):
        pairs = [
            (s * dp_count + r, (s + 1) % section_count * dp_count + (r ^ offset))
            for s in range(section_count)
            for r in range(dp_count)
        ]
        return lax.ppermute(value, ("section", "dp"), pairs)

    def after(value, *earlier):
        return lax.optimization_barrier((value, [x for x in earlier if x is not None]))[0]

    def round_one(source, cross=False):
        first, _ = routes(far, near, cross)
        if cross:
            return {d: onward(source, d * core) for d in first}
        return {d: swap(source, d * core) if d else source for d in first}

    def round_two(blocks, cross=False):
        _, second = routes(far, near, cross)
        leaving = lax.optimization_barrier([jnp.stack([blocks[b] for b in sent]) for _, sent in second])
        rest = [swap(payload, d * core) for payload, (d, _) in zip(leaving, second)]
        return [d ^ b for d, sent in second for b in sent], rest

    def of_cores(cells, cores):
        return [(cell, c) for c in cores for cell in cells]

    short_rows = short_filter[0].transpose(0, 2, 1).reshape(-1, short_filter.shape[2])
    waiting = carried[0]
    params, results, last = {}, {}, None

    def start(slot, before, behind):
        source = after(slot["source"], before["blocks"]) if before else slot["source"]
        slot["blocks"] = after(round_one(source, slot["cross"]), before.get("sums"), slot["last"])

    def spread(slot, before, behind):
        slot["cells"], slot["rest"] = round_two(after(slot["blocks"], before.get("rest")), slot["cross"])
        blocks = of_cores(slot["blocks"], [0])
        direct = after(jnp.stack(list(slot["blocks"].values())), before.get("y"))
        slot["direct"] = direct
        if params:
            slot["sums"] = project_part(blocks, core, direct, params, [], rank)
        else:
            order = [*slot["blocks"], *slot["cells"]]
            slot["sums"], loaded = project_load(
                blocks, order, core, direct, w_in[0], norm_gain, filter_taps[0], decay_rate, rank
            )
            params.update(loaded)

    def work(slot, before, behind):
        relayed = jnp.concatenate(after(slot["rest"], slot["sums"], behind.get("blocks"), before.get("y_blocks")))
        everything = jnp.concatenate([slot["direct"], relayed])
        sides = [swap(everything, c) for c in range(1, core)]
        sums = project_part(of_cores(slot["cells"], [0]), core, relayed, params, slot["sums"], rank)
        order = [*slot["blocks"], *slot["cells"]]
        sides = after(sides, sums)
        blocks = of_cores(order, range(1, core))
        slot["y"] = mix(blocks, core, norm_gain.shape[1], sides, params, sums, short_rows, rank)
        slot["y_blocks"] = after(round_one(slot["y"]), before.get("y_rest"))

    def spread_y(slot, before, behind):
        blocks = after(slot["y_blocks"], before.get("y_rest"), before.get("out"), behind.get("rest"))
        slot["y_cells"], slot["y_rest"] = round_two(blocks)

    def finish(slot, before, behind):
        direct = jnp.stack(list(slot["y_blocks"].values()))
        everything = jnp.concatenate([direct, *after(slot["y_rest"], behind.get("y"))])
        sides = [everything] + [swap(everything, c) for c in range(1, core)]
        blocks = of_cores([*slot["y_blocks"], *slot["y_cells"]], range(core))
        slot["out"] = project_out(blocks, core, sides, w_out[0], slot["blocks"][0], rank)

    phases = [start, spread, work, spread_y, finish]
    for w, ticks in enumerate(plan(section_count, tick_count)):
        slots = []
        for i in range(max(len(mine) for mine in ticks)):
            options = []
            for s in range(section_count):
                if w == 0:
                    mine = ticks[s]
                    options.append(None if i >= len(mine) else waiting if s > 0 else fresh_acts[mine[i]])
                else:
                    mine = ticks[(s + 1) % section_count]
                    if i >= len(mine):
                        options.append(None)
                    elif s + 1 == section_count:
                        options.append(fresh_acts[mine[i]])
                    else:
                        options.append(results[s, mine[i] - 1])
            slots.append({"source": pick(section_idx, options), "cross": w > 0, "last": None if i > 0 else last})
        for t in range(len(phases) + len(slots) - 1):
            for i, slot in enumerate(slots):
                if 0 <= t - i < len(phases):
                    before = slots[i - 1] if i > 0 else {}
                    behind = slots[i + 1] if i + 1 < len(slots) else {}
                    phases[t - i](slot, before, behind)
        last = slots[-1]["out"]
        for s in range(section_count):
            for i, k in enumerate(ticks[s]):
                results[s, k] = slots[i]["out"]
    outputs = [pick(section_idx, [results[s, k] for s in range(section_count)]) for k in range(tick_count)]
    return jnp.stack(outputs)[None]


def solution(mesh):
    run = functools.partial(body, mesh.shape["section"], mesh.shape["dp"])
    return jax.shard_map(
        run,
        mesh=mesh,
        in_specs=(
            P(None, None, "dp"),
            P("section", None, "dp"),
            P("section", None),
            P("section", None, "dp", None),
            P("section", None, "dp", None),
            P("section", "dp", None),
            P("section", "dp"),
            P("section", None, "dp"),
        ),
        out_specs=P("section", None, None, "dp"),
        check_vma=False,
    )
```

```python
import functools

import jax
import jax.numpy as jnp
from jax import lax
from jax.experimental import pallas as pl
from jax.experimental.pallas import tpu as pltpu
from jax.sharding import PartitionSpec as P

EPS = 1e-06
VMEM_LIMIT = 20 * 1024 * 1024
PAD = 8


def plan(section_count, tick_count):
    wave_count = min(section_count, tick_count)
    waves = [[[] for _ in range(section_count)] for _ in range(wave_count)]
    where = {}
    for k in range(tick_count):
        for s in range(section_count):
            first = where[s - 1, k - 1][0] + 1 if s > 0 and k > 0 else 0
            last = wave_count - 1 - min(section_count - 1 - s, tick_count - 1 - k)
            best = min(range(first, last + 1), key=lambda w: (len(waves[w][s]), w))
            where[s, k] = (best, len(waves[best][s]))
            waves[best][s].append(k)
    return waves


def split_dp(dp_count):
    core = 2 if dp_count % 2 == 0 else 1
    chips = dp_count // core
    near = 1
    while near * near * 4 <= chips:
        near *= 2
    return chips // near, near, core


def pick(section_idx, options):
    distinct = []
    for s, value in enumerate(options):
        if value is None:
            continue
        for held, members in distinct:
            if held is value:
                members.append(s)
                break
        else:
            distinct.append((value, [s]))
    result = distinct[0][0]
    for value, members in distinct[1:]:
        mine = functools.reduce(jnp.logical_or, [section_idx == s for s in members])
        result = jnp.where(mine, value, result)
    return result


def routes(far, near, cross):
    if (far, near) == (4, 2):
        if cross:
            return [0, 4, 2], [(1, [4, 2, 0]), (2, [4]), (3, [4])]
        return [0, 4, 2, 1], [(1, [4, 2]), (2, [4]), (3, [4])]
    line = [d * near for d in range(far)]
    return line, [(d, line) for d in range(1, near)]


def columns_of(rank_ref, core, cell, c, size):
    chip, side = lax.div(rank_ref[0], core), lax.rem(rank_ref[0], core)
    return pl.ds(pl.multiple_of(((chip ^ cell) * core + (side ^ c)) * size, size), size)


def project(blocks, core, values_of, weights_of, rank_ref, gain_ref, acc_ref, sq_ref, ready=None):
    lanes = sq_ref.shape[1]
    side = lax.rem(rank_ref[0], core)
    for n, (cell, c) in enumerate(blocks):
        values = values_of(n).astype(jnp.float32)
        feat = values.shape[1]
        gains = gain_ref[:, columns_of(rank_ref, core, cell, c, feat)]
        normed = (values * gains).astype(jnp.bfloat16)
        squares = values * values
        part = squares[:, :lanes]
        for m in range(1, feat // lanes):
            part = part + squares[:, m * lanes : (m + 1) * lanes]
        sq_ref[...] += part
        if ready is not None:
            ready(n)
        inner = pl.ds(pl.multiple_of((side ^ c) * feat, feat), feat)
        for i in range(acc_ref.shape[0]):
            acc_ref[i] += lax.dot_general(
                normed, weights_of(n)[i, :, inner], (((1,), (1,)), ((), ())), preferred_element_type=jnp.float32
            )


def load_kernel(blocks, order, core, rank_ref, x_ref, w_far, gain_far, taps_far, decay_far, *refs):
    w_refs, (acc_ref, sq_ref, gain_ref, long_ref) = refs[: len(order)], refs[len(order) : len(order) + 4]
    sems, taps_ref, decay_ref, small_sems = refs[len(order) + 4 :]
    small = [(gain_far, gain_ref), (taps_far, taps_ref), (decay_far, decay_ref)]
    small = [pltpu.make_async_copy(src, dst, small_sems.at[n]) for n, (src, dst) in enumerate(small)]
    wide = w_refs[0].shape[2]
    chip = lax.div(rank_ref[0], core)
    copies = []
    for n, cell in enumerate(order):
        columns = pl.ds(pl.multiple_of((chip ^ cell) * wide, wide), wide)
        copies.append(
            [
                pltpu.make_async_copy(w_far.at[i, :, columns], w_refs[n].at[i], sems.at[n, i])
                for i in range(w_far.shape[0])
            ]
        )
    for group in [small] + copies:
        for copy in group:
            copy.start()
    for copy in small:
        copy.wait()
    lags = lax.broadcasted_iota(jnp.int32, long_ref.shape, 0).astype(jnp.float32)
    long_ref[...] = taps_ref[...].T * jnp.exp(-decay_ref[...] * lags)
    acc_ref[...] = jnp.zeros_like(acc_ref)
    sq_ref[...] = jnp.zeros_like(sq_ref)

    def ready(n):
        for copy in copies[n]:
            copy.wait()

    project(blocks, core, lambda n: x_ref[n], lambda n: w_refs[n], rank_ref, gain_ref, acc_ref, sq_ref, ready)
    for n in range(len(blocks), len(order)):
        ready(n)


def first_kernel(blocks, core, rank_ref, x_ref, gain_ref, *refs):
    w_refs, (acc_ref, sq_ref) = refs[:-2], refs[-2:]
    acc_ref[...] = jnp.zeros_like(acc_ref)
    sq_ref[...] = jnp.zeros_like(sq_ref)
    project(blocks, core, lambda n: x_ref[n], lambda n: w_refs[n], rank_ref, gain_ref, acc_ref, sq_ref)


def more_kernel(blocks, core, rank_ref, x_ref, gain_ref, acc_in, sq_in, *refs):
    w_refs, (acc_ref, sq_ref) = refs[:-2], refs[-2:]
    acc_ref[...] = acc_in[...]
    sq_ref[...] = sq_in[...]
    project(blocks, core, lambda n: x_ref[n], lambda n: w_refs[n], rank_ref, gain_ref, acc_ref, sq_ref)


def mix_kernel(blocks, core, model_width, rank_ref, *refs):
    sides, refs = refs[: core - 1], refs[core - 1 :]
    count = len(blocks) // max(core - 1, 1)
    gain_ref, acc_in, sq_in, short_ref, long_ref = refs[:5]
    w_refs = refs[5 : 5 + count]
    y_ref, acc_ref, sq_ref, pad_ref, query_ref = refs[5 + count :]
    branches, tok_len, chan = acc_in.shape
    acc_ref[...] = acc_in[...]
    sq_ref[...] = sq_in[...]
    project(
        blocks,
        core,
        lambda n: sides[n // count][n % count],
        lambda n: w_refs[n % count],
        rank_ref,
        gain_ref,
        acc_ref,
        sq_ref,
    )

    total = jnp.sum(sq_ref[...], axis=1, keepdims=True)
    factor = lax.rsqrt(total / model_width + EPS)
    taps = short_ref.shape[0] // branches
    pad_ref[0:PAD, :] = jnp.zeros((PAD, chan), jnp.float32)

    def branch(i):
        u = acc_ref[i] * factor
        pad_ref[PAD : PAD + tok_len, :] = u
        z = short_ref[i * taps] * u
        for j in range(1, taps):
            z = z + short_ref[i * taps + j] * pad_ref[PAD - j : PAD - j + tok_len, :]
        return z

    query_ref[...] = branch(1)
    product = query_ref[...] * branch(2)
    query_ref[...] = branch(0)
    pad_ref[PAD : PAD + tok_len, :] = product
    width = min(chan, 128)
    tiles = tok_len // 8
    for c in range(0, chan, width):
        cols = slice(c, c + width)
        conv = [None] * tiles
        for b in range(8):
            moved = [pad_ref[PAD - b + 8 * i : PAD - b + 8 * i + 8, cols] for i in range(tiles)]
            for a in range(long_ref.shape[0] // 8):
                tap = long_ref[8 * a + b : 8 * a + b + 1, cols]
                for i in range(a, tiles):
                    term = tap * moved[i - a]
                    conv[i] = term if conv[i] is None else conv[i] + term
        for i in range(0, tiles, 2):
            at = slice(8 * i, 8 * i + 16)
            both = jnp.concatenate(conv[i : i + 2], axis=0)
            y_ref[at, cols] = (query_ref[at, cols] * both).astype(jnp.bfloat16)


def out_kernel(blocks, core, rank_ref, *refs):
    sides = refs[:core]
    w_ref, own_ref, result_ref, acc_ref = refs[core:]
    count, _, chan = sides[0].shape
    acc_ref[...] = own_ref[...].astype(jnp.float32)
    for n, (cell, c) in enumerate(blocks):
        rows = columns_of(rank_ref, core, cell, c, chan)
        acc_ref[...] += jnp.dot(sides[n // count][n % count], w_ref[rows, :], preferred_element_type=jnp.float32)
    result_ref[...] = acc_ref[...].astype(jnp.bfloat16)


def in_vmem(count):
    return [pl.BlockSpec(memory_space=pltpu.VMEM)] * count


def call(kernel, operands, outs, scratch, flops, name, far_operands=()):
    specs = [pl.BlockSpec(memory_space=pltpu.SMEM)] + in_vmem(len(operands) - 1)
    operands = list(operands)
    for n in far_operands:
        specs[n] = pl.BlockSpec(memory_space=pltpu.HBM)
        operands[n] = pltpu.with_memory_space_constraint(operands[n], pltpu.HBM)
    return pl.pallas_call(
        kernel,
        in_specs=specs,
        out_specs=in_vmem(len(outs)),
        out_shape=outs,
        scratch_shapes=scratch,
        compiler_params=pltpu.CompilerParams(vmem_limit_bytes=VMEM_LIMIT),
        cost_estimate=pl.CostEstimate(flops=flops, bytes_accessed=flops // 1024, transcendentals=0),
        name=name,
    )(*operands)


def sums_of(x, branches, chan):
    _, rows, feat = x.shape
    return [
        jax.ShapeDtypeStruct((branches, rows, chan), jnp.float32),
        jax.ShapeDtypeStruct((rows, min(feat, 128)), jnp.float32),
    ]


def project_load(blocks, order, core, x, w_in, gain, taps, decay, rank):
    branches, chan, model_width = w_in.shape
    piece = jax.ShapeDtypeStruct((branches, chan, model_width // len(order)), w_in.dtype)
    outs = [piece] * len(order) + sums_of(x, branches, chan)
    outs += [jax.ShapeDtypeStruct(gain.shape, gain.dtype), jax.ShapeDtypeStruct(taps.shape[::-1], taps.dtype)]
    scratch = [
        pltpu.SemaphoreType.DMA((len(order), branches)),
        pltpu.VMEM(taps.shape, taps.dtype),
        pltpu.VMEM(decay.shape, decay.dtype),
        pltpu.SemaphoreType.DMA((3,)),
    ]
    kernel = functools.partial(load_kernel, blocks, order, core)
    flops = 2 * x.size * branches * chan
    *pieces, acc, sq, gain, long_rows = call(
        kernel, [rank, x, w_in, gain, taps, decay], outs, scratch, flops, "project_load", [2, 3, 4, 5]
    )
    return [acc, sq], {"in": dict(zip(order, pieces)), "gain": gain, "long": long_rows}


def project_part(blocks, core, x, params, sums, rank):
    w_refs = [params["in"][cell] for cell, _ in blocks]
    branches, chan, _ = w_refs[0].shape
    kernel, name = (more_kernel, "project_more") if sums else (first_kernel, "project_first")
    operands = [rank, x, params["gain"], *sums, *w_refs]
    flops = 2 * x.size * branches * chan
    return call(functools.partial(kernel, blocks, core), operands, sums_of(x, branches, chan), [], flops, name)


def mix(blocks, core, model_width, sides, params, sums, short_rows, rank):
    rows, chan = sums[0].shape[1:]
    scratch = [pltpu.VMEM(total.shape, total.dtype) for total in sums]
    scratch += [pltpu.VMEM((PAD + rows, chan), jnp.float32), pltpu.VMEM((rows, chan), jnp.float32)]
    w_refs = [params["in"][cell] for cell, _ in blocks[: len(blocks) // max(core - 1, 1)]]
    return call(
        functools.partial(mix_kernel, blocks, core, model_width),
        [rank, *sides, params["gain"], *sums, short_rows, params["long"], *w_refs],
        [jax.ShapeDtypeStruct((rows, chan), jnp.bfloat16)],
        scratch,
        2 * rows * model_width * 3 * chan,
        "project_mix",
    )[0]


def project_out(blocks, core, sides, w_out, own, rank):
    rows, feat = own.shape
    return call(
        functools.partial(out_kernel, blocks, core),
        [rank, *sides, w_out, own],
        [jax.ShapeDtypeStruct((rows, feat), jnp.bfloat16)],
        [pltpu.VMEM((rows, feat), jnp.float32)],
        2 * rows * w_out.shape[0] * feat,
        "project_out",
    )[0]


def body(section_count, dp_count, fresh_acts, carried, norm_gain, w_in, short_filter, filter_taps, decay_rate, w_out):
    tick_count, tok_len, _ = fresh_acts.shape
    far, near, core = split_dp(dp_count)
    group = near * core
    section_idx = lax.axis_index("section")
    rank = lax.axis_index("dp").astype(jnp.int32).reshape(1)

    def swap(value, offset):
        return lax.ppermute(value, "dp", [(r, r ^ offset) for r in range(dp_count)])


    def onward(value, offset):
        pairs = [
            (s * dp_count + r, (s + 1) % section_count * dp_count + (r ^ offset))
            for s in range(section_count)
            for r in range(dp_count)
        ]
        return lax.ppermute(value, ("section", "dp"), pairs)

    def after(value, *earlier):
        return lax.optimization_barrier((value, [x for x in earlier if x is not None]))[0]

    def round_one(source, cross=False):
        first, _ = routes(far, near, cross)
        if cross:
            return {d: onward(source, d * core) for d in first}
        return {d: swap(source, d * core) if d else source for d in first}

    def round_two(blocks, cross=False):
        _, second = routes(far, near, cross)
        leaving = lax.optimization_barrier([jnp.stack([blocks[b] for b in sent]) for _, sent in second])
        rest = [swap(payload, d * core) for payload, (d, _) in zip(leaving, second)]
        return [d ^ b for d, sent in second for b in sent], rest

    def of_cores(cells, cores):
        return [(cell, c) for c in cores for cell in cells]

    short_rows = short_filter[0].transpose(0, 2, 1).reshape(-1, 1, short_filter.shape[2])
    waiting = carried[0]
    params, results, last = {}, {}, None

    def start(slot, before, behind):
        source = after(slot["source"], before["blocks"]) if before else slot["source"]
        slot["blocks"] = after(round_one(source, slot["cross"]), before.get("sums"), slot["last"])

    def spread(slot, before, behind):
        slot["cells"], slot["rest"] = round_two(after(slot["blocks"], before.get("rest")), slot["cross"])
        blocks = of_cores(slot["blocks"], [0])
        direct = after(jnp.stack(list(slot["blocks"].values())), before.get("y"))
        slot["direct"] = direct
        if params:
            slot["sums"] = project_part(blocks, core, direct, params, [], rank)
        else:
            order = [*slot["blocks"], *slot["cells"]]
            slot["sums"], loaded = project_load(
                blocks, order, core, direct, w_in[0], norm_gain, filter_taps[0], decay_rate, rank
            )
            params.update(loaded)

    def work(slot, before, behind):
        relayed = jnp.concatenate(after(slot["rest"], slot["sums"], behind.get("blocks"), before.get("y_blocks")))
        everything = jnp.concatenate([slot["direct"], relayed])
        sides = [swap(everything, c) for c in range(1, core)]
        sums = project_part(of_cores(slot["cells"], [0]), core, relayed, params, slot["sums"], rank)
        order = [*slot["blocks"], *slot["cells"]]
        sides = after(sides, sums)
        blocks = of_cores(order, range(1, core))
        slot["y"] = mix(blocks, core, norm_gain.shape[1], sides, params, sums, short_rows, rank)
        slot["y_blocks"] = after(round_one(slot["y"]), before.get("y_rest"))

    def spread_y(slot, before, behind):
        blocks = after(slot["y_blocks"], before.get("y_rest"), before.get("out"), behind.get("rest"))
        slot["y_cells"], slot["y_rest"] = round_two(blocks)

    def finish(slot, before, behind):
        direct = jnp.stack(list(slot["y_blocks"].values()))
        everything = jnp.concatenate([direct, *after(slot["y_rest"], behind.get("y"))])
        sides = [everything] + [swap(everything, c) for c in range(1, core)]
        blocks = of_cores([*slot["y_blocks"], *slot["y_cells"]], range(core))
        slot["out"] = project_out(blocks, core, sides, w_out[0], slot["blocks"][0], rank)

    phases = [start, spread, work, spread_y, finish]
    for w, ticks in enumerate(plan(section_count, tick_count)):
        slots = []
        for i in range(max(len(mine) for mine in ticks)):
            options = []
            for s in range(section_count):
                if w == 0:
                    mine = ticks[s]
                    options.append(None if i >= len(mine) else waiting if s > 0 else fresh_acts[mine[i]])
                else:
                    mine = ticks[(s + 1) % section_count]
                    if i >= len(mine):
                        options.append(None)
                    elif s + 1 == section_count:
                        options.append(fresh_acts[mine[i]])
                    else:
                        options.append(results[s, mine[i] - 1])
            slots.append({"source": pick(section_idx, options), "cross": w > 0, "last": None if i > 0 else last})
        for t in range(len(phases) + len(slots) - 1):
            for i, slot in enumerate(slots):
                if 0 <= t - i < len(phases):
                    before = slots[i - 1] if i > 0 else {}
                    behind = slots[i + 1] if i + 1 < len(slots) else {}
                    phases[t - i](slot, before, behind)
        last = slots[-1]["out"]
        for s in range(section_count):
            for i, k in enumerate(ticks[s]):
                results[s, k] = slots[i]["out"]
    outputs = [pick(section_idx, [results[s, k] for s in range(section_count)]) for k in range(tick_count)]
    return jnp.stack(outputs)[None]


def solution(mesh):
    run = functools.partial(body, mesh.shape["section"], mesh.shape["dp"])
    return jax.shard_map(
        run,
        mesh=mesh,
        in_specs=(
            P(None, None, "dp"),
            P("section", None, "dp"),
            P("section", None),
            P("section", None, "dp", None),
            P("section", None, "dp", None),
            P("section", "dp", None),
            P("section", "dp"),
            P("section", None, "dp"),
        ),
        out_specs=P("section", None, None, "dp"),
        check_vma=False,
    )
```

```python
import functools

import jax
import jax.numpy as jnp
from jax import lax
from jax.experimental import pallas as pl
from jax.experimental.pallas import tpu as pltpu
from jax.sharding import PartitionSpec as P

EPS = 1e-06
VMEM_LIMIT = 20 * 1024 * 1024
PAD = 8


def split_dp(dp_count):
    core = 2 if dp_count % 2 == 0 else 1
    chips = dp_count // core
    near = 1
    while near * near * 4 <= chips:
        near *= 2
    return chips // near, near, core


def routes(far, near, cross):
    if (far, near) == (4, 2):
        if cross:
            return [0, 4, 2], [(1, [4, 2, 0]), (2, [4]), (3, [4])]
        return [0, 4, 2, 1], [(1, [4, 2]), (2, [4]), (3, [4])]
    line = [d * near for d in range(far)]
    return line, [(d, line) for d in range(1, near)]


def columns_of(rank_ref, core, cell, c, size):
    chip, side = lax.div(rank_ref[0], core), lax.rem(rank_ref[0], core)
    return pl.ds(pl.multiple_of(((chip ^ cell) * core + (side ^ c)) * size, size), size)


def project(blocks, core, values_of, weights_of, rank_ref, gain_ref, acc_ref, sq_ref, ready=None):
    lanes = sq_ref.shape[1]
    side = lax.rem(rank_ref[0], core)
    for n, (cell, c) in enumerate(blocks):
        values = values_of(n).astype(jnp.float32)
        feat = values.shape[1]
        gains = gain_ref[:, columns_of(rank_ref, core, cell, c, feat)]
        normed = (values * gains).astype(jnp.bfloat16)
        squares = values * values
        part = squares[:, :lanes]
        for m in range(1, feat // lanes):
            part = part + squares[:, m * lanes : (m + 1) * lanes]
        sq_ref[...] += part
        if ready is not None:
            ready(n)
        inner = pl.ds(pl.multiple_of((side ^ c) * feat, feat), feat)
        for i in range(acc_ref.shape[0]):
            acc_ref[i] += lax.dot_general(
                normed, weights_of(n)[i, :, inner], (((1,), (1,)), ((), ())), preferred_element_type=jnp.float32
            )


def load_kernel(blocks, order, core, rank_ref, x_ref, w_far, gain_far, taps_far, decay_far, *refs):
    w_refs, (acc_ref, sq_ref, gain_ref, long_ref) = refs[: len(order)], refs[len(order) : len(order) + 4]
    sems, taps_ref, decay_ref, small_sems = refs[len(order) + 4 :]
    small = [(gain_far, gain_ref), (taps_far, taps_ref), (decay_far, decay_ref)]
    small = [pltpu.make_async_copy(src, dst, small_sems.at[n]) for n, (src, dst) in enumerate(small)]
    wide = w_refs[0].shape[2]
    chip = lax.div(rank_ref[0], core)
    copies = []
    for n, cell in enumerate(order):
        columns = pl.ds(pl.multiple_of((chip ^ cell) * wide, wide), wide)
        copies.append(
            [
                pltpu.make_async_copy(w_far.at[i, :, columns], w_refs[n].at[i], sems.at[n, i])
                for i in range(w_far.shape[0])
            ]
        )
    for group in [small] + copies:
        for copy in group:
            copy.start()
    for copy in small:
        copy.wait()
    lags = lax.broadcasted_iota(jnp.int32, long_ref.shape, 0).astype(jnp.float32)
    long_ref[...] = taps_ref[...].T * jnp.exp(-decay_ref[...] * lags)
    acc_ref[...] = jnp.zeros_like(acc_ref)
    sq_ref[...] = jnp.zeros_like(sq_ref)

    def ready(n):
        for copy in copies[n]:
            copy.wait()

    project(blocks, core, lambda n: x_ref[n], lambda n: w_refs[n], rank_ref, gain_ref, acc_ref, sq_ref, ready)
    for n in range(len(blocks), len(order)):
        ready(n)


def first_kernel(blocks, core, rank_ref, x_ref, gain_ref, *refs):
    w_refs, (acc_ref, sq_ref) = refs[:-2], refs[-2:]
    acc_ref[...] = jnp.zeros_like(acc_ref)
    sq_ref[...] = jnp.zeros_like(sq_ref)
    project(blocks, core, lambda n: x_ref[n], lambda n: w_refs[n], rank_ref, gain_ref, acc_ref, sq_ref)


def more_kernel(blocks, core, rank_ref, x_ref, gain_ref, acc_in, sq_in, *refs):
    w_refs, (acc_ref, sq_ref) = refs[:-2], refs[-2:]
    acc_ref[...] = acc_in[...]
    sq_ref[...] = sq_in[...]
    project(blocks, core, lambda n: x_ref[n], lambda n: w_refs[n], rank_ref, gain_ref, acc_ref, sq_ref)


def mix_kernel(blocks, core, model_width, rank_ref, *refs):
    sides, refs = refs[: core - 1], refs[core - 1 :]
    count = len(blocks) // max(core - 1, 1)
    gain_ref, acc_in, sq_in, short_ref, long_ref = refs[:5]
    w_refs = refs[5 : 5 + count]
    y_ref, acc_ref, sq_ref, pad_ref, query_ref = refs[5 + count :]
    branches, tok_len, chan = acc_in.shape
    acc_ref[...] = acc_in[...]
    sq_ref[...] = sq_in[...]
    project(
        blocks,
        core,
        lambda n: sides[n // count][n % count],
        lambda n: w_refs[n % count],
        rank_ref,
        gain_ref,
        acc_ref,
        sq_ref,
    )

    total = jnp.sum(sq_ref[...], axis=1, keepdims=True)
    factor = lax.rsqrt(total / model_width + EPS)
    taps = short_ref.shape[1]
    pad_ref[0:PAD, :] = jnp.zeros((PAD, chan), jnp.float32)

    def branch(i):
        u = acc_ref[i] * factor
        pad_ref[PAD : PAD + tok_len, :] = u
        z = short_ref[i, 0] * u
        for j in range(1, taps):
            z = z + short_ref[i, j] * pad_ref[PAD - j : PAD - j + tok_len, :]
        return z

    query_ref[...] = branch(1)
    product = query_ref[...] * branch(2)
    query_ref[...] = branch(0)
    pad_ref[PAD : PAD + tok_len, :] = product
    width = min(chan, 128)
    tiles = tok_len // 8
    for c in range(0, chan, width):
        cols = slice(c, c + width)
        conv = [None] * tiles
        for b in range(8):
            moved = [pad_ref[PAD - b + 8 * i : PAD - b + 8 * i + 8, cols] for i in range(tiles)]
            for a in range(long_ref.shape[0] // 8):
                tap = long_ref[8 * a + b : 8 * a + b + 1, cols]
                for i in range(a, tiles):
                    term = tap * moved[i - a]
                    conv[i] = term if conv[i] is None else conv[i] + term
        for i in range(0, tiles, 2):
            at = slice(8 * i, 8 * i + 16)
            both = jnp.concatenate(conv[i : i + 2], axis=0)
            y_ref[at, cols] = (query_ref[at, cols] * both).astype(jnp.bfloat16)


def out_kernel(blocks, core, rank_ref, *refs):
    sides, refs = refs[:core], refs[core:]
    w_ref, own_ref = refs[:2]
    count, _, chan = sides[0].shape
    acc_ref = refs[-1]
    acc_ref[...] = own_ref[...].astype(jnp.float32)
    for n, (cell, c) in enumerate(blocks):
        rows = columns_of(rank_ref, core, cell, c, chan)
        acc_ref[...] += jnp.dot(sides[n // count][n % count], w_ref[rows, :], preferred_element_type=jnp.float32)
    result = acc_ref[...].astype(jnp.bfloat16)
    if len(refs) == 4:
        refs[2][...] = result
    else:
        following_ref, result_ref, leaving_ref = refs[2:5]
        result_ref[...] = result
        leaving_ref[...] = jnp.where(rank_ref[1] == 1, following_ref[...], result)


def in_vmem(count):
    return [pl.BlockSpec(memory_space=pltpu.VMEM)] * count


def call(kernel, operands, outs, scratch, flops, name, far_operands=()):
    specs = [pl.BlockSpec(memory_space=pltpu.SMEM)] + in_vmem(len(operands) - 1)
    operands = list(operands)
    for n in far_operands:
        specs[n] = pl.BlockSpec(memory_space=pltpu.HBM)
        operands[n] = pltpu.with_memory_space_constraint(operands[n], pltpu.HBM)
    return pl.pallas_call(
        kernel,
        in_specs=specs,
        out_specs=in_vmem(len(outs)),
        out_shape=outs,
        scratch_shapes=scratch,
        compiler_params=pltpu.CompilerParams(vmem_limit_bytes=VMEM_LIMIT),
        cost_estimate=pl.CostEstimate(flops=flops, bytes_accessed=flops // 1024, transcendentals=0),
        name=name,
    )(*operands)


def sums_of(x, branches, chan):
    _, rows, feat = x.shape
    return [
        jax.ShapeDtypeStruct((branches, rows, chan), jnp.float32),
        jax.ShapeDtypeStruct((rows, min(feat, 128)), jnp.float32),
    ]


def project_load(blocks, order, core, x, w_in, gain, taps, decay, rank):
    branches, chan, model_width = w_in.shape
    piece = jax.ShapeDtypeStruct((branches, chan, model_width // len(order)), w_in.dtype)
    outs = [piece] * len(order) + sums_of(x, branches, chan)
    outs += [jax.ShapeDtypeStruct(gain.shape, gain.dtype), jax.ShapeDtypeStruct(taps.shape[::-1], taps.dtype)]
    scratch = [
        pltpu.SemaphoreType.DMA((len(order), branches)),
        pltpu.VMEM(taps.shape, taps.dtype),
        pltpu.VMEM(decay.shape, decay.dtype),
        pltpu.SemaphoreType.DMA((3,)),
    ]
    kernel = functools.partial(load_kernel, blocks, order, core)
    flops = 2 * x.size * branches * chan
    *pieces, acc, sq, gain, long_rows = call(
        kernel, [rank, x, w_in, gain, taps, decay], outs, scratch, flops, "project_load", [2, 3, 4, 5]
    )
    return [acc, sq], {"in": dict(zip(order, pieces)), "gain": gain, "long": long_rows}


def project_part(blocks, core, x, params, sums, rank):
    w_refs = [params["in"][cell] for cell, _ in blocks]
    branches, chan, _ = w_refs[0].shape
    kernel, name = (more_kernel, "project_more") if sums else (first_kernel, "project_first")
    operands = [rank, x, params["gain"], *sums, *w_refs]
    flops = 2 * x.size * branches * chan
    return call(functools.partial(kernel, blocks, core), operands, sums_of(x, branches, chan), [], flops, name)


def mix(blocks, core, model_width, sides, params, sums, short_rows, rank):
    rows, chan = sums[0].shape[1:]
    scratch = [pltpu.VMEM(total.shape, total.dtype) for total in sums]
    scratch += [pltpu.VMEM((PAD + rows, chan), jnp.float32), pltpu.VMEM((rows, chan), jnp.float32)]
    w_refs = [params["in"][cell] for cell, _ in blocks[: len(blocks) // max(core - 1, 1)]]
    return call(
        functools.partial(mix_kernel, blocks, core, model_width),
        [rank, *sides, params["gain"], *sums, short_rows, params["long"], *w_refs],
        [jax.ShapeDtypeStruct((rows, chan), jnp.bfloat16)],
        scratch,
        2 * rows * model_width * 3 * chan,
        "project_mix",
    )[0]


def project_out(blocks, core, sides, w_out, own, following, rank):
    rows, feat = own.shape
    result = jax.ShapeDtypeStruct((rows, feat), jnp.bfloat16)
    return call(
        functools.partial(out_kernel, blocks, core),
        [rank, *sides, w_out, own] + ([] if following is None else [following]),
        [result] if following is None else [result, result],
        [pltpu.VMEM((rows, feat), jnp.float32)],
        2 * rows * w_out.shape[0] * feat,
        "project_out",
    )


def body(section_count, dp_count, fresh_acts, carried, norm_gain, w_in, short_filter, filter_taps, decay_rate, w_out):
    tick_count, tok_len, _ = fresh_acts.shape
    far, near, core = split_dp(dp_count)
    group = near * core
    section_idx = lax.axis_index("section")
    rank = jnp.stack([lax.axis_index("dp"), (section_idx == section_count - 1).astype(jnp.int32)])

    def swap(value, offset):
        return lax.ppermute(value, "dp", [(r, r ^ offset) for r in range(dp_count)])


    def onward(value, offset):
        pairs = [
            (s * dp_count + r, (s + 1) % section_count * dp_count + (r ^ offset))
            for s in range(section_count)
            for r in range(dp_count)
        ]
        return lax.ppermute(value, ("section", "dp"), pairs)

    def after(value, *earlier):
        return lax.optimization_barrier((value, [x for x in earlier if x is not None]))[0]

    def round_one(source, cross=False):
        first, _ = routes(far, near, cross)
        if cross:
            return {d: onward(source, d * core) for d in first}
        return {d: swap(source, d * core) if d else source for d in first}

    def round_two(blocks, cross=False):
        _, second = routes(far, near, cross)
        leaving = lax.optimization_barrier([jnp.stack([blocks[b] for b in sent]) for _, sent in second])
        rest = [swap(payload, d * core) for payload, (d, _) in zip(leaving, second)]
        return [d ^ b for d, sent in second for b in sent], rest

    def of_cores(cells, cores):
        return [(cell, c) for c in cores for cell in cells]

    short_rows = short_filter.transpose(1, 3, 0, 2)
    source = jnp.where(section_idx == 0, fresh_acts[0], carried[0])
    params, made = {}, []
    for k in range(tick_count):
        blocks = after(round_one(source, k > 0))
        cells, rest = round_two(blocks, k > 0)
        order = [*blocks, *cells]
        direct = jnp.stack(list(blocks.values()))
        here = of_cores(blocks, [0])
        if params:
            sums = project_part(here, core, direct, params, [], rank)
        else:
            sums, params = project_load(
                here, order, core, direct, w_in[0], norm_gain, filter_taps[0], decay_rate, rank
            )
        relayed = jnp.concatenate(after(rest, sums))
        everything = jnp.concatenate([direct, relayed])
        sides = [swap(everything, c) for c in range(1, core)]
        sums = project_part(of_cores(cells, [0]), core, relayed, params, sums, rank)
        sides = after(sides, sums)
        y = mix(of_cores(order, range(1, core)), core, norm_gain.shape[1], sides, params, sums, short_rows, rank)
        y_blocks = after(round_one(y))
        cells, rest = round_two(y_blocks)
        everything = jnp.concatenate([jnp.stack(list(y_blocks.values())), *rest])
        sides = [everything] + [swap(everything, c) for c in range(1, core)]
        following = fresh_acts[k + 1] if k + 1 < tick_count else None
        around = of_cores([*y_blocks, *cells], range(core))
        result, *leaving = project_out(around, core, sides, w_out[0], blocks[0], following, rank)
        made.append(result)
        source = leaving[0] if leaving else None
    return jnp.stack(made)[None]


def solution(mesh):
    run = functools.partial(body, mesh.shape["section"], mesh.shape["dp"])
    return jax.shard_map(
        run,
        mesh=mesh,
        in_specs=(
            P(None, None, "dp"),
            P("section", None, "dp"),
            P("section", None),
            P("section", None, "dp", None),
            P("section", None, "dp", None),
            P("section", "dp", None),
            P("section", "dp"),
            P("section", None, "dp"),
        ),
        out_specs=P("section", None, None, "dp"),
        check_vma=False,
    )
```

```python
import functools

import jax
import jax.numpy as jnp
from jax import lax
from jax.experimental import pallas as pl
from jax.experimental.pallas import tpu as pltpu
from jax.sharding import PartitionSpec as P

EPS = 1e-06
VMEM_LIMIT = 20 * 1024 * 1024
PAD = 8
GROUP = 4


def split_dp(dp_count):
    core = 2 if dp_count % 2 == 0 else 1
    chips = dp_count // core
    near = 1
    while near * near * 4 <= chips:
        near *= 2
    return chips // near, near, core


def routes(far, near, cross):
    if (far, near) == (4, 2):
        if cross:
            return [4, 2, 0], [(1, [4, 2, 0]), (2, [4]), (3, [4])]
        return [4, 2, 1, 0], [(1, [4, 2]), (2, [4]), (3, [4])]
    line = [d * near for d in range(far)]
    return line, [(d, line) for d in range(1, near)]


def columns_of(rank_ref, core, cell, c, size):
    chip, side = lax.div(rank_ref[0], core), lax.rem(rank_ref[0], core)
    return pl.ds(pl.multiple_of(((chip ^ cell) * core + (side ^ c)) * size, size), size)


def project(blocks, core, values_of, weights_of, rank_ref, gain_ref, acc_ref, sq_ref, before=None, ready=None):
    lanes = sq_ref.shape[1]
    side = lax.rem(rank_ref[0], core)
    for first in range(0, len(blocks), GROUP):
        group = range(first, min(first + GROUP, len(blocks)))
        normed, columns, parts = [], [], []
        for n in group:
            cell, c = blocks[n]
            values = values_of(n).astype(jnp.float32)
            feat = values.shape[1]
            gains = gain_ref[:, columns_of(rank_ref, core, cell, c, feat)]
            normed.append((values * gains).astype(jnp.bfloat16))
            columns.append(pl.ds(pl.multiple_of((side ^ c) * feat, feat), feat))
            squares = values * values
            parts += [squares[:, m : m + lanes] for m in range(0, feat, lanes)]
        if ready is not None:
            for n in group:
                ready(n)
        if first == 0 and before is not None:
            parts.append(before[1][...])
        part = functools.reduce(jnp.add, parts)
        sq_ref[...] = part if first == 0 else sq_ref[...] + part
        for i in range(acc_ref.shape[0]):
            terms = [
                lax.dot_general(
                    normed[n - first],
                    weights_of(n)[i, :, columns[n - first]],
                    (((1,), (1,)), ((), ())),
                    preferred_element_type=jnp.float32,
                )
                for n in group
            ]
            if first > 0:
                terms.append(acc_ref[i])
            elif before is not None:
                terms.append(before[0][i])
            acc_ref[i] = functools.reduce(jnp.add, terms)


def load_kernel(blocks, order, core, rank_ref, x_ref, w_far, gain_far, taps_far, decay_far, *refs):
    w_refs, (acc_ref, sq_ref, gain_ref, long_ref) = refs[: len(order)], refs[len(order) : len(order) + 4]
    sems, taps_ref, decay_ref, small_sems = refs[len(order) + 4 :]
    small = [(gain_far, gain_ref), (taps_far, taps_ref), (decay_far, decay_ref)]
    small = [pltpu.make_async_copy(src, dst, small_sems.at[n]) for n, (src, dst) in enumerate(small)]
    wide = w_refs[0].shape[2]
    chip = lax.div(rank_ref[0], core)
    copies = []
    for n, cell in enumerate(order):
        columns = pl.ds(pl.multiple_of((chip ^ cell) * wide, wide), wide)
        copies.append(
            [
                pltpu.make_async_copy(w_far.at[i, :, columns], w_refs[n].at[i], sems.at[n, i])
                for i in range(w_far.shape[0])
            ]
        )
    for group in [small] + copies:
        for copy in group:
            copy.start()
    for copy in small:
        copy.wait()
    lags = lax.broadcasted_iota(jnp.int32, long_ref.shape, 0).astype(jnp.float32)
    long_ref[...] = taps_ref[...].T * jnp.exp(-decay_ref[...] * lags)

    def ready(n):
        for copy in copies[n]:
            copy.wait()

    project(blocks, core, lambda n: x_ref[n], lambda n: w_refs[n], rank_ref, gain_ref, acc_ref, sq_ref, None, ready)
    for n in range(len(blocks), len(order)):
        ready(n)


def first_kernel(blocks, core, rank_ref, x_ref, gain_ref, *refs):
    w_refs, (acc_ref, sq_ref) = refs[:-2], refs[-2:]
    project(blocks, core, lambda n: x_ref[n], lambda n: w_refs[n], rank_ref, gain_ref, acc_ref, sq_ref)


def more_kernel(blocks, core, rank_ref, x_ref, gain_ref, acc_in, sq_in, *refs):
    w_refs, (acc_ref, sq_ref) = refs[:-2], refs[-2:]
    before = (acc_in, sq_in)
    project(blocks, core, lambda n: x_ref[n], lambda n: w_refs[n], rank_ref, gain_ref, acc_ref, sq_ref, before)


def mix_kernel(blocks, core, model_width, rank_ref, *refs):
    sides, refs = refs[: core - 1], refs[core - 1 :]
    count = len(blocks) // max(core - 1, 1)
    gain_ref, acc_in, sq_in, short_ref, long_ref = refs[:5]
    w_refs = refs[5 : 5 + count]
    y_ref, acc_ref, sq_ref, pad_ref, query_ref = refs[5 + count :]
    branches, tok_len, chan = acc_in.shape
    project(
        blocks,
        core,
        lambda n: sides[n // count][n % count],
        lambda n: w_refs[n % count],
        rank_ref,
        gain_ref,
        acc_ref,
        sq_ref,
        (acc_in, sq_in),
    )

    total = jnp.sum(sq_ref[...], axis=1, keepdims=True)
    factor = lax.rsqrt(total / model_width + EPS)
    taps = short_ref.shape[1]
    pad_ref[0:PAD, :] = jnp.zeros((PAD, chan), jnp.float32)

    def branch(i):
        u = acc_ref[i] * factor
        pad_ref[PAD : PAD + tok_len, :] = u
        z = short_ref[i, 0] * u
        for j in range(1, taps):
            z = z + short_ref[i, j] * pad_ref[PAD - j : PAD - j + tok_len, :]
        return z

    query_ref[...] = branch(1)
    product = query_ref[...] * branch(2)
    query_ref[...] = branch(0)
    pad_ref[PAD : PAD + tok_len, :] = product
    width = min(chan, 128)
    tiles = tok_len // 8
    for c in range(0, chan, width):
        cols = slice(c, c + width)
        conv = [None] * tiles
        for b in range(8):
            moved = [pad_ref[PAD - b + 8 * i : PAD - b + 8 * i + 8, cols] for i in range(tiles)]
            for a in range(long_ref.shape[0] // 8):
                tap = long_ref[8 * a + b : 8 * a + b + 1, cols]
                for i in range(a, tiles):
                    term = tap * moved[i - a]
                    conv[i] = term if conv[i] is None else conv[i] + term
        for i in range(0, tiles, 2):
            at = slice(8 * i, 8 * i + 16)
            both = jnp.concatenate(conv[i : i + 2], axis=0)
            y_ref[at, cols] = (query_ref[at, cols] * both).astype(jnp.bfloat16)


def share_of_out(blocks, core, side_ref, rank_ref, w_ref, total):
    chan = side_ref.shape[2]
    for first in range(0, len(blocks), GROUP):
        terms = []
        for n in range(first, min(first + GROUP, len(blocks))):
            rows = columns_of(rank_ref, core, *blocks[n], chan)
            terms.append(jnp.dot(side_ref[n], w_ref[rows, :], preferred_element_type=jnp.float32))
        total = functools.reduce(jnp.add, terms, total)
    return total


def out_early_kernel(blocks, core, rank_ref, side_ref, w_ref, own_ref, sum_ref):
    sum_ref[...] = share_of_out(blocks, core, side_ref, rank_ref, w_ref, own_ref[...].astype(jnp.float32))


def out_kernel(blocks, core, tick, rank_ref, *refs):
    sides, (w_ref, sum_ref, fresh_ref, *result_refs) = refs[: core - 1], refs[core - 1 :]
    total = sum_ref[...]
    for c, side_ref in enumerate(sides):
        count = side_ref.shape[0]
        total = share_of_out(blocks[c * count : (c + 1) * count], core, side_ref, rank_ref, w_ref, total)
    result = total.astype(jnp.bfloat16)
    result_refs[0][...] = result
    if len(result_refs) > 1:
        result_refs[1][...] = jnp.where(rank_ref[1] == 1, fresh_ref[tick + 1], result)


def in_vmem(count):
    return [pl.BlockSpec(memory_space=pltpu.VMEM)] * count


def call(kernel, operands, outs, scratch, flops, name, far_operands=()):
    specs = [pl.BlockSpec(memory_space=pltpu.SMEM)] + in_vmem(len(operands) - 1)
    operands = list(operands)
    for n in far_operands:
        specs[n] = pl.BlockSpec(memory_space=pltpu.HBM)
        operands[n] = pltpu.with_memory_space_constraint(operands[n], pltpu.HBM)
    return pl.pallas_call(
        kernel,
        in_specs=specs,
        out_specs=in_vmem(len(outs)),
        out_shape=outs,
        scratch_shapes=scratch,
        compiler_params=pltpu.CompilerParams(vmem_limit_bytes=VMEM_LIMIT),
        cost_estimate=pl.CostEstimate(flops=flops, bytes_accessed=flops // 1024, transcendentals=0),
        name=name,
    )(*operands)


def sums_of(x, branches, chan):
    _, rows, feat = x.shape
    return [
        jax.ShapeDtypeStruct((branches, rows, chan), jnp.float32),
        jax.ShapeDtypeStruct((rows, min(feat, 128)), jnp.float32),
    ]


def project_load(blocks, order, core, x, w_in, gain, taps, decay, rank):
    branches, chan, model_width = w_in.shape
    piece = jax.ShapeDtypeStruct((branches, chan, model_width // len(order)), w_in.dtype)
    outs = [piece] * len(order) + sums_of(x, branches, chan)
    outs += [jax.ShapeDtypeStruct(gain.shape, gain.dtype), jax.ShapeDtypeStruct(taps.shape[::-1], taps.dtype)]
    scratch = [
        pltpu.SemaphoreType.DMA((len(order), branches)),
        pltpu.VMEM(taps.shape, taps.dtype),
        pltpu.VMEM(decay.shape, decay.dtype),
        pltpu.SemaphoreType.DMA((3,)),
    ]
    kernel = functools.partial(load_kernel, blocks, order, core)
    flops = 2 * x.size * branches * chan
    *pieces, acc, sq, gain, long_rows = call(
        kernel, [rank, x, w_in, gain, taps, decay], outs, scratch, flops, "project_load", [2, 3, 4, 5]
    )
    return [acc, sq], {"in": dict(zip(order, pieces)), "gain": gain, "long": long_rows}


def project_part(blocks, core, x, params, sums, rank):
    w_refs = [params["in"][cell] for cell, _ in blocks]
    branches, chan, _ = w_refs[0].shape
    kernel, name = (more_kernel, "project_more") if sums else (first_kernel, "project_first")
    operands = [rank, x, params["gain"], *sums, *w_refs]
    flops = 2 * x.size * branches * chan
    return call(functools.partial(kernel, blocks, core), operands, sums_of(x, branches, chan), [], flops, name)


def mix(blocks, core, model_width, sides, params, sums, short_rows, rank):
    rows, chan = sums[0].shape[1:]
    scratch = [pltpu.VMEM(total.shape, total.dtype) for total in sums]
    scratch += [pltpu.VMEM((PAD + rows, chan), jnp.float32), pltpu.VMEM((rows, chan), jnp.float32)]
    w_refs = [params["in"][cell] for cell, _ in blocks[: len(blocks) // max(core - 1, 1)]]
    return call(
        functools.partial(mix_kernel, blocks, core, model_width),
        [rank, *sides, params["gain"], *sums, short_rows, params["long"], *w_refs],
        [jax.ShapeDtypeStruct((rows, chan), jnp.bfloat16)],
        scratch,
        2 * rows * model_width * 3 * chan,
        "project_mix",
    )[0]


def project_out_early(blocks, core, side, w_out, own, rank):
    return call(
        functools.partial(out_early_kernel, blocks, core),
        [rank, side, w_out, own],
        [jax.ShapeDtypeStruct(own.shape, jnp.float32)],
        [],
        2 * side.size * w_out.shape[1],
        "project_out_early",
    )[0]


def project_out(blocks, core, tick, sides, w_out, total, fresh, rank):
    result = jax.ShapeDtypeStruct(total.shape, jnp.bfloat16)
    return call(
        functools.partial(out_kernel, blocks, core, tick),
        [rank, *sides, w_out, total, fresh],
        [result, result] if tick + 1 < fresh.shape[0] else [result],
        [],
        total.size * w_out.shape[0],
        "project_out",
    )


def body(section_count, dp_count, fresh_acts, carried, norm_gain, w_in, short_filter, filter_taps, decay_rate, w_out):
    tick_count, tok_len, _ = fresh_acts.shape
    far, near, core = split_dp(dp_count)
    group = near * core
    section_idx = lax.axis_index("section")
    rank = jnp.stack([lax.axis_index("dp"), (section_idx == section_count - 1).astype(jnp.int32)])

    def swap(value, offset):
        return lax.ppermute(value, "dp", [(r, r ^ offset) for r in range(dp_count)])


    def onward(value, offset):
        pairs = [
            (s * dp_count + r, (s + 1) % section_count * dp_count + (r ^ offset))
            for s in range(section_count)
            for r in range(dp_count)
        ]
        return lax.ppermute(value, ("section", "dp"), pairs)

    def after(value, *earlier):
        return lax.optimization_barrier((value, [x for x in earlier if x is not None]))[0]

    def round_one(source, cross=False):
        first, _ = routes(far, near, cross)
        if cross:
            blocks = [onward(source, d * core) for d in first]
        else:
            blocks = [swap(source, d * core) if d else source for d in first]
        return dict(zip(first, lax.optimization_barrier(blocks)))

    def round_two(blocks, cross=False):
        _, second = routes(far, near, cross)
        leaving = lax.optimization_barrier([jnp.stack([blocks[b] for b in sent]) for _, sent in second])
        rest = [swap(payload, d * core) for payload, (d, _) in zip(leaving, second)]
        return [d ^ b for d, sent in second for b in sent], rest

    def of_cores(cells, cores):
        return [(cell, c) for c in cores for cell in cells]

    short_rows = short_filter.transpose(1, 3, 0, 2)
    source = jnp.where(section_idx == 0, fresh_acts[0], carried[0])
    params, made = {}, []
    for k in range(tick_count):
        blocks = round_one(source, k > 0)
        cells, rest = round_two(blocks, k > 0)
        order = [*blocks, *cells]
        direct = jnp.stack(list(blocks.values()))
        here = of_cores(blocks, [0])
        if params:
            sums = project_part(here, core, direct, params, [], rank)
        else:
            sums, params = project_load(
                here, order, core, direct, w_in[0], norm_gain, filter_taps[0], decay_rate, rank
            )
        relayed = jnp.concatenate(after(rest, sums))
        everything = jnp.concatenate([direct, relayed])
        sides = [swap(everything, c) for c in range(1, core)]
        sums = project_part(of_cores(cells, [0]), core, relayed, params, sums, rank)
        sides = after(sides, sums)
        y = mix(of_cores(order, range(1, core)), core, norm_gain.shape[1], sides, params, sums, short_rows, rank)
        y_blocks = round_one(y)
        cells, rest = round_two(y_blocks)
        everything = jnp.concatenate([jnp.stack(list(y_blocks.values())), *rest])
        sides = [swap(everything, c) for c in range(1, core)]
        order = [*y_blocks, *cells]
        total = project_out_early(of_cores(order, [0]), core, everything, w_out[0], blocks[0], rank)
        sides = after(sides, total)
        blocks = of_cores(order, range(1, core))
        result, *leaving = project_out(blocks, core, k, sides, w_out[0], total, fresh_acts, rank)
        made.append(result)
        source = leaving[0] if leaving else None
    return jnp.stack(made)[None]


def solution(mesh):
    run = functools.partial(body, mesh.shape["section"], mesh.shape["dp"])
    return jax.shard_map(
        run,
        mesh=mesh,
        in_specs=(
            P(None, None, "dp"),
            P("section", None, "dp"),
            P("section", None),
            P("section", None, "dp", None),
            P("section", None, "dp", None),
            P("section", "dp", None),
            P("section", "dp"),
            P("section", None, "dp"),
        ),
        out_specs=P("section", None, None, "dp"),
        check_vma=False,
    )
```

```python
import functools

import jax
import jax.numpy as jnp
from jax import lax
from jax.experimental import pallas as pl
from jax.experimental.pallas import tpu as pltpu
from jax.sharding import PartitionSpec as P

EPS = 1e-06
VMEM_LIMIT = 20 * 1024 * 1024
PAD = 8
GROUP = 4


def split_dp(dp_count):
    core = 2 if dp_count % 2 == 0 else 1
    chips = dp_count // core
    near = 1
    while near * near * 4 <= chips:
        near *= 2
    return chips // near, near, core


def routes(far, near, cross):
    if (far, near) == (4, 2):
        if cross:
            return [0, 2, 4], [(1, [2, 4]), (2, [4]), (3, [4])], [1]
        return [0, 1, 2, 4], [(1, [2, 4]), (2, [4]), (3, [4])], []
    line = [d * near for d in range(far)]
    return line, [(d, line) for d in range(1, near)], []


def columns_of(rank_ref, core, cell, c, size):
    chip, side = lax.div(rank_ref[0], core), lax.rem(rank_ref[0], core)
    return pl.ds(pl.multiple_of(((chip ^ cell) * core + (side ^ c)) * size, size), size)


def project(blocks, core, values_of, weights_of, rank_ref, gain_ref, acc_ref, sq_ref, before=None, ready=None):
    lanes = sq_ref.shape[1]
    side = lax.rem(rank_ref[0], core)
    for first in range(0, len(blocks), GROUP):
        group = range(first, min(first + GROUP, len(blocks)))
        normed, columns, parts = [], [], []
        for n in group:
            cell, c = blocks[n]
            values = values_of(n).astype(jnp.float32)
            feat = values.shape[1]
            gains = gain_ref[:, columns_of(rank_ref, core, cell, c, feat)]
            normed.append((values * gains).astype(jnp.bfloat16))
            columns.append(pl.ds(pl.multiple_of((side ^ c) * feat, feat), feat))
            squares = values * values
            parts += [squares[:, m : m + lanes] for m in range(0, feat, lanes)]
        if ready is not None:
            for n in group:
                ready(n)
        if first == 0 and before is not None:
            parts.append(before[1][...])
        part = functools.reduce(jnp.add, parts)
        sq_ref[...] = part if first == 0 else sq_ref[...] + part
        for i in range(acc_ref.shape[0]):
            terms = [
                lax.dot_general(
                    normed[n - first],
                    weights_of(n)[i, :, columns[n - first]],
                    (((1,), (1,)), ((), ())),
                    preferred_element_type=jnp.float32,
                )
                for n in group
            ]
            if first > 0:
                terms.append(acc_ref[i])
            elif before is not None:
                terms.append(before[0][i])
            acc_ref[i] = functools.reduce(jnp.add, terms)


def load_kernel(blocks, order, core, rank_ref, x_ref, w_far, gain_far, taps_far, decay_far, *refs):
    w_refs, (acc_ref, sq_ref, gain_ref, long_ref) = refs[: len(order)], refs[len(order) : len(order) + 4]
    sems, taps_ref, decay_ref, small_sems = refs[len(order) + 4 :]
    small = [(gain_far, gain_ref), (taps_far, taps_ref), (decay_far, decay_ref)]
    small = [pltpu.make_async_copy(src, dst, small_sems.at[n]) for n, (src, dst) in enumerate(small)]
    wide = w_refs[0].shape[2]
    chip = lax.div(rank_ref[0], core)
    copies = []
    for n, cell in enumerate(order):
        columns = pl.ds(pl.multiple_of((chip ^ cell) * wide, wide), wide)
        copies.append(
            [
                pltpu.make_async_copy(w_far.at[i, :, columns], w_refs[n].at[i], sems.at[n, i])
                for i in range(w_far.shape[0])
            ]
        )
    for group in [small] + copies:
        for copy in group:
            copy.start()
    for copy in small:
        copy.wait()
    lags = lax.broadcasted_iota(jnp.int32, long_ref.shape, 0).astype(jnp.float32)
    long_ref[...] = taps_ref[...].T * jnp.exp(-decay_ref[...] * lags)

    def ready(n):
        for copy in copies[n]:
            copy.wait()

    project(blocks, core, lambda n: x_ref[n], lambda n: w_refs[n], rank_ref, gain_ref, acc_ref, sq_ref, None, ready)
    for n in range(len(blocks), len(order)):
        ready(n)


def first_kernel(blocks, core, rank_ref, x_ref, gain_ref, *refs):
    w_refs, (acc_ref, sq_ref) = refs[:-2], refs[-2:]
    project(blocks, core, lambda n: x_ref[n], lambda n: w_refs[n], rank_ref, gain_ref, acc_ref, sq_ref)


def more_kernel(blocks, core, rank_ref, x_ref, gain_ref, acc_in, sq_in, *refs):
    w_refs, (acc_ref, sq_ref) = refs[:-2], refs[-2:]
    before = (acc_in, sq_in)
    project(blocks, core, lambda n: x_ref[n], lambda n: w_refs[n], rank_ref, gain_ref, acc_ref, sq_ref, before)


def mix_kernel(blocks, core, model_width, rank_ref, *refs):
    sides, refs = refs[: core - 1], refs[core - 1 :]
    count = len(blocks) // max(core - 1, 1)
    gain_ref, acc_in, sq_in, short_ref, long_ref = refs[:5]
    w_refs = refs[5 : 5 + count]
    y_ref, acc_ref, sq_ref, pad_ref, query_ref = refs[5 + count :]
    branches, tok_len, chan = acc_in.shape
    project(
        blocks,
        core,
        lambda n: sides[n // count][n % count],
        lambda n: w_refs[n % count],
        rank_ref,
        gain_ref,
        acc_ref,
        sq_ref,
        (acc_in, sq_in),
    )

    total = jnp.sum(sq_ref[...], axis=1, keepdims=True)
    factor = lax.rsqrt(total / model_width + EPS)
    taps = short_ref.shape[1]
    pad_ref[0:PAD, :] = jnp.zeros((PAD, chan), jnp.float32)

    def branch(i):
        u = acc_ref[i] * factor
        pad_ref[PAD : PAD + tok_len, :] = u
        z = short_ref[i, 0] * u
        for j in range(1, taps):
            z = z + short_ref[i, j] * pad_ref[PAD - j : PAD - j + tok_len, :]
        return z

    query_ref[...] = branch(1)
    product = query_ref[...] * branch(2)
    query_ref[...] = branch(0)
    pad_ref[PAD : PAD + tok_len, :] = product
    width = min(chan, 128)
    tiles = tok_len // 8
    for c in range(0, chan, width):
        cols = slice(c, c + width)
        conv = [None] * tiles
        for b in range(8):
            moved = [pad_ref[PAD - b + 8 * i : PAD - b + 8 * i + 8, cols] for i in range(tiles)]
            for a in range(long_ref.shape[0] // 8):
                tap = long_ref[8 * a + b : 8 * a + b + 1, cols]
                for i in range(a, tiles):
                    term = tap * moved[i - a]
                    conv[i] = term if conv[i] is None else conv[i] + term
        for i in range(0, tiles, 2):
            at = slice(8 * i, 8 * i + 16)
            both = jnp.concatenate(conv[i : i + 2], axis=0)
            y_ref[at, cols] = (query_ref[at, cols] * both).astype(jnp.bfloat16)


def share_of_out(blocks, core, side_ref, rank_ref, w_ref, total):
    chan = side_ref.shape[2]
    for first in range(0, len(blocks), GROUP):
        terms = []
        for n in range(first, min(first + GROUP, len(blocks))):
            rows = columns_of(rank_ref, core, *blocks[n], chan)
            terms.append(jnp.dot(side_ref[n], w_ref[rows, :], preferred_element_type=jnp.float32))
        total = functools.reduce(jnp.add, terms, total)
    return total


def out_early_kernel(blocks, core, rank_ref, side_ref, w_ref, own_ref, sum_ref):
    sum_ref[...] = share_of_out(blocks, core, side_ref, rank_ref, w_ref, own_ref[...].astype(jnp.float32))


def out_kernel(blocks, core, tick, rank_ref, *refs):
    sides, (w_ref, sum_ref, fresh_ref, *result_refs) = refs[: core - 1], refs[core - 1 :]
    total = sum_ref[...]
    for c, side_ref in enumerate(sides):
        count = side_ref.shape[0]
        total = share_of_out(blocks[c * count : (c + 1) * count], core, side_ref, rank_ref, w_ref, total)
    result = total.astype(jnp.bfloat16)
    result_refs[0][...] = result
    if len(result_refs) > 1:
        result_refs[1][...] = jnp.where(rank_ref[1] == 1, fresh_ref[tick + 1], result)


def in_vmem(count):
    return [pl.BlockSpec(memory_space=pltpu.VMEM)] * count


def call(kernel, operands, outs, scratch, flops, name, far_operands=()):
    specs = [pl.BlockSpec(memory_space=pltpu.SMEM)] + in_vmem(len(operands) - 1)
    operands = list(operands)
    for n in far_operands:
        specs[n] = pl.BlockSpec(memory_space=pltpu.HBM)
        operands[n] = pltpu.with_memory_space_constraint(operands[n], pltpu.HBM)
    return pl.pallas_call(
        kernel,
        in_specs=specs,
        out_specs=in_vmem(len(outs)),
        out_shape=outs,
        scratch_shapes=scratch,
        compiler_params=pltpu.CompilerParams(vmem_limit_bytes=VMEM_LIMIT),
        cost_estimate=pl.CostEstimate(flops=flops, bytes_accessed=flops // 1024, transcendentals=0),
        name=name,
    )(*operands)


def sums_of(x, branches, chan):
    _, rows, feat = x.shape
    return [
        jax.ShapeDtypeStruct((branches, rows, chan), jnp.float32),
        jax.ShapeDtypeStruct((rows, min(feat, 128)), jnp.float32),
    ]


def project_load(blocks, order, core, x, w_in, gain, taps, decay, rank):
    branches, chan, model_width = w_in.shape
    piece = jax.ShapeDtypeStruct((branches, chan, model_width // len(order)), w_in.dtype)
    outs = [piece] * len(order) + sums_of(x, branches, chan)
    outs += [jax.ShapeDtypeStruct(gain.shape, gain.dtype), jax.ShapeDtypeStruct(taps.shape[::-1], taps.dtype)]
    scratch = [
        pltpu.SemaphoreType.DMA((len(order), branches)),
        pltpu.VMEM(taps.shape, taps.dtype),
        pltpu.VMEM(decay.shape, decay.dtype),
        pltpu.SemaphoreType.DMA((3,)),
    ]
    kernel = functools.partial(load_kernel, blocks, order, core)
    flops = 2 * x.size * branches * chan
    *pieces, acc, sq, gain, long_rows = call(
        kernel, [rank, x, w_in, gain, taps, decay], outs, scratch, flops, "project_load", [2, 3, 4, 5]
    )
    return [acc, sq], {"in": dict(zip(order, pieces)), "gain": gain, "long": long_rows}


def project_part(blocks, core, x, params, sums, rank):
    w_refs = [params["in"][cell] for cell, _ in blocks]
    branches, chan, _ = w_refs[0].shape
    kernel, name = (more_kernel, "project_more") if sums else (first_kernel, "project_first")
    operands = [rank, x, params["gain"], *sums, *w_refs]
    flops = 2 * x.size * branches * chan
    return call(functools.partial(kernel, blocks, core), operands, sums_of(x, branches, chan), [], flops, name)


def mix(blocks, core, model_width, sides, params, sums, short_rows, rank):
    rows, chan = sums[0].shape[1:]
    scratch = [pltpu.VMEM(total.shape, total.dtype) for total in sums]
    scratch += [pltpu.VMEM((PAD + rows, chan), jnp.float32), pltpu.VMEM((rows, chan), jnp.float32)]
    w_refs = [params["in"][cell] for cell, _ in blocks[: len(blocks) // max(core - 1, 1)]]
    return call(
        functools.partial(mix_kernel, blocks, core, model_width),
        [rank, *sides, params["gain"], *sums, short_rows, params["long"], *w_refs],
        [jax.ShapeDtypeStruct((rows, chan), jnp.bfloat16)],
        scratch,
        2 * rows * model_width * 3 * chan,
        "project_mix",
    )[0]


def project_out_early(blocks, core, side, w_out, own, rank):
    return call(
        functools.partial(out_early_kernel, blocks, core),
        [rank, side, w_out, own],
        [jax.ShapeDtypeStruct(own.shape, jnp.float32)],
        [],
        2 * side.size * w_out.shape[1],
        "project_out_early",
    )[0]


def project_out(blocks, core, tick, sides, w_out, total, fresh, rank):
    result = jax.ShapeDtypeStruct(total.shape, jnp.bfloat16)
    return call(
        functools.partial(out_kernel, blocks, core, tick),
        [rank, *sides, w_out, total, fresh],
        [result, result] if tick + 1 < fresh.shape[0] else [result],
        [],
        total.size * w_out.shape[0],
        "project_out",
    )


def body(section_count, dp_count, fresh_acts, carried, norm_gain, w_in, short_filter, filter_taps, decay_rate, w_out):
    tick_count, tok_len, _ = fresh_acts.shape
    far, near, core = split_dp(dp_count)
    group = near * core
    section_idx = lax.axis_index("section")
    rank = jnp.stack([lax.axis_index("dp"), (section_idx == section_count - 1).astype(jnp.int32)])

    def swap(value, offset):
        return lax.ppermute(value, "dp", [(r, r ^ offset) for r in range(dp_count)])


    def onward(value, offset):
        pairs = [
            (s * dp_count + r, (s + 1) % section_count * dp_count + (r ^ offset))
            for s in range(section_count)
            for r in range(dp_count)
        ]
        return lax.ppermute(value, ("section", "dp"), pairs)

    def after(value, *earlier):
        return lax.optimization_barrier((value, [x for x in earlier if x is not None]))[0]

    def round_one(source, cross=False):
        first, _, later = routes(far, near, cross)
        if cross:
            blocks = [onward(source, d * core) for d in first]
        else:
            blocks = [swap(source, d * core) if d else source for d in first]
        blocks, aside = lax.optimization_barrier((blocks, [swap(source, d * core) for d in later]))
        return dict(zip(first, blocks)), aside

    def round_two(blocks, aside, cross=False):
        _, second, later = routes(far, near, cross)
        leaving = lax.optimization_barrier([jnp.stack([blocks[b] for b in sent]) for _, sent in second])
        rest = [swap(payload, d * core) for payload, (d, _) in zip(leaving, second)]
        rest += [onward(block, 0)[None] for block in aside]
        return [d ^ b for d, sent in second for b in sent] + later, rest

    def of_cores(cells, cores):
        return [(cell, c) for c in cores for cell in cells]

    short_rows = short_filter.transpose(1, 3, 0, 2)
    source = jnp.where(section_idx == 0, fresh_acts[0], carried[0])
    params, made = {}, []
    for k in range(tick_count):
        blocks, aside = round_one(source, k > 0)
        cells, rest = round_two(blocks, aside, k > 0)
        order = [*blocks, *cells]
        direct = jnp.stack(list(blocks.values()))
        here = of_cores(blocks, [0])
        if params:
            sums = project_part(here, core, after(direct, rest[1 % len(rest)]), params, [], rank)
        else:
            sums, params = project_load(
                here, order, core, direct, w_in[0], norm_gain, filter_taps[0], decay_rate, rank
            )
        relayed = jnp.concatenate(after(rest, sums))
        everything = jnp.concatenate([direct, relayed])
        sides = [swap(everything, c) for c in range(1, core)]
        sums = project_part(of_cores(cells, [0]), core, relayed, params, sums, rank)
        sides = after(sides, sums)
        y = mix(of_cores(order, range(1, core)), core, norm_gain.shape[1], sides, params, sums, short_rows, rank)
        y_blocks, _ = round_one(y)
        cells, rest = round_two(y_blocks, [])
        everything = jnp.concatenate([jnp.stack(list(y_blocks.values())), *rest])
        sides = [swap(everything, c) for c in range(1, core)]
        order = [*y_blocks, *cells]
        total = project_out_early(of_cores(order, [0]), core, everything, w_out[0], blocks[0], rank)
        sides = after(sides, total)
        blocks = of_cores(order, range(1, core))
        result, *leaving = project_out(blocks, core, k, sides, w_out[0], total, fresh_acts, rank)
        made.append(result)
        source = leaving[0] if leaving else None
    return jnp.stack(made)[None]


def solution(mesh):
    run = functools.partial(body, mesh.shape["section"], mesh.shape["dp"])
    return jax.shard_map(
        run,
        mesh=mesh,
        in_specs=(
            P(None, None, "dp"),
            P("section", None, "dp"),
            P("section", None),
            P("section", None, "dp", None),
            P("section", None, "dp", None),
            P("section", "dp", None),
            P("section", "dp"),
            P("section", None, "dp"),
        ),
        out_specs=P("section", None, None, "dp"),
        check_vma=False,
    )
```

```python
import functools

import jax
import jax.numpy as jnp
from jax import lax
from jax.experimental import pallas as pl
from jax.experimental.pallas import tpu as pltpu
from jax.sharding import PartitionSpec as P

EPS = 1e-06
VMEM_LIMIT = 20 * 1024 * 1024
PAD = 8
GROUP = 4


def split_dp(dp_count):
    core = 2 if dp_count % 2 == 0 else 1
    chips = dp_count // core
    near = 1
    while near * near * 4 <= chips:
        near *= 2
    return chips // near, near, core


def routes(far, near, cross):
    if (far, near) == (4, 2):
        if cross:
            return [0, 2, 4], [(1, [2, 4]), (3, [4]), (2, [4])], [1]
        return [0, 1, 2, 4], [(1, [2, 4]), (3, [4]), (2, [4])], []
    line = [d * near for d in range(far)]
    return line, [(d, line) for d in range(1, near)], []


def columns_of(rank_ref, core, cell, c, size):
    chip, side = lax.div(rank_ref[0], core), lax.rem(rank_ref[0], core)
    return pl.ds(pl.multiple_of(((chip ^ cell) * core + (side ^ c)) * size, size), size)


def project(blocks, core, values_of, weights_of, rank_ref, gain_ref, acc_ref, sq_ref, before=None, ready=None):
    lanes = sq_ref.shape[1]
    side = lax.rem(rank_ref[0], core)
    for first in range(0, len(blocks), GROUP):
        group = range(first, min(first + GROUP, len(blocks)))
        normed, columns, parts = [], [], []
        for n in group:
            cell, c = blocks[n]
            values = values_of(n).astype(jnp.float32)
            feat = values.shape[1]
            gains = gain_ref[:, columns_of(rank_ref, core, cell, c, feat)]
            normed.append((values * gains).astype(jnp.bfloat16))
            columns.append(pl.ds(pl.multiple_of((side ^ c) * feat, feat), feat))
            squares = values * values
            parts += [squares[:, m : m + lanes] for m in range(0, feat, lanes)]
        if ready is not None:
            for n in group:
                ready(n)
        if first == 0 and before is not None:
            parts.append(before[1][...])
        part = functools.reduce(jnp.add, parts)
        sq_ref[...] = part if first == 0 else sq_ref[...] + part
        for i in range(acc_ref.shape[0]):
            terms = [
                lax.dot_general(
                    normed[n - first],
                    weights_of(n)[i, :, columns[n - first]],
                    (((1,), (1,)), ((), ())),
                    preferred_element_type=jnp.float32,
                )
                for n in group
            ]
            if first > 0:
                terms.append(acc_ref[i])
            elif before is not None:
                terms.append(before[0][i])
            acc_ref[i] = functools.reduce(jnp.add, terms)


def load_kernel(blocks, order, core, rank_ref, x_ref, w_far, gain_far, taps_far, decay_far, *refs):
    w_refs, (acc_ref, sq_ref, gain_ref, long_ref) = refs[: len(order)], refs[len(order) : len(order) + 4]
    sems, taps_ref, decay_ref, small_sems = refs[len(order) + 4 :]
    small = [(gain_far, gain_ref), (taps_far, taps_ref), (decay_far, decay_ref)]
    small = [pltpu.make_async_copy(src, dst, small_sems.at[n]) for n, (src, dst) in enumerate(small)]
    wide = w_refs[0].shape[2]
    chip = lax.div(rank_ref[0], core)
    copies = []
    for n, cell in enumerate(order):
        columns = pl.ds(pl.multiple_of((chip ^ cell) * wide, wide), wide)
        copies.append(
            [
                pltpu.make_async_copy(w_far.at[i, :, columns], w_refs[n].at[i], sems.at[n, i])
                for i in range(w_far.shape[0])
            ]
        )
    for group in [small] + copies:
        for copy in group:
            copy.start()
    for copy in small:
        copy.wait()
    lags = lax.broadcasted_iota(jnp.int32, long_ref.shape, 0).astype(jnp.float32)
    long_ref[...] = taps_ref[...].T * jnp.exp(-decay_ref[...] * lags)

    def ready(n):
        for copy in copies[n]:
            copy.wait()

    project(blocks, core, lambda n: x_ref[n], lambda n: w_refs[n], rank_ref, gain_ref, acc_ref, sq_ref, None, ready)
    for n in range(len(blocks), len(order)):
        ready(n)


def first_kernel(blocks, core, rank_ref, x_ref, gain_ref, *refs):
    w_refs, (acc_ref, sq_ref) = refs[:-2], refs[-2:]
    project(blocks, core, lambda n: x_ref[n], lambda n: w_refs[n], rank_ref, gain_ref, acc_ref, sq_ref)


def more_kernel(blocks, core, rank_ref, x_ref, gain_ref, acc_in, sq_in, *refs):
    w_refs, (acc_ref, sq_ref) = refs[:-2], refs[-2:]
    before = (acc_in, sq_in)
    project(blocks, core, lambda n: x_ref[n], lambda n: w_refs[n], rank_ref, gain_ref, acc_ref, sq_ref, before)


def mix_kernel(blocks, core, model_width, rank_ref, *refs):
    sides, refs = refs[: core - 1], refs[core - 1 :]
    count = len(blocks) // max(core - 1, 1)
    gain_ref, acc_in, sq_in, short_ref, long_ref = refs[:5]
    w_refs = refs[5 : 5 + count]
    y_ref, acc_ref, sq_ref, pad_ref, query_ref = refs[5 + count :]
    branches, tok_len, chan = acc_in.shape
    project(
        blocks,
        core,
        lambda n: sides[n // count][n % count],
        lambda n: w_refs[n % count],
        rank_ref,
        gain_ref,
        acc_ref,
        sq_ref,
        (acc_in, sq_in),
    )

    total = jnp.sum(sq_ref[...], axis=1, keepdims=True)
    factor = lax.rsqrt(total / model_width + EPS)
    taps = short_ref.shape[1]
    pad_ref[0:PAD, :] = jnp.zeros((PAD, chan), jnp.float32)

    def branch(i):
        u = acc_ref[i] * factor
        pad_ref[PAD : PAD + tok_len, :] = u
        z = short_ref[i, 0] * u
        for j in range(1, taps):
            z = z + short_ref[i, j] * pad_ref[PAD - j : PAD - j + tok_len, :]
        return z

    query_ref[...] = branch(1)
    product = query_ref[...] * branch(2)
    query_ref[...] = branch(0)
    pad_ref[PAD : PAD + tok_len, :] = product
    width = min(chan, 128)
    tiles = tok_len // 8
    for c in range(0, chan, width):
        cols = slice(c, c + width)
        conv = [None] * tiles
        for b in range(8):
            moved = [pad_ref[PAD - b + 8 * i : PAD - b + 8 * i + 8, cols] for i in range(tiles)]
            for a in range(long_ref.shape[0] // 8):
                tap = long_ref[8 * a + b : 8 * a + b + 1, cols]
                for i in range(a, tiles):
                    term = tap * moved[i - a]
                    conv[i] = term if conv[i] is None else conv[i] + term
        for i in range(0, tiles, 2):
            at = slice(8 * i, 8 * i + 16)
            both = jnp.concatenate(conv[i : i + 2], axis=0)
            y_ref[at, cols] = (query_ref[at, cols] * both).astype(jnp.bfloat16)


def share_of_out(blocks, core, side_ref, rank_ref, w_ref, total):
    chan = side_ref.shape[2]
    for first in range(0, len(blocks), GROUP):
        terms = []
        for n in range(first, min(first + GROUP, len(blocks))):
            rows = columns_of(rank_ref, core, *blocks[n], chan)
            terms.append(jnp.dot(side_ref[n], w_ref[rows, :], preferred_element_type=jnp.float32))
        total = functools.reduce(jnp.add, terms, total)
    return total


def out_early_kernel(blocks, core, rank_ref, side_ref, w_ref, own_ref, sum_ref):
    sum_ref[...] = share_of_out(blocks, core, side_ref, rank_ref, w_ref, own_ref[...].astype(jnp.float32))


def out_kernel(blocks, core, tick, rank_ref, *refs):
    sides, (w_ref, sum_ref, fresh_ref, *result_refs) = refs[: core - 1], refs[core - 1 :]
    total = sum_ref[...]
    for c, side_ref in enumerate(sides):
        count = side_ref.shape[0]
        total = share_of_out(blocks[c * count : (c + 1) * count], core, side_ref, rank_ref, w_ref, total)
    result = total.astype(jnp.bfloat16)
    result_refs[0][...] = result
    if len(result_refs) > 1:
        result_refs[1][...] = jnp.where(rank_ref[1] == 1, fresh_ref[tick + 1], result)


def in_vmem(count):
    return [pl.BlockSpec(memory_space=pltpu.VMEM)] * count


def call(kernel, operands, outs, scratch, flops, name, far_operands=()):
    specs = [pl.BlockSpec(memory_space=pltpu.SMEM)] + in_vmem(len(operands) - 1)
    operands = list(operands)
    for n in far_operands:
        specs[n] = pl.BlockSpec(memory_space=pltpu.HBM)
        operands[n] = pltpu.with_memory_space_constraint(operands[n], pltpu.HBM)
    return pl.pallas_call(
        kernel,
        in_specs=specs,
        out_specs=in_vmem(len(outs)),
        out_shape=outs,
        scratch_shapes=scratch,
        compiler_params=pltpu.CompilerParams(vmem_limit_bytes=VMEM_LIMIT),
        cost_estimate=pl.CostEstimate(flops=flops, bytes_accessed=flops // 1024, transcendentals=0),
        name=name,
    )(*operands)


def sums_of(x, branches, chan):
    _, rows, feat = x.shape
    return [
        jax.ShapeDtypeStruct((branches, rows, chan), jnp.float32),
        jax.ShapeDtypeStruct((rows, min(feat, 128)), jnp.float32),
    ]


def project_load(blocks, order, core, x, w_in, gain, taps, decay, rank):
    branches, chan, model_width = w_in.shape
    piece = jax.ShapeDtypeStruct((branches, chan, model_width // len(order)), w_in.dtype)
    outs = [piece] * len(order) + sums_of(x, branches, chan)
    outs += [jax.ShapeDtypeStruct(gain.shape, gain.dtype), jax.ShapeDtypeStruct(taps.shape[::-1], taps.dtype)]
    scratch = [
        pltpu.SemaphoreType.DMA((len(order), branches)),
        pltpu.VMEM(taps.shape, taps.dtype),
        pltpu.VMEM(decay.shape, decay.dtype),
        pltpu.SemaphoreType.DMA((3,)),
    ]
    kernel = functools.partial(load_kernel, blocks, order, core)
    flops = 2 * x.size * branches * chan
    *pieces, acc, sq, gain, long_rows = call(
        kernel, [rank, x, w_in, gain, taps, decay], outs, scratch, flops, "project_load", [2, 3, 4, 5]
    )
    return [acc, sq], {"in": dict(zip(order, pieces)), "gain": gain, "long": long_rows}


def project_part(blocks, core, x, params, sums, rank):
    w_refs = [params["in"][cell] for cell, _ in blocks]
    branches, chan, _ = w_refs[0].shape
    kernel, name = (more_kernel, "project_more") if sums else (first_kernel, "project_first")
    operands = [rank, x, params["gain"], *sums, *w_refs]
    flops = 2 * x.size * branches * chan
    return call(functools.partial(kernel, blocks, core), operands, sums_of(x, branches, chan), [], flops, name)


def mix(blocks, core, model_width, sides, params, sums, short_rows, rank):
    rows, chan = sums[0].shape[1:]
    scratch = [pltpu.VMEM(total.shape, total.dtype) for total in sums]
    scratch += [pltpu.VMEM((PAD + rows, chan), jnp.float32), pltpu.VMEM((rows, chan), jnp.float32)]
    w_refs = [params["in"][cell] for cell, _ in blocks[: len(blocks) // max(core - 1, 1)]]
    return call(
        functools.partial(mix_kernel, blocks, core, model_width),
        [rank, *sides, params["gain"], *sums, short_rows, params["long"], *w_refs],
        [jax.ShapeDtypeStruct((rows, chan), jnp.bfloat16)],
        scratch,
        2 * rows * model_width * 3 * chan,
        "project_mix",
    )[0]


def project_out_early(blocks, core, side, w_out, own, rank):
    return call(
        functools.partial(out_early_kernel, blocks, core),
        [rank, side, w_out, own],
        [jax.ShapeDtypeStruct(own.shape, jnp.float32)],
        [],
        2 * side.size * w_out.shape[1],
        "project_out_early",
    )[0]


def project_out(blocks, core, tick, sides, w_out, total, fresh, rank):
    result = jax.ShapeDtypeStruct(total.shape, jnp.bfloat16)
    return call(
        functools.partial(out_kernel, blocks, core, tick),
        [rank, *sides, w_out, total, fresh],
        [result, result] if tick + 1 < fresh.shape[0] else [result],
        [],
        total.size * w_out.shape[0],
        "project_out",
    )


def body(section_count, dp_count, fresh_acts, carried, norm_gain, w_in, short_filter, filter_taps, decay_rate, w_out):
    tick_count, tok_len, _ = fresh_acts.shape
    far, near, core = split_dp(dp_count)
    group = near * core
    section_idx = lax.axis_index("section")
    rank = jnp.stack([lax.axis_index("dp"), (section_idx == section_count - 1).astype(jnp.int32)])

    def swap(value, offset):
        return lax.ppermute(value, "dp", [(r, r ^ offset) for r in range(dp_count)])


    def onward(value, offset):
        pairs = [
            (s * dp_count + r, (s + 1) % section_count * dp_count + (r ^ offset))
            for s in range(section_count)
            for r in range(dp_count)
        ]
        return lax.ppermute(value, ("section", "dp"), pairs)

    def after(value, *earlier):
        return lax.optimization_barrier((value, [x for x in earlier if x is not None]))[0]

    def round_one(source, cross=False):
        first, _, later = routes(far, near, cross)
        if cross:
            blocks = [onward(source, d * core) for d in first]
        else:
            blocks = [swap(source, d * core) if d else source for d in first]
        blocks, aside = lax.optimization_barrier((blocks, [swap(source, d * core) for d in later]))
        return dict(zip(first, blocks)), aside

    def round_two(blocks, aside, cross=False):
        _, second, later = routes(far, near, cross)
        leaving = lax.optimization_barrier([jnp.stack([blocks[b] for b in sent]) for _, sent in second])
        rest = [swap(payload, d * core) for payload, (d, _) in zip(leaving, second)]
        rest += [onward(block, 0)[None] for block in aside]
        return [d ^ b for d, sent in second for b in sent] + later, rest

    def of_cores(cells, cores):
        return [(cell, c) for c in cores for cell in cells]

    short_rows = short_filter.transpose(1, 3, 0, 2)
    source = jnp.where(section_idx == 0, fresh_acts[0], carried[0])
    params, made = {}, []
    for k in range(tick_count):
        blocks, aside = round_one(source, k > 0)
        cells, rest = round_two(blocks, aside, k > 0)
        order = [*blocks, *cells]
        direct = jnp.stack(list(blocks.values()))
        here = of_cores(blocks, [0])
        if params:
            sums = project_part(here, core, after(direct, rest[min(2, len(rest) - 1)]), params, [], rank)
        else:
            sums, params = project_load(
                here, order, core, direct, w_in[0], norm_gain, filter_taps[0], decay_rate, rank
            )
        relayed = jnp.concatenate(after(rest, sums))
        everything = jnp.concatenate([direct, relayed])
        sides = [swap(everything, c) for c in range(1, core)]
        sums = project_part(of_cores(cells, [0]), core, relayed, params, sums, rank)
        sides = after(sides, sums)
        y = mix(of_cores(order, range(1, core)), core, norm_gain.shape[1], sides, params, sums, short_rows, rank)
        y_blocks, _ = round_one(y)
        cells, rest = round_two(y_blocks, [])
        everything = jnp.concatenate([jnp.stack(list(y_blocks.values())), *rest])
        sides = [swap(everything, c) for c in range(1, core)]
        order = [*y_blocks, *cells]
        total = project_out_early(of_cores(order, [0]), core, everything, w_out[0], blocks[0], rank)
        sides = after(sides, total)
        blocks = of_cores(order, range(1, core))
        result, *leaving = project_out(blocks, core, k, sides, w_out[0], total, fresh_acts, rank)
        made.append(result)
        source = leaving[0] if leaving else None
    return jnp.stack(made)[None]


def solution(mesh):
    run = functools.partial(body, mesh.shape["section"], mesh.shape["dp"])
    return jax.shard_map(
        run,
        mesh=mesh,
        in_specs=(
            P(None, None, "dp"),
            P("section", None, "dp"),
            P("section", None),
            P("section", None, "dp", None),
            P("section", None, "dp", None),
            P("section", "dp", None),
            P("section", "dp"),
            P("section", None, "dp"),
        ),
        out_specs=P("section", None, None, "dp"),
        check_vma=False,
    )
```

```python
import functools

import jax
import jax.numpy as jnp
from jax import lax
from jax.experimental import pallas as pl
from jax.experimental.pallas import tpu as pltpu
from jax.sharding import PartitionSpec as P

EPS = 1e-06
VMEM_LIMIT = 20 * 1024 * 1024
PAD = 8
GROUP = 4


def split_dp(dp_count):
    core = 2 if dp_count % 2 == 0 else 1
    chips = dp_count // core
    near = 1
    while near * near * 4 <= chips:
        near *= 2
    return chips // near, near, core


def routes(far, near, cross):
    if (far, near) == (4, 2):
        if cross:
            return [0, 2, 4], [(1, [2, 4]), (3, [4]), (2, [4])], [1]
        return [0, 1, 2, 4], [(1, [2, 4]), (3, [4]), (2, [4])], []
    line = [d * near for d in range(far)]
    return line, [(d, line) for d in range(1, near)], []


def columns_of(rank_ref, core, cell, c, size):
    chip, side = lax.div(rank_ref[0], core), lax.rem(rank_ref[0], core)
    return pl.ds(pl.multiple_of(((chip ^ cell) * core + (side ^ c)) * size, size), size)


def project(blocks, core, values_of, weights_of, rank_ref, gain_ref, acc_ref, sq_ref, before=None, ready=None):
    lanes = sq_ref.shape[1]
    side = lax.rem(rank_ref[0], core)
    for first in range(0, len(blocks), GROUP):
        group = range(first, min(first + GROUP, len(blocks)))
        normed, columns, parts = [], [], []
        for n in group:
            cell, c = blocks[n]
            values = values_of(n).astype(jnp.float32)
            feat = values.shape[1]
            gains = gain_ref[:, columns_of(rank_ref, core, cell, c, feat)]
            normed.append((values * gains).astype(jnp.bfloat16))
            columns.append(pl.ds(pl.multiple_of((side ^ c) * feat, feat), feat))
            squares = values * values
            parts += [squares[:, m : m + lanes] for m in range(0, feat, lanes)]
        if ready is not None:
            for n in group:
                ready(n)
        if first == 0 and before is not None:
            parts.append(before[1][...])
        part = functools.reduce(jnp.add, parts)
        sq_ref[...] = part if first == 0 else sq_ref[...] + part
        for i in range(acc_ref.shape[0]):
            terms = [
                lax.dot_general(
                    normed[n - first],
                    weights_of(n)[i, :, columns[n - first]],
                    (((1,), (1,)), ((), ())),
                    preferred_element_type=jnp.float32,
                )
                for n in group
            ]
            if first > 0:
                terms.append(acc_ref[i])
            elif before is not None:
                terms.append(before[0][i])
            acc_ref[i] = functools.reduce(jnp.add, terms)


def load_kernel(blocks, order, core, rank_ref, x_ref, w_far, gain_far, taps_far, decay_far, *refs):
    w_refs, (acc_ref, sq_ref, gain_ref, long_ref) = refs[: len(order)], refs[len(order) : len(order) + 4]
    sems, taps_ref, decay_ref, small_sems = refs[len(order) + 4 :]
    small = [(gain_far, gain_ref), (taps_far, taps_ref), (decay_far, decay_ref)]
    small = [pltpu.make_async_copy(src, dst, small_sems.at[n]) for n, (src, dst) in enumerate(small)]
    wide = w_refs[0].shape[2]
    chip = lax.div(rank_ref[0], core)
    copies = []
    for n, cell in enumerate(order):
        columns = pl.ds(pl.multiple_of((chip ^ cell) * wide, wide), wide)
        copies.append(
            [
                pltpu.make_async_copy(w_far.at[i, :, columns], w_refs[n].at[i], sems.at[n, i])
                for i in range(w_far.shape[0])
            ]
        )
    for group in [small] + copies:
        for copy in group:
            copy.start()
    for copy in small:
        copy.wait()
    lags = lax.broadcasted_iota(jnp.int32, long_ref.shape, 0).astype(jnp.float32)
    long_ref[...] = taps_ref[...].T * jnp.exp(-decay_ref[...] * lags)

    def ready(n):
        for copy in copies[n]:
            copy.wait()

    project(blocks, core, lambda n: x_ref[n], lambda n: w_refs[n], rank_ref, gain_ref, acc_ref, sq_ref, None, ready)
    for n in range(len(blocks), len(order)):
        ready(n)


def first_kernel(blocks, core, rank_ref, x_ref, gain_ref, *refs):
    w_refs, (acc_ref, sq_ref) = refs[:-2], refs[-2:]
    project(blocks, core, lambda n: x_ref[n], lambda n: w_refs[n], rank_ref, gain_ref, acc_ref, sq_ref)


def mix_kernel(blocks, core, model_width, rank_ref, *refs):
    sides, refs = refs[: core - 1], refs[core - 1 :]
    count = len(blocks) // max(core - 1, 1)
    gain_ref, acc_in, sq_in, acc_more, sq_more, short_ref, long_ref = refs[:7]
    w_refs = refs[7 : 7 + count]
    y_ref, acc_ref, sq_ref, pad_ref, query_ref = refs[7 + count :]
    branches, tok_len, chan = acc_in.shape
    project(
        blocks,
        core,
        lambda n: sides[n // count][n % count],
        lambda n: w_refs[n % count],
        rank_ref,
        gain_ref,
        acc_ref,
        sq_ref,
        (acc_in, sq_in),
    )

    total = jnp.sum(sq_ref[...] + sq_more[...], axis=1, keepdims=True)
    factor = lax.rsqrt(total / model_width + EPS)
    taps = short_ref.shape[1]
    pad_ref[0:PAD, :] = jnp.zeros((PAD, chan), jnp.float32)

    def branch(i):
        u = (acc_ref[i] + acc_more[i]) * factor
        pad_ref[PAD : PAD + tok_len, :] = u
        z = short_ref[i, 0] * u
        for j in range(1, taps):
            z = z + short_ref[i, j] * pad_ref[PAD - j : PAD - j + tok_len, :]
        return z

    query_ref[...] = branch(1)
    product = query_ref[...] * branch(2)
    query_ref[...] = branch(0)
    pad_ref[PAD : PAD + tok_len, :] = product
    width = min(chan, 128)
    tiles = tok_len // 8
    for c in range(0, chan, width):
        cols = slice(c, c + width)
        conv = [None] * tiles
        for b in range(8):
            moved = [pad_ref[PAD - b + 8 * i : PAD - b + 8 * i + 8, cols] for i in range(tiles)]
            for a in range(long_ref.shape[0] // 8):
                tap = long_ref[8 * a + b : 8 * a + b + 1, cols]
                for i in range(a, tiles):
                    term = tap * moved[i - a]
                    conv[i] = term if conv[i] is None else conv[i] + term
        for i in range(0, tiles, 2):
            at = slice(8 * i, 8 * i + 16)
            both = jnp.concatenate(conv[i : i + 2], axis=0)
            y_ref[at, cols] = (query_ref[at, cols] * both).astype(jnp.bfloat16)


def share_of_out(blocks, core, side_ref, rank_ref, w_ref, total):
    chan = side_ref.shape[2]
    for first in range(0, len(blocks), GROUP):
        terms = []
        for n in range(first, min(first + GROUP, len(blocks))):
            rows = columns_of(rank_ref, core, *blocks[n], chan)
            terms.append(jnp.dot(side_ref[n], w_ref[rows, :], preferred_element_type=jnp.float32))
        total = functools.reduce(jnp.add, terms, total)
    return total


def out_early_kernel(blocks, core, rank_ref, side_ref, w_ref, own_ref, sum_ref):
    sum_ref[...] = share_of_out(blocks, core, side_ref, rank_ref, w_ref, own_ref[...].astype(jnp.float32))


def out_kernel(blocks, core, tick, rank_ref, *refs):
    sides, (w_ref, sum_ref, fresh_ref, *result_refs) = refs[: core - 1], refs[core - 1 :]
    total = sum_ref[...]
    for c, side_ref in enumerate(sides):
        count = side_ref.shape[0]
        total = share_of_out(blocks[c * count : (c + 1) * count], core, side_ref, rank_ref, w_ref, total)
    result = total.astype(jnp.bfloat16)
    result_refs[0][...] = result
    if len(result_refs) > 1:
        result_refs[1][...] = jnp.where(rank_ref[1] == 1, fresh_ref[tick + 1], result)


def in_vmem(count):
    return [pl.BlockSpec(memory_space=pltpu.VMEM)] * count


def call(kernel, operands, outs, scratch, flops, name, far_operands=()):
    specs = [pl.BlockSpec(memory_space=pltpu.SMEM)] + in_vmem(len(operands) - 1)
    operands = list(operands)
    for n in far_operands:
        specs[n] = pl.BlockSpec(memory_space=pltpu.HBM)
        operands[n] = pltpu.with_memory_space_constraint(operands[n], pltpu.HBM)
    return pl.pallas_call(
        kernel,
        in_specs=specs,
        out_specs=in_vmem(len(outs)),
        out_shape=outs,
        scratch_shapes=scratch,
        compiler_params=pltpu.CompilerParams(vmem_limit_bytes=VMEM_LIMIT),
        cost_estimate=pl.CostEstimate(flops=flops, bytes_accessed=flops // 1024, transcendentals=0),
        name=name,
    )(*operands)


def sums_of(x, branches, chan):
    _, rows, feat = x.shape
    return [
        jax.ShapeDtypeStruct((branches, rows, chan), jnp.float32),
        jax.ShapeDtypeStruct((rows, min(feat, 128)), jnp.float32),
    ]


def project_load(blocks, order, core, x, w_in, gain, taps, decay, rank):
    branches, chan, model_width = w_in.shape
    piece = jax.ShapeDtypeStruct((branches, chan, model_width // len(order)), w_in.dtype)
    outs = [piece] * len(order) + sums_of(x, branches, chan)
    outs += [jax.ShapeDtypeStruct(gain.shape, gain.dtype), jax.ShapeDtypeStruct(taps.shape[::-1], taps.dtype)]
    scratch = [
        pltpu.SemaphoreType.DMA((len(order), branches)),
        pltpu.VMEM(taps.shape, taps.dtype),
        pltpu.VMEM(decay.shape, decay.dtype),
        pltpu.SemaphoreType.DMA((3,)),
    ]
    kernel = functools.partial(load_kernel, blocks, order, core)
    flops = 2 * x.size * branches * chan
    *pieces, acc, sq, gain, long_rows = call(
        kernel, [rank, x, w_in, gain, taps, decay], outs, scratch, flops, "project_load", [2, 3, 4, 5]
    )
    return [acc, sq], {"in": dict(zip(order, pieces)), "gain": gain, "long": long_rows}


def project_part(blocks, core, x, params, rank, name):
    w_refs = [params["in"][cell] for cell, _ in blocks]
    branches, chan, _ = w_refs[0].shape
    operands = [rank, x, params["gain"], *w_refs]
    flops = 2 * x.size * branches * chan
    return call(functools.partial(first_kernel, blocks, core), operands, sums_of(x, branches, chan), [], flops, name)


def mix(blocks, core, model_width, sides, params, sums, more, short_rows, rank):
    rows, chan = sums[0].shape[1:]
    scratch = [pltpu.VMEM(total.shape, total.dtype) for total in sums]
    scratch += [pltpu.VMEM((PAD + rows, chan), jnp.float32), pltpu.VMEM((rows, chan), jnp.float32)]
    w_refs = [params["in"][cell] for cell, _ in blocks[: len(blocks) // max(core - 1, 1)]]
    return call(
        functools.partial(mix_kernel, blocks, core, model_width),
        [rank, *sides, params["gain"], *sums, *more, short_rows, params["long"], *w_refs],
        [jax.ShapeDtypeStruct((rows, chan), jnp.bfloat16)],
        scratch,
        2 * rows * model_width * 3 * chan,
        "project_mix",
    )[0]


def project_out_early(blocks, core, side, w_out, own, rank):
    return call(
        functools.partial(out_early_kernel, blocks, core),
        [rank, side, w_out, own],
        [jax.ShapeDtypeStruct(own.shape, jnp.float32)],
        [],
        2 * side.size * w_out.shape[1],
        "project_out_early",
    )[0]


def project_out(blocks, core, tick, sides, w_out, total, fresh, rank):
    result = jax.ShapeDtypeStruct(total.shape, jnp.bfloat16)
    return call(
        functools.partial(out_kernel, blocks, core, tick),
        [rank, *sides, w_out, total, fresh],
        [result, result] if tick + 1 < fresh.shape[0] else [result],
        [],
        total.size * w_out.shape[0],
        "project_out",
    )


def body(section_count, dp_count, fresh_acts, carried, norm_gain, w_in, short_filter, filter_taps, decay_rate, w_out):
    tick_count, tok_len, _ = fresh_acts.shape
    far, near, core = split_dp(dp_count)
    group = near * core
    section_idx = lax.axis_index("section")
    rank = jnp.stack([lax.axis_index("dp"), (section_idx == section_count - 1).astype(jnp.int32)])

    def swap(value, offset):
        return lax.ppermute(value, "dp", [(r, r ^ offset) for r in range(dp_count)])


    def onward(value, offset):
        pairs = [
            (s * dp_count + r, (s + 1) % section_count * dp_count + (r ^ offset))
            for s in range(section_count)
            for r in range(dp_count)
        ]
        return lax.ppermute(value, ("section", "dp"), pairs)

    def after(value, *earlier):
        return lax.optimization_barrier((value, [x for x in earlier if x is not None]))[0]

    def round_one(source, cross=False):
        first, _, later = routes(far, near, cross)
        if cross:
            blocks = [onward(source, d * core) for d in first]
        else:
            blocks = [swap(source, d * core) if d else source for d in first]
        blocks, aside = lax.optimization_barrier((blocks, [swap(source, d * core) for d in later]))
        return dict(zip(first, blocks)), aside

    def round_two(blocks, aside, cross=False):
        _, second, later = routes(far, near, cross)
        leaving = lax.optimization_barrier([jnp.stack([blocks[b] for b in sent]) for _, sent in second])
        rest = [swap(payload, d * core) for payload, (d, _) in zip(leaving, second)]
        rest += [onward(block, 0)[None] for block in aside]
        return [d ^ b for d, sent in second for b in sent] + later, rest

    def of_cores(cells, cores):
        return [(cell, c) for c in cores for cell in cells]

    short_rows = short_filter.transpose(1, 3, 0, 2)
    source = jnp.where(section_idx == 0, fresh_acts[0], carried[0])
    params, made = {}, []
    for k in range(tick_count):
        blocks, aside = round_one(source, k > 0)
        cells, rest = round_two(blocks, aside, k > 0)
        order = [*blocks, *cells]
        direct = jnp.stack(list(blocks.values()))
        here = of_cores(blocks, [0])
        if params:
            sums = project_part(here, core, after(direct, rest[min(2, len(rest) - 1)]), params, rank, "project_first")
        else:
            sums, params = project_load(
                here, order, core, direct, w_in[0], norm_gain, filter_taps[0], decay_rate, rank
            )
        relayed = jnp.concatenate(after(rest, sums))
        everything = jnp.concatenate([direct, relayed])
        sides = [swap(everything, c) for c in range(1, core)]
        more = project_part(of_cores(cells, [0]), core, relayed, params, rank, "project_more")
        sides = after(sides, more)
        y = mix(of_cores(order, range(1, core)), core, norm_gain.shape[1], sides, params, sums, more, short_rows, rank)
        y_blocks, _ = round_one(y)
        cells, rest = round_two(y_blocks, [])
        everything = jnp.concatenate([jnp.stack(list(y_blocks.values())), *rest])
        sides = [swap(everything, c) for c in range(1, core)]
        order = [*y_blocks, *cells]
        total = project_out_early(of_cores(order, [0]), core, everything, w_out[0], blocks[0], rank)
        sides = after(sides, total)
        blocks = of_cores(order, range(1, core))
        result, *leaving = project_out(blocks, core, k, sides, w_out[0], total, fresh_acts, rank)
        made.append(result)
        source = leaving[0] if leaving else None
    return jnp.stack(made)[None]


def solution(mesh):
    run = functools.partial(body, mesh.shape["section"], mesh.shape["dp"])
    return jax.shard_map(
        run,
        mesh=mesh,
        in_specs=(
            P(None, None, "dp"),
            P("section", None, "dp"),
            P("section", None),
            P("section", None, "dp", None),
            P("section", None, "dp", None),
            P("section", "dp", None),
            P("section", "dp"),
            P("section", None, "dp"),
        ),
        out_specs=P("section", None, None, "dp"),
        check_vma=False,
    )
```

```python
import functools

import jax
import jax.numpy as jnp
from jax import lax
from jax.experimental import pallas as pl
from jax.experimental.pallas import tpu as pltpu
from jax.sharding import PartitionSpec as P

EPS = 1e-06
VMEM_LIMIT = 20 * 1024 * 1024
PAD = 8
GROUP = 4


def split_dp(dp_count):
    core = 2 if dp_count % 2 == 0 else 1
    chips = dp_count // core
    near = 1
    while near * near * 4 <= chips:
        near *= 2
    return chips // near, near, core


def routes(far, near, cross):
    if (far, near) == (4, 2):
        if cross:
            return [0, 2, 4], [(1, [2, 4]), (3, [4]), (2, [4])], [1]
        return [0, 1, 2, 4], [(1, [2, 4]), (3, [4]), (2, [4])], []
    line = [d * near for d in range(far)]
    return line, [(d, line) for d in range(1, near)], []


def columns_of(rank_ref, core, cell, c, size):
    chip, side = lax.div(rank_ref[0], core), lax.rem(rank_ref[0], core)
    return pl.ds(pl.multiple_of(((chip ^ cell) * core + (side ^ c)) * size, size), size)


def project(blocks, core, values_of, weights_of, rank_ref, gain_ref, acc_ref, sq_ref, before=None, ready=None):
    lanes = sq_ref.shape[1]
    side = lax.rem(rank_ref[0], core)
    for first in range(0, len(blocks), GROUP):
        group = range(first, min(first + GROUP, len(blocks)))
        normed, columns, parts = [], [], []
        for n in group:
            cell, c = blocks[n]
            values = values_of(n).astype(jnp.float32)
            feat = values.shape[1]
            gains = gain_ref[:, columns_of(rank_ref, core, cell, c, feat)]
            normed.append((values * gains).astype(jnp.bfloat16))
            columns.append(pl.ds(pl.multiple_of((side ^ c) * feat, feat), feat))
            squares = values * values
            parts += [squares[:, m : m + lanes] for m in range(0, feat, lanes)]
        if ready is not None:
            for n in group:
                ready(n)
        if first == 0 and before is not None:
            parts.append(before[1][...])
        part = functools.reduce(jnp.add, parts)
        sq_ref[...] = part if first == 0 else sq_ref[...] + part
        for i in range(acc_ref.shape[0]):
            terms = [
                lax.dot_general(
                    normed[n - first],
                    weights_of(n)[i, :, columns[n - first]],
                    (((1,), (1,)), ((), ())),
                    preferred_element_type=jnp.float32,
                )
                for n in group
            ]
            if first > 0:
                terms.append(acc_ref[i])
            elif before is not None:
                terms.append(before[0][i])
            acc_ref[i] = functools.reduce(jnp.add, terms)


def load_kernel(blocks, order, core, rank_ref, x_ref, w_far, gain_far, taps_far, decay_far, *refs):
    w_refs, (acc_ref, sq_ref, gain_ref, long_ref) = refs[: len(order)], refs[len(order) : len(order) + 4]
    sems, taps_ref, decay_ref, small_sems = refs[len(order) + 4 :]
    small = [(gain_far, gain_ref), (taps_far, taps_ref), (decay_far, decay_ref)]
    small = [pltpu.make_async_copy(src, dst, small_sems.at[n]) for n, (src, dst) in enumerate(small)]
    wide = w_refs[0].shape[2]
    chip = lax.div(rank_ref[0], core)
    copies = []
    for n, cell in enumerate(order):
        columns = pl.ds(pl.multiple_of((chip ^ cell) * wide, wide), wide)
        copies.append(
            [
                pltpu.make_async_copy(w_far.at[i, :, columns], w_refs[n].at[i], sems.at[n, i])
                for i in range(w_far.shape[0])
            ]
        )
    for group in [small] + copies:
        for copy in group:
            copy.start()
    small[0].wait()

    def ready(n):
        for copy in copies[n]:
            copy.wait()

    project(blocks, core, lambda n: x_ref[n], lambda n: w_refs[n], rank_ref, gain_ref, acc_ref, sq_ref, None, ready)
    for copy in small[1:]:
        copy.wait()
    lags = lax.broadcasted_iota(jnp.int32, long_ref.shape, 0).astype(jnp.float32)
    long_ref[...] = taps_ref[...].T * jnp.exp(-decay_ref[...] * lags)
    for n in range(len(blocks), len(order)):
        ready(n)


def first_kernel(blocks, core, rank_ref, x_ref, gain_ref, *refs):
    w_refs, (acc_ref, sq_ref) = refs[:-2], refs[-2:]
    project(blocks, core, lambda n: x_ref[n], lambda n: w_refs[n], rank_ref, gain_ref, acc_ref, sq_ref)


def mix_kernel(blocks, core, model_width, rank_ref, *refs):
    sides, refs = refs[: core - 1], refs[core - 1 :]
    count = len(blocks) // max(core - 1, 1)
    gain_ref, acc_in, sq_in, acc_more, sq_more, short_ref, long_ref = refs[:7]
    w_refs = refs[7 : 7 + count]
    y_ref, acc_ref, sq_ref, pad_ref, query_ref = refs[7 + count :]
    branches, tok_len, chan = acc_in.shape
    project(
        blocks,
        core,
        lambda n: sides[n // count][n % count],
        lambda n: w_refs[n % count],
        rank_ref,
        gain_ref,
        acc_ref,
        sq_ref,
        (acc_in, sq_in),
    )

    total = jnp.sum(sq_ref[...] + sq_more[...], axis=1, keepdims=True)
    factor = lax.rsqrt(total / model_width + EPS)
    taps = short_ref.shape[1]
    pad_ref[0:PAD, :] = jnp.zeros((PAD, chan), jnp.float32)

    def branch(i):
        u = (acc_ref[i] + acc_more[i]) * factor
        pad_ref[PAD : PAD + tok_len, :] = u
        z = short_ref[i, 0] * u
        for j in range(1, taps):
            z = z + short_ref[i, j] * pad_ref[PAD - j : PAD - j + tok_len, :]
        return z

    query_ref[...] = branch(1)
    product = query_ref[...] * branch(2)
    query_ref[...] = branch(0)
    pad_ref[PAD : PAD + tok_len, :] = product
    width = min(chan, 128)
    tiles = tok_len // 8
    for c in range(0, chan, width):
        cols = slice(c, c + width)
        conv = [None] * tiles
        for b in range(8):
            moved = [pad_ref[PAD - b + 8 * i : PAD - b + 8 * i + 8, cols] for i in range(tiles)]
            for a in range(long_ref.shape[0] // 8):
                tap = long_ref[8 * a + b : 8 * a + b + 1, cols]
                for i in range(a, tiles):
                    term = tap * moved[i - a]
                    conv[i] = term if conv[i] is None else conv[i] + term
        for i in range(0, tiles, 2):
            at = slice(8 * i, 8 * i + 16)
            both = jnp.concatenate(conv[i : i + 2], axis=0)
            y_ref[at, cols] = (query_ref[at, cols] * both).astype(jnp.bfloat16)


def share_of_out(blocks, core, side_ref, rank_ref, w_ref, total):
    chan = side_ref.shape[2]
    for first in range(0, len(blocks), GROUP):
        terms = []
        for n in range(first, min(first + GROUP, len(blocks))):
            rows = columns_of(rank_ref, core, *blocks[n], chan)
            terms.append(jnp.dot(side_ref[n], w_ref[rows, :], preferred_element_type=jnp.float32))
        total = functools.reduce(jnp.add, terms, total)
    return total


def out_early_kernel(blocks, core, rank_ref, side_ref, w_ref, own_ref, sum_ref):
    sum_ref[...] = share_of_out(blocks, core, side_ref, rank_ref, w_ref, own_ref[...].astype(jnp.float32))


def out_kernel(blocks, core, tick, rank_ref, *refs):
    sides, (w_ref, sum_ref, fresh_ref, *result_refs) = refs[: core - 1], refs[core - 1 :]
    total = sum_ref[...]
    for c, side_ref in enumerate(sides):
        count = side_ref.shape[0]
        total = share_of_out(blocks[c * count : (c + 1) * count], core, side_ref, rank_ref, w_ref, total)
    result = total.astype(jnp.bfloat16)
    result_refs[0][...] = result
    if len(result_refs) > 1:
        result_refs[1][...] = jnp.where(rank_ref[1] == 1, fresh_ref[tick + 1], result)


def in_vmem(count):
    return [pl.BlockSpec(memory_space=pltpu.VMEM)] * count


def call(kernel, operands, outs, scratch, flops, name, far_operands=()):
    specs = [pl.BlockSpec(memory_space=pltpu.SMEM)] + in_vmem(len(operands) - 1)
    operands = list(operands)
    for n in far_operands:
        specs[n] = pl.BlockSpec(memory_space=pltpu.HBM)
        operands[n] = pltpu.with_memory_space_constraint(operands[n], pltpu.HBM)
    return pl.pallas_call(
        kernel,
        in_specs=specs,
        out_specs=in_vmem(len(outs)),
        out_shape=outs,
        scratch_shapes=scratch,
        compiler_params=pltpu.CompilerParams(vmem_limit_bytes=VMEM_LIMIT),
        cost_estimate=pl.CostEstimate(flops=flops, bytes_accessed=flops // 1024, transcendentals=0),
        name=name,
    )(*operands)


def sums_of(x, branches, chan):
    _, rows, feat = x.shape
    return [
        jax.ShapeDtypeStruct((branches, rows, chan), jnp.float32),
        jax.ShapeDtypeStruct((rows, min(feat, 128)), jnp.float32),
    ]


def project_load(blocks, order, core, x, w_in, gain, taps, decay, rank):
    branches, chan, model_width = w_in.shape
    piece = jax.ShapeDtypeStruct((branches, chan, model_width // len(order)), w_in.dtype)
    outs = [piece] * len(order) + sums_of(x, branches, chan)
    outs += [jax.ShapeDtypeStruct(gain.shape, gain.dtype), jax.ShapeDtypeStruct(taps.shape[::-1], taps.dtype)]
    scratch = [
        pltpu.SemaphoreType.DMA((len(order), branches)),
        pltpu.VMEM(taps.shape, taps.dtype),
        pltpu.VMEM(decay.shape, decay.dtype),
        pltpu.SemaphoreType.DMA((3,)),
    ]
    kernel = functools.partial(load_kernel, blocks, order, core)
    flops = 2 * x.size * branches * chan
    *pieces, acc, sq, gain, long_rows = call(
        kernel, [rank, x, w_in, gain, taps, decay], outs, scratch, flops, "project_load", [2, 3, 4, 5]
    )
    return [acc, sq], {"in": dict(zip(order, pieces)), "gain": gain, "long": long_rows}


def project_part(blocks, core, x, params, rank, name):
    w_refs = [params["in"][cell] for cell, _ in blocks]
    branches, chan, _ = w_refs[0].shape
    operands = [rank, x, params["gain"], *w_refs]
    flops = 2 * x.size * branches * chan
    return call(functools.partial(first_kernel, blocks, core), operands, sums_of(x, branches, chan), [], flops, name)


def mix(blocks, core, model_width, sides, params, sums, more, short_rows, rank):
    rows, chan = sums[0].shape[1:]
    scratch = [pltpu.VMEM(total.shape, total.dtype) for total in sums]
    scratch += [pltpu.VMEM((PAD + rows, chan), jnp.float32), pltpu.VMEM((rows, chan), jnp.float32)]
    w_refs = [params["in"][cell] for cell, _ in blocks[: len(blocks) // max(core - 1, 1)]]
    return call(
        functools.partial(mix_kernel, blocks, core, model_width),
        [rank, *sides, params["gain"], *sums, *more, short_rows, params["long"], *w_refs],
        [jax.ShapeDtypeStruct((rows, chan), jnp.bfloat16)],
        scratch,
        2 * rows * model_width * 3 * chan,
        "project_mix",
    )[0]


def project_out_early(blocks, core, side, w_out, own, rank):
    return call(
        functools.partial(out_early_kernel, blocks, core),
        [rank, side, w_out, own],
        [jax.ShapeDtypeStruct(own.shape, jnp.float32)],
        [],
        2 * side.size * w_out.shape[1],
        "project_out_early",
    )[0]


def project_out(blocks, core, tick, sides, w_out, total, fresh, rank):
    result = jax.ShapeDtypeStruct(total.shape, jnp.bfloat16)
    return call(
        functools.partial(out_kernel, blocks, core, tick),
        [rank, *sides, w_out, total, fresh],
        [result, result] if tick + 1 < fresh.shape[0] else [result],
        [],
        total.size * w_out.shape[0],
        "project_out",
    )


def body(section_count, dp_count, fresh_acts, carried, norm_gain, w_in, short_filter, filter_taps, decay_rate, w_out):
    tick_count, tok_len, _ = fresh_acts.shape
    far, near, core = split_dp(dp_count)
    group = near * core
    section_idx = lax.axis_index("section")
    rank = jnp.stack([lax.axis_index("dp"), (section_idx == section_count - 1).astype(jnp.int32)])

    def swap(value, offset):
        return lax.ppermute(value, "dp", [(r, r ^ offset) for r in range(dp_count)])


    def onward(value, offset):
        pairs = [
            (s * dp_count + r, (s + 1) % section_count * dp_count + (r ^ offset))
            for s in range(section_count)
            for r in range(dp_count)
        ]
        return lax.ppermute(value, ("section", "dp"), pairs)

    def after(value, *earlier):
        return lax.optimization_barrier((value, [x for x in earlier if x is not None]))[0]

    def round_one(source, cross=False):
        first, _, later = routes(far, near, cross)
        if cross:
            blocks = [onward(source, d * core) for d in first]
        else:
            blocks = [swap(source, d * core) if d else source for d in first]
        blocks, aside = lax.optimization_barrier((blocks, [swap(source, d * core) for d in later]))
        return dict(zip(first, blocks)), aside

    def round_two(blocks, aside, cross=False):
        _, second, later = routes(far, near, cross)
        leaving = lax.optimization_barrier([jnp.stack([blocks[b] for b in sent]) for _, sent in second])
        rest = [swap(payload, d * core) for payload, (d, _) in zip(leaving, second)]
        rest += [onward(block, 0)[None] for block in aside]
        return [d ^ b for d, sent in second for b in sent] + later, rest

    def of_cores(cells, cores):
        return [(cell, c) for c in cores for cell in cells]

    short_rows = short_filter.transpose(1, 3, 0, 2)
    source = jnp.where(section_idx == 0, fresh_acts[0], carried[0])
    params, made = {}, []
    for k in range(tick_count):
        blocks, aside = round_one(source, k > 0)
        cells, rest = round_two(blocks, aside, k > 0)
        order = [*blocks, *cells]
        direct = jnp.stack(list(blocks.values()))
        here = of_cores(blocks, [0])
        if params:
            sums = project_part(here, core, after(direct, rest[min(2, len(rest) - 1)]), params, rank, "project_first")
        else:
            sums, params = project_load(
                here, order, core, direct, w_in[0], norm_gain, filter_taps[0], decay_rate, rank
            )
        relayed = jnp.concatenate(after(rest, sums))
        everything = jnp.concatenate([direct, relayed])
        sides = [swap(everything, c) for c in range(1, core)]
        more = project_part(of_cores(cells, [0]), core, relayed, params, rank, "project_more")
        sides = after(sides, more)
        y = mix(of_cores(order, range(1, core)), core, norm_gain.shape[1], sides, params, sums, more, short_rows, rank)
        y_blocks, _ = round_one(y)
        cells, rest = round_two(y_blocks, [])
        everything = jnp.concatenate([jnp.stack(list(y_blocks.values())), *rest])
        sides = [swap(everything, c) for c in range(1, core)]
        order = [*y_blocks, *cells]
        total = project_out_early(of_cores(order, [0]), core, everything, w_out[0], blocks[0], rank)
        sides = after(sides, total)
        blocks = of_cores(order, range(1, core))
        result, *leaving = project_out(blocks, core, k, sides, w_out[0], total, fresh_acts, rank)
        made.append(result)
        source = leaving[0] if leaving else None
    return jnp.stack(made)[None]


def solution(mesh):
    run = functools.partial(body, mesh.shape["section"], mesh.shape["dp"])
    return jax.shard_map(
        run,
        mesh=mesh,
        in_specs=(
            P(None, None, "dp"),
            P("section", None, "dp"),
            P("section", None),
            P("section", None, "dp", None),
            P("section", None, "dp", None),
            P("section", "dp", None),
            P("section", "dp"),
            P("section", None, "dp"),
        ),
        out_specs=P("section", None, None, "dp"),
        check_vma=False,
    )
```
